32 devices in a mesh: seq: 8 (over z, y), head: 4 (over x, core).
Axes of the slice: x: 2, y: 2, z: 4, core: 2. Of those that a mesh axis runs over, the one named last changes fastest.
Arguments:
- tokens: bfloat16 [8192, 1024], P('seq', 'head'), may hold values from -6 to 6
- lengths: int32 [4], replicated, may hold values from 128 to 7680, as said below
- pad_mask: int32 [8192], P('seq'), may hold values from 0 to 1, as said below
- ln1_gain: float32 [1024], replicated, may hold values from 0.5 to 1.5
- ln1_bias: float32 [1024], replicated, may hold values from -4 to 4
- ln2_gain: float32 [1024], replicated, may hold values from 0.5 to 1.5
- ln2_bias: float32 [1024], replicated, may hold values from -4 to 4
- w_qkv: bfloat16 [3, 1024, 1024], P(None, None, 'head'), may hold values from -0.1875 to 0.1875
- b_qkv: float32 [3, 1024], P(None, 'head'), may hold values from -4 to 4
- feat_weight: float32 [16, 64], P('head'), may hold values from 0.3 to 3
- w_out: bfloat16 [1024, 1024], P('head'), may hold values from -0.75 to 0.75
- b_out: float32 [1024], replicated, may hold values from -4 to 4
- w_in: bfloat16 [1024, 4096], P(None, 'head'), may hold values from -0.1875 to 0.1875
- b_in: float32 [4096], P('head'), may hold values from -4 to 4
- w_down: bfloat16 [4096, 1024], P('head'), may hold values from -0.09375 to 0.09375
- b_down: float32 [1024], replicated, may hold values from -4 to 4
- grad_out: bfloat16 [8192, 1024], P('seq', 'head'), may hold values from -6 to 6
Outputs:
- mixed: bfloat16 [8192, 1024], P('seq', 'head')
- grad_input: float32 [8192, 1024], P('seq', 'head')
- grad_ln1_gain: float32 [1024], P('head')
- grad_ln1_bias: float32 [1024], P('head')
- grad_ln2_gain: float32 [1024], P('head')
- grad_ln2_bias: float32 [1024], P('head')
- grad_w_qkv: float32 [3, 1024, 1024], P(None, None, 'head')
- grad_b_qkv: float32 [3, 1024], P(None, 'head')
- grad_feat_weight: float32 [16, 64], P('head')
- grad_w_out: float32 [1024, 1024], P('head')
- grad_b_out: float32 [1024], P('head')
- grad_w_in: float32 [1024, 4096], P(None, 'head')
- grad_b_in: float32 [4096], P('head')
- grad_w_down: float32 [4096, 1024], P('head')
- grad_b_down: float32 [1024], P('head')
The draws below stay inside these ranges and needn't reach their ends.
Inputs may be any that keep to these rules, and one draw needn't show every extreme that they name: `lengths`: sequences are laid end to end and fill the stream; one of them, which one drawn from the seed, starts within the first 1024 tokens and ends within the last 1024; each other one holds 128 or 256 tokens. `pad_mask`: each sequence is real tokens followed by 0 to 32 padding tokens.
All inputs are finite; a program needn't handle non-finite values.
Results may differ from the reference program's by a relative error of at most 0.015.
Values may be sent and summed in bfloat16 or wider, within the bound.
No kernel may reach another device: no remote copies, remote signals or barrier semaphores. Data moves between devices by JAX's collectives and lax.ppermute only.
A program may use at most 192 MiB of HBM per device.

```python
import math
import jax
import jax.numpy as jnp
from jax import lax

D = 1024
HEADS = 16
HDIM = 64
ROT = 16
FEAT = 64
FF = 4096
TOK_DEV = 1024
NSEQ = 4
SHORT = 128
TOKENS = 8192


def sequence_lengths(key):
    order = jax.random.permutation(key, NSEQ)
    others = jnp.where((order >= 2) & (order % 2 == 0), 2 * SHORT, SHORT)
    others = jnp.where(order == 0, 0, others)
    return jnp.where(order == 0, TOKENS - jnp.sum(others), others).astype(jnp.int32)


def draw_lengths(key, part):
    shared = sequence_lengths(key)
    return shared


def draw_pad_mask(key, part):
    seq_lengths = sequence_lengths(key)
    key = jax.random.fold_in(key, 5)
    padding = jax.random.randint(key, (NSEQ,), 0, SHORT // 4 + 1)
    seq_ends = jnp.cumsum(seq_lengths).astype(jnp.int32)
    index_all = jnp.arange(TOKENS).astype(jnp.int32)
    segment = jnp.sum((index_all[:, None] >= seq_ends[None, :]).astype(jnp.int32), 1)
    picked = segment[:, None] == jnp.arange(NSEQ)[None, :]
    limits = jnp.sum(jnp.where(picked, (seq_ends - padding)[None, :], 0), 1)
    return (index_all < limits).astype(jnp.int32)


def block_levels(key, shape, pieces, smallest, top_value):
    gain, own = 1.0, jax.random.fold_in(key, 6)
    for dim, parts in pieces:
        steps = jnp.exp(jax.random.uniform(jax.random.fold_in(own, dim), (parts,), jnp.float32, smallest / len(pieces), top_value / len(pieces)))
        gain = gain * jnp.repeat(steps, shape[dim] // parts).reshape([-1 if axis == dim else 1 for axis in range(len(shape))])
    return gain


def bell_draw(key, extent, width, most, split=(), dtype=jnp.bfloat16):
    loudness = block_levels(key, extent, split, -0.22, 0.18) if split else 1.0
    result = jax.random.normal(key, extent, jnp.float32) * width * loudness
    return jnp.minimum(jnp.maximum(result, -most), most).astype(dtype)


def setup_inputs(seed: int = 0) -> dict:
    keys = jax.random.split(jax.random.key(seed), 18)
    return {
        "tokens": bell_draw(keys[0], (TOKENS, D), 1.0, 6.0, ((0, 8), (1, 4))),
        "lengths": draw_lengths(jax.random.fold_in(keys[17], 71), 0),
        "pad_mask": draw_pad_mask(jax.random.fold_in(keys[17], 71), 0),
        "ln1_gain": jnp.clip(1.0 + 0.1 * jax.random.normal(keys[3], (D,), jnp.float32), 0.5, 1.5),
        "ln1_bias": bell_draw(keys[4], (D,), 0.3, 4.0, (), jnp.float32),
        "ln2_gain": jnp.clip(1.0 + 0.1 * jax.random.normal(keys[5], (D,), jnp.float32), 0.5, 1.5),
        "ln2_bias": bell_draw(keys[6], (D,), 0.3, 4.0, (), jnp.float32),
        "w_qkv": bell_draw(keys[7], (3, D, D), D ** -0.5, 0.1875, ((2, 4),)),
        "b_qkv": bell_draw(keys[8], (3, D), 0.3, 4.0, ((1, 4),), jnp.float32),
        "feat_weight": jnp.clip(jnp.exp(math.log(3.0) - 2.3025851 * jax.random.uniform(keys[9], (HEADS, FEAT), jnp.float32) ** block_levels(keys[9], (HEADS, FEAT), ((0, 4),), -0.2, 0.2)), 0.3, 3.0),
        "w_out": bell_draw(keys[10], (D, D), (D // 16) ** -0.5, 0.75, ((0, 4),)),
        "b_out": bell_draw(keys[11], (D,), 0.3, 4.0, (), jnp.float32),
        "w_in": bell_draw(keys[12], (D, FF), D ** -0.5, 0.1875, ((1, 4),)),
        "b_in": bell_draw(keys[13], (FF,), 0.3, 4.0, ((0, 4),), jnp.float32),
        "w_down": bell_draw(keys[14], (FF, D), FF ** -0.5, 0.09375, ((0, 4),)),
        "b_down": bell_draw(keys[15], (D,), 0.3, 4.0, (), jnp.float32),
        "grad_out": bell_draw(keys[16], (TOKENS, D), 1.0, 6.0, ((0, 8), (1, 4))),
    }


eps_norm = 1e-05
rope_base = 10000.0
feature_scale = 0.5
highest = lax.Precision.HIGHEST

@jax.custom_vjp
def low(v):
    return lax.optimization_barrier(v.astype(jnp.bfloat16)).astype(jnp.float32)

@jax.custom_vjp
def low_back(v):
    return v

def low_keep(v):
    return (low(v), None)

def low_pass(kept, grad):
    return (grad,)

def back_keep(v):
    return (v, None)

def back_low(kept, grad):
    return (low(grad),)
low.defvjp(low_keep, low_pass)
low_back.defvjp(back_keep, back_low)

def feature_table(feat_count, head_size):
    row_ids = jnp.arange(feat_count).astype(jnp.float32)
    col_ids = jnp.arange(head_size).astype(jnp.float32)
    cosines = jnp.cos(math.pi * (col_ids[None, :] + 0.5) * row_ids[:, None] / head_size)
    scaling = jnp.where(row_ids == 0, math.sqrt(1.0 / head_size), math.sqrt(2.0 / head_size))
    points = math.sqrt(2.0) * lax.erf_inv(2.0 * (row_ids + 0.5) / feat_count - 1.0)
    return feature_scale * (points * scaling)[:, None] * cosines

def rope_tables(position, rot_dims):
    half_dims = rot_dims // 2
    inverse = jnp.power(rope_base, -2.0 * jnp.arange(half_dims).astype(jnp.float32) / rot_dims)
    angles = position.astype(jnp.float32)[:, None] * inverse[None, :]
    return (jnp.cos(angles)[:, None, :], jnp.sin(angles)[:, None, :])

def rotate(values, cosine, sine):
    half_dims = cosine.shape[-1]
    first = values[..., :half_dims]
    second = values[..., half_dims:2 * half_dims]
    return jnp.concatenate([first * cosine - second * sine, second * cosine + first * sine, values[..., 2 * half_dims:]], -1)

def positions(lengths, index_all):
    seq_ends = jnp.cumsum(lengths).astype(jnp.int32)
    starts = (seq_ends - lengths).astype(jnp.int32)
    segment = lax.optimization_barrier(jnp.sum((index_all[:, None] >= seq_ends[None, :]).astype(jnp.int32), 1)).astype(jnp.int32)
    picked = segment[:, None] == jnp.arange(lengths.shape[0]).astype(jnp.int32)[None, :]
    position = (index_all - lax.optimization_barrier(jnp.sum(jnp.where(picked, starts[None, :], 0), 1))).astype(jnp.int32)
    return (segment, position)

def layer_block(param_set, carry_in, inputs):
    ln1_gain, ln1_bias, ln2_gain, ln2_bias, w_qkv, b_qkv, feat_weight, w_out, b_out, w_in, b_in, w_down, b_down = param_set
    block_x, segment, position, valid_keys = inputs
    block_rows = block_x.shape[0]
    state_in, norm_in, label_in = carry_in
    mean_row = lax.optimization_barrier(jnp.mean(block_x, -1, keepdims=True))
    centered = block_x - mean_row
    normed = centered * lax.rsqrt(lax.optimization_barrier(jnp.mean(centered * centered, -1, keepdims=True)) + eps_norm)
    ln1_out = low(normed * ln1_gain + ln1_bias)
    ln2_out = low(normed * ln2_gain + ln2_bias)
    qkv_all = low_back(jnp.einsum('td,cde->cte', ln1_out, w_qkv, precision=highest)) + b_qkv[:, None, :]
    cosine, sine = rope_tables(position, ROT)
    queries = rotate(qkv_all[0].reshape(block_rows, HEADS, HDIM), cosine, sine)
    keys_rot = rotate(qkv_all[1].reshape(block_rows, HEADS, HDIM), cosine, sine)
    values_low = low(qkv_all[2].reshape(block_rows, HEADS, HDIM))
    feat_table = feature_table(FEAT, HDIM)
    query_feat = low(feat_weight[None] * jnp.exp(jnp.einsum('thd,fd->thf', queries, feat_table, precision=highest)))
    key_feat = low(feat_weight[None] * jnp.exp(jnp.einsum('thd,fd->thf', keys_rot, feat_table, precision=highest)) * valid_keys[:, None, None])
    row_ids = jnp.arange(block_rows)
    joined = ((segment[:, None] == segment[None, :]) & (row_ids[:, None] >= row_ids[None, :])).astype(jnp.float32)
    raw_scores = jnp.einsum('thf,shf->hts', query_feat, key_feat, precision=highest) * joined[None]
    scores = low(low_back(raw_scores))
    enters = (segment == label_in).astype(jnp.float32)
    numerator = low_back(jnp.einsum('hts,shd->thd', scores, values_low, precision=highest)) + enters[:, None, None] * jnp.einsum('thf,hfd->thd', query_feat, state_in, precision=highest)
    denominator = lax.optimization_barrier(jnp.sum(scores, -1)).T + enters[:, None] * jnp.einsum('thf,hf->th', query_feat, norm_in, precision=highest)
    attended = low((numerator / denominator[:, :, None]).reshape(block_rows, D))
    last_seg = segment[-1]
    tail_rows = (segment == last_seg).astype(jnp.float32)[:, None, None]
    linked = (label_in == last_seg).astype(jnp.float32)
    state_out = linked * state_in + jnp.einsum('thf,thd->hfd', key_feat * tail_rows, values_low, precision=highest)
    norm_out = linked * norm_in + lax.optimization_barrier(jnp.sum(key_feat * tail_rows, 0))
    hidden = low(jax.nn.gelu(low_back(jnp.dot(ln2_out, w_in, precision=highest)) + b_in, approximate=False))
    mixed = block_x + jnp.dot(attended, w_out, precision=highest) + b_out + jnp.dot(hidden, w_down, precision=highest) + b_down
    return ((state_out, norm_out, last_seg), mixed)

def reference(tokens, lengths, pad_mask, ln1_gain, ln1_bias, ln2_gain, ln2_bias, w_qkv, b_qkv, feat_weight, w_out, b_out, w_in, b_in, w_down, b_down, grad_out):
    index_all = jnp.arange(TOKENS).astype(jnp.int32)
    segment, position = positions(lengths, index_all)
    block_rows = min(512, TOK_DEV)
    block_count = TOKENS // block_rows
    side = (segment.reshape(block_count, block_rows), position.reshape(block_count, block_rows), pad_mask.astype(jnp.float32).reshape(block_count, block_rows))
    param_set = (ln1_gain.astype(jnp.float32), ln1_bias.astype(jnp.float32), ln2_gain.astype(jnp.float32), ln2_bias.astype(jnp.float32), w_qkv.astype(jnp.float32), b_qkv.astype(jnp.float32), feat_weight.astype(jnp.float32), w_out.astype(jnp.float32), b_out.astype(jnp.float32), w_in.astype(jnp.float32), b_in.astype(jnp.float32), w_down.astype(jnp.float32), b_down.astype(jnp.float32))

    def forward(tokens_in, params_in):
        step_fn = jax.checkpoint(layer_block)

        def scan_step(carry_in, inputs):
            return step_fn(params_in, carry_in, inputs)
        initial = (jnp.zeros((HEADS, FEAT, HDIM), jnp.float32), jnp.zeros((HEADS, FEAT), jnp.float32), jnp.zeros((), jnp.int32))
        final_carry, outputs = lax.scan(scan_step, initial, (tokens_in.reshape(block_count, block_rows, D),) + side)
        return outputs.reshape(TOKENS, D)
    mixed, pull_back = jax.vjp(forward, tokens.astype(jnp.float32), param_set)
    grad_tokens, grad_params = pull_back(grad_out.astype(jnp.float32))
    return (mixed.astype(jnp.bfloat16), grad_tokens, grad_params[0], grad_params[1], grad_params[2], grad_params[3], grad_params[4], grad_params[5], grad_params[6], grad_params[7], grad_params[8], grad_params[9], grad_params[10], grad_params[11], grad_params[12])
```

```python
import functools
import math
from statistics import NormalDist

import jax
import jax.numpy as jnp
import numpy as np
from jax import lax
from jax.experimental import pallas as pl
from jax.experimental.pallas import tpu as pltpu
from jax.sharding import PartitionSpec as P

ROT = 16
eps_norm = 1e-05
rope_base = 10000.0
feature_scale = 0.5
BT = 256
LANES = 128
bf16 = jnp.bfloat16
f32 = jnp.float32
VMEM_LIMIT = 56 * 1024 * 1024


def nn(a, b):
    return lax.dot_general(a, b, (((1,), (0,)), ((), ())), preferred_element_type=f32)


def nt(a, b):
    return lax.dot_general(a, b, (((1,), (1,)), ((), ())), preferred_element_type=f32)


def tn(a, b):
    return lax.dot_general(a, b, (((0,), (0,)), ((), ())), preferred_element_type=f32)


def split(x):
    hi = x.astype(bf16)
    return hi, (x - hi.astype(f32)).astype(bf16)


def feature_table(feat_count, head_size):
    rows = np.arange(feat_count)
    cols = np.arange(head_size)
    cosines = np.cos(math.pi * (cols[None, :] + 0.5) * rows[:, None] / head_size)
    scaling = np.where(rows == 0, math.sqrt(1.0 / head_size), math.sqrt(2.0 / head_size))
    points = np.array([NormalDist().inv_cdf((r + 0.5) / feat_count) for r in range(feat_count)])
    return feature_scale * (points * scaling)[:, None] * cosines


def lane_head(shape, head_size):
    return lax.broadcasted_iota(jnp.int32, shape, len(shape) - 1) // head_size


def block_ones(size, head_size):
    rows = lax.broadcasted_iota(jnp.int32, (size, size), 0) // head_size
    cols = lax.broadcasted_iota(jnp.int32, (size, size), 1) // head_size
    return rows == cols


def swap_halves(x, head_size):
    width = x.shape[1]
    lane = lax.broadcasted_iota(jnp.int32, x.shape, 1) % head_size
    ahead = pltpu.roll(x, width - ROT // 2, 1)
    behind = pltpu.roll(x, ROT // 2, 1)
    return jnp.where(lane < ROT // 2, ahead, behind)


def widen(table, width):
    return table if table.shape[1] == width else jnp.concatenate([table] * (width // table.shape[1]), 1)


def pack_state(state, norm, head_size):
    size = state.shape[0]
    masked = jnp.where(block_ones(size, head_size), state, 0.0)
    packed = masked[:head_size]
    for h in range(1, size // head_size):
        packed = packed + masked[h * head_size : (h + 1) * head_size]
    return packed, norm


def unpack_state(packed, head_size):
    size = packed.shape[1]
    rows = jnp.concatenate([packed[:head_size]] * (size // head_size), 0)
    return jnp.where(block_ones(size, head_size), rows, 0.0)


def pre_kernel(
    head_size,
    labels_ref,
    x_ref,
    gains_ref,
    w_ref,
    bq_ref,
    fw_ref,
    tab_ref,
    cos_ref,
    sin_ref,
    valid_ref,
    seg_ref,
    ln1t_ref,
    ln2_ref,
    ln2t_ref,
    xhat_ref,
    inv_ref,
    qe_ref,
    ke_ref,
    qf_ref,
    kf_ref,
    v_ref,
    pk_ref,
    state_ref,
    norm_ref,
):
    step = pl.program_id(0)
    width = qe_ref.shape[1]
    x = x_ref[...].astype(f32)
    centered = x - jnp.mean(x, -1, keepdims=True)
    inv = lax.rsqrt(jnp.mean(centered * centered, -1, keepdims=True) + eps_norm)
    xhat = centered * inv
    inv_ref[...] = inv
    xhat_ref[...] = xhat.astype(bf16)
    ln1 = (xhat * gains_ref[0:1] + gains_ref[1:2]).astype(bf16)
    ln2 = (xhat * gains_ref[2:3] + gains_ref[3:4]).astype(bf16)
    ln2_ref[...] = ln2
    ln1t_ref[...] = ln1.T
    ln2t_ref[...] = ln2.T
    cosine = widen(cos_ref[...], width)
    sine = widen(sin_ref[...], width)

    def features(c):
        raw = nn(ln1, w_ref[c]) + bq_ref[c : c + 1]
        turned = raw * cosine + swap_halves(raw, head_size) * sine
        hi, lo = split(turned)
        return jnp.exp(nn(hi, tab_ref[0]) + nn(lo, tab_ref[0]) + nn(hi, tab_ref[1]))

    fw = fw_ref[...]
    qe = features(0)
    ke = features(1) * valid_ref[...]
    qe_ref[...] = qe
    ke_ref[...] = ke
    qf_ref[...] = (fw * qe).astype(bf16)
    kf = (fw * ke).astype(bf16)
    kf_ref[...] = kf
    v = (nn(ln1, w_ref[2]) + bq_ref[2:3]).astype(bf16)
    v_ref[...] = v

    @pl.when(step == 0)
    def _():
        state_ref[...] = jnp.zeros_like(state_ref)
        norm_ref[...] = jnp.zeros_like(norm_ref)

    tail = kf.astype(f32) * (seg_ref[...] == labels_ref[pl.num_programs(0) - 1, 1]).astype(f32)
    state_ref[...] += tn(tail.astype(bf16), v)
    norm_ref[...] += jnp.broadcast_to(jnp.sum(tail, 0, keepdims=True), norm_ref.shape)

    @pl.when(step == pl.num_programs(0) - 1)
    def _():
        packed, norm = pack_state(state_ref[...], norm_ref[...], head_size)
        pk_ref[:head_size] = packed
        pk_ref[head_size:] = norm


def ff_kernel(ln2_ref, ln2t_ref, grad_ref, win_ref, bin_ref, wdown_ref, hid_ref, dpre_ref, gdown_ref, gin_ref, gb_ref):
    rows = ln2_ref.shape[0]
    half = rows // 4
    sums = jnp.zeros((1, win_ref.shape[1]), f32)
    for r in range(4):
        part = slice(r * half, (r + 1) * half)
        pre = nn(ln2_ref[part], win_ref[...]) + bin_ref[...]
        phi_cum = 0.5 + 0.5 * lax.erf(pre * (1.0 / math.sqrt(2.0)))
        hid_ref[part] = (pre * phi_cum).astype(bf16)
        slope = phi_cum + pre * jnp.exp(-0.5 * pre * pre) * (1.0 / math.sqrt(2.0 * math.pi))
        dpre = nt(grad_ref[part], wdown_ref[...]) * slope
        sums = sums + jnp.sum(dpre, 0, keepdims=True)
        dpre_ref[part] = dpre.astype(bf16)
    gb_ref[...] = sums
    gdown_ref[...] = tn(hid_ref[...], grad_ref[...]).astype(bf16)
    gin_ref[...] = nn(ln2t_ref[...], dpre_ref[...]).astype(bf16)


def attn_kernel(
    head_size,
    labels_ref,
    qf_ref,
    kf_ref,
    v_ref,
    grad_ref,
    wout_ref,
    segc_ref,
    segr_ref,
    spk_ref,
    att_ref,
    dq_ref,
    dk_ref,
    dv_ref,
    gb_ref,
    gzb_ref,
    gpk_ref,
    state_ref,
    norm_ref,
    lead_ref,
    leadz_ref,
):
    step = pl.program_id(0)
    last = pl.num_programs(0) - 1
    rows, width = qf_ref.shape
    heads = width // head_size
    same = block_ones(width, head_size)
    ones = same.astype(f32).astype(bf16)

    def head_sum(x):
        hi, lo = split(x)
        return nn(hi, ones) + nn(lo, ones)

    @pl.when(step == 0)
    def _():
        state_ref[...] = unpack_state(spk_ref[...], head_size)
        norm_ref[...] = spk_ref[head_size : head_size + 8]
        lead_ref[...] = jnp.zeros_like(lead_ref)
        leadz_ref[...] = jnp.zeros_like(leadz_ref)

    seg = segc_ref[...]
    enters = (seg == labels_ref[step, 0]).astype(f32)
    tail = (seg == labels_ref[step, 1]).astype(f32)
    lead = (seg == labels_ref[0, 2]).astype(f32)
    linked = (labels_ref[step, 0] == labels_ref[step, 1]).astype(f32)
    qf = qf_ref[...]
    kf = kf_ref[...]
    v = v_ref[...]
    qf32 = qf.astype(f32)
    norm = norm_ref[0:1]
    lane = lane_head((rows, width), head_size)
    zero16 = jnp.zeros((rows, width), bf16)

    def stack(x):
        return jnp.concatenate([jnp.where(lane == h, x, zero16) for h in range(heads)], 0)

    def unstack(x):
        total = jnp.where(lane == 0, x[:rows], 0.0)
        for h in range(1, heads):
            total = jnp.where(lane == h, x[h * rows : (h + 1) * rows], total)
        return total

    causal = lax.broadcasted_iota(jnp.int32, (rows, rows), 0) >= lax.broadcasted_iota(
        jnp.int32, (rows, rows), 1
    )
    joined = causal & (seg == segr_ref[...])
    joined_all = jnp.concatenate([joined.astype(f32)] * heads, 0)
    q_stack = stack(qf)
    scores = (nt(q_stack, kf) * joined_all).astype(bf16)
    ones_v = jnp.ones((rows, LANES), bf16)
    sums = nn(scores, ones_v)
    den_in = jnp.where(lane == 0, widen(sums[:rows], width), 0.0)
    for h in range(1, heads):
        den_in = jnp.where(lane == h, widen(sums[h * rows : (h + 1) * rows], width), den_in)
    s_hi, s_lo = split(state_ref[...])
    num = unstack(nn(scores, v)) + enters * (nn(qf, s_hi) + nn(qf, s_lo))
    den = den_in + enters * head_sum(qf32 * norm)
    inv_den = 1.0 / den
    att = num * inv_den
    att_ref[...] = att.astype(bf16)
    d_att = nt(grad_ref[...], wout_ref[...])
    d_num = d_att * inv_den
    d_den = -head_sum(d_att * att) * inv_den
    dn_hi, dn_lo = split(d_num)
    dn_stack = stack(dn_hi)
    dden_all = jnp.concatenate([d_den[:, h * head_size : h * head_size + 1] for h in range(heads)], 0)
    d_scores = ((nt(dn_stack, v) + dden_all) * joined_all).astype(bf16)
    inter = nt(dn_hi, s_hi) + nt(dn_lo, s_hi) + nt(dn_hi, s_lo) + d_den * norm
    dq_ref[...] = unstack(nn(d_scores, kf)) + enters * inter
    dk_ref[...] = tn(d_scores, q_stack)
    dv_ref[...] = tn(scores, dn_stack)
    q_in = (qf32 * enters).astype(bf16)
    gb_ref[0] = jnp.where(same, tn(q_in, dn_hi) + tn(q_in, dn_lo), 0.0)
    weighted = qf32 * d_den
    gzb_ref[0] = jnp.broadcast_to(jnp.sum(weighted * enters, 0, keepdims=True), (8, width))
    q_lead = (qf32 * lead).astype(bf16)
    lead_ref[...] += tn(q_lead, dn_hi) + tn(q_lead, dn_lo)
    leadz_ref[...] += jnp.broadcast_to(jnp.sum(weighted * lead, 0, keepdims=True), (8, width))
    k_tail = kf.astype(f32) * tail
    state_ref[...] = linked * state_ref[...] + jnp.where(same, tn(k_tail.astype(bf16), v), 0.0)
    norm_ref[...] = linked * norm_ref[...] + jnp.broadcast_to(jnp.sum(k_tail, 0, keepdims=True), (8, width))

    @pl.when(step == last)
    def _():
        packed, z = pack_state(lead_ref[...], leadz_ref[...], head_size)
        gpk_ref[:head_size] = packed
        gpk_ref[head_size:] = z


def value_kernel(
    hid_ref,
    wdown_ref,
    att_ref,
    wout_ref,
    dpre_ref,
    win_ref,
    grad_ref,
    xhat_ref,
    gains_ref,
    val_ref,
    e2_ref,
    sums_ref,
    gwout_ref,
    acc_ref,
):
    step = pl.program_id(0)
    val_ref[...] = (nn(hid_ref[...], wdown_ref[...]) + nn(att_ref[...], wout_ref[...])).astype(bf16)
    d_ln2 = nt(dpre_ref[...], win_ref[...])
    e2_ref[...] = (d_ln2 * gains_ref[2:3]).astype(bf16)

    @pl.when(step == 0)
    def _():
        sums_ref[...] = jnp.zeros_like(sums_ref)
        acc_ref[...] = jnp.zeros_like(acc_ref)

    sums_ref[0:1] += jnp.sum(d_ln2 * xhat_ref[...].astype(f32), 0, keepdims=True)
    sums_ref[1:2] += jnp.sum(d_ln2, 0, keepdims=True)
    acc_ref[...] += tn(att_ref[...], grad_ref[...])

    @pl.when(step == pl.num_programs(0) - 1)
    def _():
        gwout_ref[...] = acc_ref[...].astype(bf16)


def tail_kernel(
    head_size,
    labels_ref,
    dq_ref,
    dk_ref,
    dv_ref,
    qe_ref,
    ke_ref,
    kf_ref,
    v_ref,
    gb_ref,
    gzb_ref,
    gin_ref,
    segc_ref,
    cos_ref,
    sin_ref,
    fw_ref,
    tab_ref,
    w_ref,
    ln1t_ref,
    xhat_ref,
    e2_ref,
    gains_ref,
    e_ref,
    stat_ref,
    sums_ref,
    small_ref,
    gw_ref,
    state_ref,
    norm_ref,
    low_ref,
):
    step = pl.program_id(0)
    last = pl.num_programs(0) - 1
    block = last - step
    rows, width = dq_ref.shape

    @pl.when(step == 0)
    def _():
        state_ref[...] = unpack_state(gin_ref[...], head_size)
        norm_ref[...] = gin_ref[head_size : head_size + 8]
        sums_ref[...] = jnp.zeros_like(sums_ref)
        small_ref[...] = jnp.zeros_like(small_ref)

    tail = (segc_ref[...] == labels_ref[block, 1]).astype(f32)
    linked = (labels_ref[block, 0] == labels_ref[block, 1]).astype(f32)
    g_hi, g_lo = split(state_ref[...])
    v = v_ref[...]
    kf = kf_ref[...]
    dk = dk_ref[...] + tail * (nt(v, g_hi) + nt(v, g_lo) + norm_ref[0:1])
    dv = dv_ref[...] + tail * (nn(kf, g_hi) + nn(kf, g_lo))
    state_ref[...] = linked * state_ref[...] + gb_ref[0]
    norm_ref[...] = linked * norm_ref[...] + gzb_ref[0]
    fw = fw_ref[...]
    gq = dq_ref[...] * qe_ref[...]
    gk = dk * ke_ref[...]
    cosine = widen(cos_ref[...], width)
    sine = widen(sin_ref[...], width)

    def back(g):
        hi, lo = split(g * fw)
        turned = nt(hi, tab_ref[0]) + nt(lo, tab_ref[0]) + nt(hi, tab_ref[1])
        return turned * cosine - swap_halves(turned, head_size) * sine

    dq_raw = back(gq)
    dk_raw = back(gk)
    small_ref[0:1] += jnp.sum(dq_raw, 0, keepdims=True)
    small_ref[1:2] += jnp.sum(dk_raw, 0, keepdims=True)
    small_ref[2:3] += jnp.sum(dv, 0, keepdims=True)
    small_ref[3:4] += jnp.sum(gq + gk, 0, keepdims=True)
    lows = [d.astype(bf16) for d in (dq_raw, dk_raw, dv)]
    d_ln1 = nt(lows[0], w_ref[0]) + nt(lows[1], w_ref[1]) + nt(lows[2], w_ref[2])
    start = pl.multiple_of(block * rows, rows)
    for c in range(3):
        low_ref[c, pl.ds(start, rows)] = lows[c]
    xhat = xhat_ref[...].astype(f32)
    e = d_ln1 * gains_ref[0:1] + e2_ref[...].astype(f32)
    e_ref[...] = e.astype(bf16)
    stat_ref[:, 0:1] = jnp.sum(e, 1, keepdims=True)
    stat_ref[:, 1:2] = jnp.sum(e * xhat, 1, keepdims=True)
    sums_ref[0:1] += jnp.sum(d_ln1 * xhat, 0, keepdims=True)
    sums_ref[1:2] += jnp.sum(d_ln1, 0, keepdims=True)

    @pl.when(step == last)
    def _():
        for c in range(3):
            gw_ref[c] = nn(ln1t_ref[...], low_ref[c]).astype(bf16)


def whole(*shape):
    return pl.BlockSpec(shape, lambda *_: (0,) * len(shape))


def rows_of(*shape):
    return pl.BlockSpec(shape, lambda i: (i,) + (0,) * (len(shape) - 1))


def smem():
    return pl.BlockSpec(memory_space=pltpu.SMEM)


def sds(shape, dtype):
    return jax.ShapeDtypeStruct(shape, dtype)


def call(kernel, grid, in_specs, out_specs, out_shape, scratch, flops, moved):
    return pl.pallas_call(
        kernel,
        grid=(grid,),
        in_specs=in_specs,
        out_specs=out_specs,
        out_shape=out_shape,
        scratch_shapes=scratch,
        compiler_params=pltpu.CompilerParams(vmem_limit_bytes=VMEM_LIMIT),
        cost_estimate=pl.CostEstimate(flops=int(flops), bytes_accessed=int(moved), transcendentals=0),
    )


def neighbour_sum(packet, sign):
    count = lax.axis_size("seq")
    outer = 4 if count % 4 == 0 else 1
    inner = count // outer
    me = lax.axis_index("seq")
    mine = me % inner
    group = packet
    before = jnp.zeros_like(packet)
    for k in range(1, inner):
        route = [(i, i - i % inner + (i % inner + k) % inner) for i in range(count)]
        got = lax.ppermute(packet, "seq", route)
        sender = (mine - k) % inner
        group = group + got
        before = before + jnp.where((sender < mine) if sign > 0 else (sender > mine), got, 0.0)
    for k in range(1, outer):
        shift = sign * k * inner
        route = [(i, i + shift) for i in range(count) if 0 <= i + shift < count]
        before = before + lax.ppermute(group, "seq", route)
    return before


def body(
    tokens,
    lengths,
    pad_mask,
    ln1_gain,
    ln1_bias,
    ln2_gain,
    ln2_bias,
    w_qkv,
    b_qkv,
    feat_weight,
    w_out,
    b_out,
    w_in,
    b_in,
    w_down,
    b_down,
    grad_out,
):
    rows, share = tokens.shape
    heads, feats = feat_weight.shape
    width = w_qkv.shape[2]
    head_size = width // heads
    model, hidden = w_in.shape
    blocks = rows // BT
    n_head = lax.axis_size("head")
    offset = lax.axis_index("head") * share
    full_tokens = lax.all_gather(tokens, "head", axis=1, tiled=True)
    full_grad = lax.all_gather(grad_out, "head", axis=1, tiled=True)

    index_all = lax.axis_index("seq") * rows + jnp.arange(rows, dtype=jnp.int32)
    seq_ends = jnp.cumsum(lengths).astype(jnp.int32)
    starts = seq_ends - lengths

    def seg_of(index):
        return jnp.sum((index[:, None] >= seq_ends[None, :]).astype(jnp.int32), 1)

    segment = seg_of(index_all)
    picked = segment[:, None] == jnp.arange(lengths.shape[0])[None, :]
    position = index_all - jnp.sum(jnp.where(picked, starts[None, :], 0), 1)
    base = lax.axis_index("seq") * rows + jnp.arange(blocks, dtype=jnp.int32) * BT
    label_in = seg_of(jnp.maximum(base - 1, 0))
    label_last = seg_of(base + (BT - 1))
    label_first = jnp.broadcast_to(segment[0], (blocks,))
    labels = jnp.stack([label_in, label_last, label_first], 1)
    seg_col = segment[:, None]
    seg_row = segment[None, :]
    lane = np.arange(LANES) % head_size
    inverse = np.where(lane < ROT, rope_base ** (-2.0 * (lane % (ROT // 2)) / ROT), 0.0)
    angles = position.astype(f32)[:, None] * jnp.asarray(inverse, f32)[None, :]
    sign = np.where(lane < ROT // 2, -1.0, np.where(lane < ROT, 1.0, 0.0))
    cosine = jnp.cos(angles)
    sine = jnp.sin(angles) * jnp.asarray(sign, f32)[None, :]
    valid = pad_mask.astype(f32)[:, None]
    table = np.kron(np.eye(heads), feature_table(feats, head_size).T).astype(np.float32)
    table_hi = table.astype(bf16)
    table_lo = (table - table_hi.astype(np.float32)).astype(bf16)
    tab = jnp.asarray(np.stack([table_hi, table_lo]))
    gains = jnp.stack([ln1_gain, ln1_bias, ln2_gain, ln2_bias])
    fw = feat_weight.reshape(1, width)
    packet_shape = (head_size + 8, width)

    ln1t, ln2, ln2t, xhat, inv_std, q_expo, k_expo, qf, kf, v, s_own = call(
        functools.partial(pre_kernel, head_size),
        blocks,
        [
            smem(),
            rows_of(BT, model),
            whole(4, model),
            whole(3, model, width),
            whole(3, width),
            whole(1, width),
            whole(2, width, width),
            rows_of(BT, LANES),
            rows_of(BT, LANES),
            rows_of(BT, 1),
            rows_of(BT, 1),
        ],
        [
            pl.BlockSpec((model, BT), lambda i: (0, i)),
            rows_of(BT, model),
            pl.BlockSpec((model, BT), lambda i: (0, i)),
            rows_of(BT, model),
            rows_of(BT, 1),
            rows_of(BT, width),
            rows_of(BT, width),
            rows_of(BT, width),
            rows_of(BT, width),
            rows_of(BT, width),
            whole(*packet_shape),
        ],
        [
            sds((model, rows), bf16),
            sds((rows, model), bf16),
            sds((model, rows), bf16),
            sds((rows, model), bf16),
            sds((rows, 1), f32),
            sds((rows, width), f32),
            sds((rows, width), f32),
            sds((rows, width), bf16),
            sds((rows, width), bf16),
            sds((rows, width), bf16),
            sds(packet_shape, f32),
        ],
        [pltpu.VMEM((width, width), f32), pltpu.VMEM((8, width), f32)],
        2 * rows * model * 3 * width + 16 * rows * width * width,
        rows * model * 10 + 6 * model * width,
    )(labels, full_tokens, gains, w_qkv, b_qkv, fw, tab, cosine, sine, valid, seg_col)

    s_in = neighbour_sum(s_own, 1)

    fb = 256
    hid, dpre, g_down, g_in, gb_in = call(
        ff_kernel,
        hidden // fb,
        [
            whole(rows, model),
            whole(model, rows),
            whole(rows, model),
            pl.BlockSpec((model, fb), lambda i: (0, i)),
            pl.BlockSpec((1, fb), lambda i: (0, i)),
            pl.BlockSpec((fb, model), lambda i: (i, 0)),
        ],
        [
            pl.BlockSpec((rows, fb), lambda i: (0, i)),
            pl.BlockSpec((rows, fb), lambda i: (0, i)),
            pl.BlockSpec((fb, model), lambda i: (i, 0)),
            pl.BlockSpec((model, fb), lambda i: (0, i)),
            pl.BlockSpec((1, fb), lambda i: (0, i)),
        ],
        [
            sds((rows, hidden), bf16),
            sds((rows, hidden), bf16),
            sds((hidden, model), bf16),
            sds((model, hidden), bf16),
            sds((1, hidden), f32),
        ],
        [],
        8 * rows * model * hidden,
        6 * rows * model + 8 * model * hidden,
    )(ln2, ln2t, full_grad, w_in, b_in[None, :], w_down)

    g_down = lax.psum(g_down, "seq")
    g_in = lax.psum(g_in, "seq")

    att, dq, dk, dv, gb, gzb, g_own = call(
        functools.partial(attn_kernel, head_size),
        blocks,
        [
            smem(),
            rows_of(BT, width),
            rows_of(BT, width),
            rows_of(BT, width),
            rows_of(BT, model),
            whole(width, model),
            rows_of(BT, 1),
            pl.BlockSpec((1, BT), lambda i: (0, i)),
            whole(*packet_shape),
        ],
        [
            rows_of(BT, width),
            rows_of(BT, width),
            rows_of(BT, width),
            rows_of(BT, width),
            rows_of(1, width, width),
            rows_of(1, 8, width),
            whole(*packet_shape),
        ],
        [
            sds((rows, width), bf16),
            sds((rows, width), f32),
            sds((rows, width), f32),
            sds((rows, width), f32),
            sds((blocks, width, width), f32),
            sds((blocks, 8, width), f32),
            sds(packet_shape, f32),
        ],
        [
            pltpu.VMEM((width, width), f32),
            pltpu.VMEM((8, width), f32),
            pltpu.VMEM((width, width), f32),
            pltpu.VMEM((8, width), f32),
        ],
        24 * rows * heads * BT * width,
        rows * model * 2 + rows * width * 20,
    )(labels, qf, kf, v, full_grad, w_out, seg_col, seg_row, s_in)

    grad_in = neighbour_sum(g_own, -1)

    value, e2, sums2, g_out = call(
        value_kernel,
        blocks,
        [
            rows_of(BT, hidden),
            whole(hidden, model),
            rows_of(BT, width),
            whole(width, model),
            rows_of(BT, hidden),
            whole(model, hidden),
            rows_of(BT, model),
            rows_of(BT, model),
            whole(4, model),
        ],
        [rows_of(BT, model), rows_of(BT, model), whole(8, model), whole(width, model)],
        [
            sds((rows, model), bf16),
            sds((rows, model), bf16),
            sds((8, model), f32),
            sds((width, model), bf16),
        ],
        [pltpu.VMEM((width, model), f32)],
        4 * rows * model * (hidden + width),
        12 * rows * model + 4 * model * hidden,
    )(hid, w_down, att, w_out, dpre, w_in, full_grad, xhat, gains)

    mixed_share = lax.psum_scatter(value, "head", scatter_dimension=1, tiled=True)

    def back_rows(*shape):
        return pl.BlockSpec(shape, lambda i: (blocks - 1 - i,) + (0,) * (len(shape) - 1))

    e_part, stats, sums1, small, g_qkv = call(
        functools.partial(tail_kernel, head_size),
        blocks,
        [
            smem(),
            back_rows(BT, width),
            back_rows(BT, width),
            back_rows(BT, width),
            back_rows(BT, width),
            back_rows(BT, width),
            back_rows(BT, width),
            back_rows(BT, width),
            back_rows(1, width, width),
            back_rows(1, 8, width),
            whole(*packet_shape),
            back_rows(BT, 1),
            back_rows(BT, LANES),
            back_rows(BT, LANES),
            whole(1, width),
            whole(2, width, width),
            whole(3, model, width),
            whole(model, rows),
            back_rows(BT, model),
            back_rows(BT, model),
            whole(4, model),
        ],
        [
            back_rows(BT, model),
            back_rows(BT, 2),
            whole(8, model),
            whole(8, width),
            whole(3, model, width),
        ],
        [
            sds((rows, model), bf16),
            sds((rows, 2), f32),
            sds((8, model), f32),
            sds((8, width), f32),
            sds((3, model, width), bf16),
        ],
        [
            pltpu.VMEM((width, width), f32),
            pltpu.VMEM((8, width), f32),
            pltpu.VMEM((3, rows, width), bf16),
        ],
        4 * rows * model * 3 * width,
        rows * width * 30 + rows * model * 8,
    )(
        labels,
        dq,
        dk,
        dv,
        q_expo,
        k_expo,
        kf,
        v,
        gb,
        gzb,
        grad_in,
        seg_col,
        cosine,
        sine,
        fw,
        tab,
        w_qkv,
        ln1t,
        xhat,
        e2,
        gains,
    )

    g_qkv, g_out = lax.psum((g_qkv, g_out), "seq")
    e_share = lax.psum_scatter(e_part, "head", scatter_dimension=1, tiled=True)
    stats, gain_sums = lax.psum((stats, jnp.concatenate([sums1[:2], sums2[:2]], 0)), "head")
    bias_out = jnp.sum(grad_out.astype(f32), 0)
    gain_share = lax.dynamic_slice_in_dim(gain_sums, offset, share, 1)
    gain_share, small, gb_in, bias_out = lax.psum((gain_share, small[:4], gb_in, bias_out), "seq")

    bias = lax.dynamic_slice_in_dim(b_out, offset, share) + lax.dynamic_slice_in_dim(b_down, offset, share)
    mixed = (tokens.astype(f32) + mixed_share.astype(f32) + bias).astype(bf16)
    xhat_share = lax.dynamic_slice_in_dim(xhat, offset, share, 1).astype(f32)
    stats = stats * (1.0 / model)
    grad_input = grad_out.astype(f32) + inv_std * (
        e_share.astype(f32) - stats[:, 0:1] - xhat_share * stats[:, 1:2]
    )
    return (
        mixed,
        grad_input,
        gain_share[0],
        gain_share[1],
        gain_share[2],
        gain_share[3],
        g_qkv.astype(f32),
        small[:3],
        small[3].reshape(heads, feats),
        g_out.astype(f32),
        bias_out,
        g_in.astype(f32),
        gb_in[0],
        g_down.astype(f32),
        bias_out,
    )


def solution(mesh):
    in_specs = (
        P("seq", "head"),
        P(),
        P("seq"),
        P(),
        P(),
        P(),
        P(),
        P(None, None, "head"),
        P(None, "head"),
        P("head", None),
        P("head", None),
        P(),
        P(None, "head"),
        P("head"),
        P("head", None),
        P(),
        P("seq", "head"),
    )
    out_specs = (
        P("seq", "head"),
        P("seq", "head"),
        P("head"),
        P("head"),
        P("head"),
        P("head"),
        P(None, None, "head"),
        P(None, "head"),
        P("head", None),
        P("head", None),
        P("head"),
        P(None, "head"),
        P("head"),
        P("head", None),
        P("head"),
    )
    return jax.shard_map(body, mesh=mesh, in_specs=in_specs, out_specs=out_specs, check_vma=False)
```

```python
import functools
import math
from statistics import NormalDist

import jax
import jax.numpy as jnp
import numpy as np
from jax import lax
from jax.experimental import pallas as pl
from jax.experimental.pallas import tpu as pltpu
from jax.sharding import PartitionSpec as P

ROT = 16
eps_norm = 1e-05
rope_base = 10000.0
feature_scale = 0.5
BT = 256
LANES = 128
bf16 = jnp.bfloat16
f32 = jnp.float32
COST_SCALE = 0.02
END_COST = 12
VMEM_LIMIT = 56 * 1024 * 1024


def nn(a, b):
    return lax.dot_general(a, b, (((1,), (0,)), ((), ())), preferred_element_type=f32)


def nt(a, b):
    return lax.dot_general(a, b, (((1,), (1,)), ((), ())), preferred_element_type=f32)


def tn(a, b):
    return lax.dot_general(a, b, (((0,), (0,)), ((), ())), preferred_element_type=f32)


def split(x):
    hi = x.astype(bf16)
    return hi, (x - hi.astype(f32)).astype(bf16)


def feature_table(feat_count, head_size):
    rows = np.arange(feat_count)
    cols = np.arange(head_size)
    cosines = np.cos(math.pi * (cols[None, :] + 0.5) * rows[:, None] / head_size)
    scaling = np.where(rows == 0, math.sqrt(1.0 / head_size), math.sqrt(2.0 / head_size))
    points = np.array([NormalDist().inv_cdf((r + 0.5) / feat_count) for r in range(feat_count)])
    return feature_scale * (points * scaling)[:, None] * cosines


def lane_head(shape, head_size):
    return lax.broadcasted_iota(jnp.int32, shape, len(shape) - 1) // head_size


def block_ones(size, head_size):
    rows = lax.broadcasted_iota(jnp.int32, (size, size), 0) // head_size
    cols = lax.broadcasted_iota(jnp.int32, (size, size), 1) // head_size
    return rows == cols


def swap_halves(x, head_size):
    width = x.shape[1]
    lane = lax.broadcasted_iota(jnp.int32, x.shape, 1) % head_size
    ahead = pltpu.roll(x, width - ROT // 2, 1)
    behind = pltpu.roll(x, ROT // 2, 1)
    return jnp.where(lane < ROT // 2, ahead, behind)


def widen(table, width):
    return table if table.shape[1] == width else jnp.concatenate([table] * (width // table.shape[1]), 1)


def pack_state(state, norm, head_size):
    size = state.shape[0]
    masked = jnp.where(block_ones(size, head_size), state, 0.0)
    packed = masked[:head_size]
    for h in range(1, size // head_size):
        packed = packed + masked[h * head_size : (h + 1) * head_size]
    return packed, norm


def unpack_state(packed, head_size):
    size = packed.shape[1]
    rows = jnp.concatenate([packed[:head_size]] * (size // head_size), 0)
    return jnp.where(block_ones(size, head_size), rows, 0.0)


def place(full_ref, piece_refs, me_ref):
    for k, ref in enumerate(piece_refs):
        size = ref.shape[1]
        start = pl.multiple_of((me_ref[0] ^ k) * size, LANES)
        full_ref[:, pl.ds(start, size)] = ref[...]


def pre_kernel(
    head_size,
    pieces,
    labels_ref,
    me_ref,
    *refs,
):
    x_refs = refs[:pieces]
    (
        gains_ref,
        w_ref,
        bq_ref,
        fw_ref,
        tab_ref,
        cos_ref,
        sin_ref,
        valid_ref,
        seg_ref,
        ln1t_ref,
        ln2_ref,
        ln2t_ref,
        xhat_ref,
        inv_ref,
        qe_ref,
        ke_ref,
        qf_ref,
        kf_ref,
        v_ref,
        pk_ref,
        full_ref,
        state_ref,
        norm_ref,
    ) = refs[pieces:]
    step = pl.program_id(0)
    width = qe_ref.shape[1]
    place(full_ref, x_refs, me_ref)
    x = full_ref[...].astype(f32)
    centered = x - jnp.mean(x, -1, keepdims=True)
    inv = lax.rsqrt(jnp.mean(centered * centered, -1, keepdims=True) + eps_norm)
    xhat = centered * inv
    inv_ref[...] = inv
    xhat_ref[...] = xhat.astype(bf16)
    ln1 = (xhat * gains_ref[0:1] + gains_ref[1:2]).astype(bf16)
    ln2 = (xhat * gains_ref[2:3] + gains_ref[3:4]).astype(bf16)
    ln2_ref[...] = ln2
    ln1t_ref[...] = ln1.T
    ln2t_ref[...] = ln2.T
    cosine = widen(cos_ref[...], width)
    sine = widen(sin_ref[...], width)

    def features(c):
        raw = nn(ln1, w_ref[c]) + bq_ref[c : c + 1]
        turned = raw * cosine + swap_halves(raw, head_size) * sine
        hi, lo = split(turned)
        return jnp.exp(nn(hi, tab_ref[0]) + nn(lo, tab_ref[0]) + nn(hi, tab_ref[1]))

    fw = fw_ref[...]
    qe = features(0)
    ke = features(1) * valid_ref[...]
    qe_ref[...] = qe
    ke_ref[...] = ke
    qf_ref[...] = (fw * qe).astype(bf16)
    kf = (fw * ke).astype(bf16)
    kf_ref[...] = kf
    v = (nn(ln1, w_ref[2]) + bq_ref[2:3]).astype(bf16)
    v_ref[...] = v

    @pl.when(step == 0)
    def _():
        state_ref[...] = jnp.zeros_like(state_ref)
        norm_ref[...] = jnp.zeros_like(norm_ref)

    tail = kf.astype(f32) * (seg_ref[...] == labels_ref[pl.num_programs(0) - 1, 1]).astype(f32)
    state_ref[...] += tn(tail.astype(bf16), v)
    norm_ref[...] += jnp.broadcast_to(jnp.sum(tail, 0, keepdims=True), norm_ref.shape)

    @pl.when(step == pl.num_programs(0) - 1)
    def _():
        packed, norm = pack_state(state_ref[...], norm_ref[...], head_size)
        pk_ref[:head_size] = packed
        pk_ref[head_size:] = norm


def store_blocks(block, base, me, keep_at, send_at, part):
    for parity in range(2):

        @pl.when(me % 2 == parity)
        def _():
            for j in range(block.shape[0] // part):
                put = keep_at if j % 2 == parity else send_at
                put((me ^ (base + j)) // 2, block[j * part : (j + 1) * part])


def ff_kernel(pieces, me_ref, *refs):
    grad_refs = refs[:pieces]
    (
        ln2_ref,
        ln2t_ref,
        win_ref,
        bin_ref,
        wdown_ref,
        grad_ref,
        hid_ref,
        dpre_ref,
        gdown_ref,
        gin_ref,
        gb_ref,
    ) = refs[pieces:]

    @pl.when(pl.program_id(0) == 0)
    def _():
        place(grad_ref, grad_refs, me_ref)

    chunk = ln2_ref.shape[0] // 4
    sums = jnp.zeros((1, win_ref.shape[1]), f32)
    for r in range(4):
        part = slice(r * chunk, (r + 1) * chunk)
        pre = nn(ln2_ref[part], win_ref[...]) + bin_ref[...]
        phi_cum = 0.5 + 0.5 * lax.erf(pre * (1.0 / math.sqrt(2.0)))
        hid_ref[part] = (pre * phi_cum).astype(bf16)
        slope = phi_cum + pre * jnp.exp(-0.5 * pre * pre) * (1.0 / math.sqrt(2.0 * math.pi))
        dpre = nt(grad_ref[part], wdown_ref[...]) * slope
        sums = sums + jnp.sum(dpre, 0, keepdims=True)
        dpre_ref[part] = dpre.astype(bf16)
    gb_ref[...] = sums
    gdown_ref[...] = tn(hid_ref[...], grad_ref[...]).astype(bf16)
    gin_ref[...] = nn(ln2t_ref[...], dpre_ref[...]).astype(bf16)


def attn_kernel(
    head_size,
    labels_ref,
    qf_ref,
    kf_ref,
    v_ref,
    grad_ref,
    wout_ref,
    segc_ref,
    segr_ref,
    spk_ref,
    att_ref,
    dq_ref,
    dk_ref,
    dv_ref,
    gb_ref,
    gzb_ref,
    gpk_ref,
    state_ref,
    norm_ref,
    lead_ref,
    leadz_ref,
):
    step = pl.program_id(0)
    last = pl.num_programs(0) - 1
    rows, width = qf_ref.shape
    heads = width // head_size
    same = block_ones(width, head_size)
    ones = same.astype(f32).astype(bf16)

    def head_sum(x):
        hi, lo = split(x)
        return nn(hi, ones) + nn(lo, ones)

    @pl.when(step == 0)
    def _():
        state_ref[...] = unpack_state(spk_ref[...], head_size)
        norm_ref[...] = spk_ref[head_size : head_size + 8]
        lead_ref[...] = jnp.zeros_like(lead_ref)
        leadz_ref[...] = jnp.zeros_like(leadz_ref)

    seg = segc_ref[...]
    enters = (seg == labels_ref[step, 0]).astype(f32)
    tail = (seg == labels_ref[step, 1]).astype(f32)
    lead = (seg == labels_ref[0, 2]).astype(f32)
    linked = (labels_ref[step, 0] == labels_ref[step, 1]).astype(f32)
    qf = qf_ref[...]
    kf = kf_ref[...]
    v = v_ref[...]
    qf32 = qf.astype(f32)
    norm = norm_ref[0:1]
    lane = lane_head((rows, width), head_size)
    zero16 = jnp.zeros((rows, width), bf16)

    def stack(x):
        return jnp.concatenate([jnp.where(lane == h, x, zero16) for h in range(heads)], 0)

    def unstack(x):
        total = jnp.where(lane == 0, x[:rows], 0.0)
        for h in range(1, heads):
            total = jnp.where(lane == h, x[h * rows : (h + 1) * rows], total)
        return total

    causal = lax.broadcasted_iota(jnp.int32, (rows, rows), 0) >= lax.broadcasted_iota(
        jnp.int32, (rows, rows), 1
    )
    joined = causal & (seg == segr_ref[...])
    joined_all = jnp.concatenate([joined.astype(f32)] * heads, 0)
    q_stack = stack(qf)
    scores = (nt(q_stack, kf) * joined_all).astype(bf16)
    ones_v = jnp.ones((rows, LANES), bf16)
    sums = nn(scores, ones_v)
    den_in = jnp.where(lane == 0, widen(sums[:rows], width), 0.0)
    for h in range(1, heads):
        den_in = jnp.where(lane == h, widen(sums[h * rows : (h + 1) * rows], width), den_in)
    s_hi, s_lo = split(state_ref[...])
    num = unstack(nn(scores, v)) + enters * (nn(qf, s_hi) + nn(qf, s_lo))
    den = den_in + enters * head_sum(qf32 * norm)
    inv_den = 1.0 / den
    att = num * inv_den
    att_ref[...] = att.astype(bf16)
    d_att = nt(grad_ref[...], wout_ref[...])
    d_num = d_att * inv_den
    d_den = -head_sum(d_att * att) * inv_den
    dn_hi, dn_lo = split(d_num)
    dn_stack = stack(dn_hi)
    dden_all = jnp.concatenate([d_den[:, h * head_size : h * head_size + 1] for h in range(heads)], 0)
    d_scores = ((nt(dn_stack, v) + dden_all) * joined_all).astype(bf16)
    inter = nt(dn_hi, s_hi) + nt(dn_lo, s_hi) + nt(dn_hi, s_lo) + d_den * norm
    dq_ref[...] = unstack(nn(d_scores, kf)) + enters * inter
    dk_ref[...] = tn(d_scores, q_stack)
    dv_ref[...] = tn(scores, dn_stack)
    q_in = (qf32 * enters).astype(bf16)
    gb_ref[0] = jnp.where(same, tn(q_in, dn_hi) + tn(q_in, dn_lo), 0.0)
    weighted = qf32 * d_den
    gzb_ref[0] = jnp.broadcast_to(jnp.sum(weighted * enters, 0, keepdims=True), (8, width))
    q_lead = (qf32 * lead).astype(bf16)
    lead_ref[...] += tn(q_lead, dn_hi) + tn(q_lead, dn_lo)
    leadz_ref[...] += jnp.broadcast_to(jnp.sum(weighted * lead, 0, keepdims=True), (8, width))
    k_tail = kf.astype(f32) * tail
    state_ref[...] = linked * state_ref[...] + jnp.where(same, tn(k_tail.astype(bf16), v), 0.0)
    norm_ref[...] = linked * norm_ref[...] + jnp.broadcast_to(jnp.sum(k_tail, 0, keepdims=True), (8, width))

    @pl.when(step == last)
    def _():
        packed, z = pack_state(lead_ref[...], leadz_ref[...], head_size)
        gpk_ref[:head_size] = packed
        gpk_ref[head_size:] = z


def spread(full, keep_ref, send_ref, scratch_ref, me_ref):
    scratch_ref[...] = full.astype(bf16)
    size = keep_ref.shape[2]
    for k in range(2 * keep_ref.shape[0]):
        start = pl.multiple_of((me_ref[0] ^ k) * size, LANES)
        (send_ref if k % 2 else keep_ref)[k // 2] = scratch_ref[:, pl.ds(start, size)]


def tail_kernel(
    head_size,
    labels_ref,
    dq_ref,
    dk_ref,
    dv_ref,
    qe_ref,
    ke_ref,
    kf_ref,
    v_ref,
    gb_ref,
    gzb_ref,
    gin_ref,
    segc_ref,
    cos_ref,
    sin_ref,
    fw_ref,
    tab_ref,
    ln1t_ref,
    gout_ref,
    rank_ref,
    low_ref,
    small_ref,
    keep0_ref,
    send0_ref,
    keep1_ref,
    send1_ref,
    state_ref,
    norm_ref,
    all_ref,
):
    step = pl.program_id(0)
    last = pl.num_programs(0) - 1
    block = last - step
    rows, width = dq_ref.shape

    @pl.when(step == 0)
    def _():
        state_ref[...] = unpack_state(gin_ref[...], head_size)
        norm_ref[...] = gin_ref[head_size : head_size + 8]
        small_ref[...] = jnp.zeros_like(small_ref)

    tail = (segc_ref[...] == labels_ref[block, 1]).astype(f32)
    linked = (labels_ref[block, 0] == labels_ref[block, 1]).astype(f32)
    g_hi, g_lo = split(state_ref[...])
    v = v_ref[...]
    kf = kf_ref[...]
    dk = dk_ref[...] + tail * (nt(v, g_hi) + nt(v, g_lo) + norm_ref[0:1])
    dv = dv_ref[...] + tail * (nn(kf, g_hi) + nn(kf, g_lo))
    state_ref[...] = linked * state_ref[...] + gb_ref[0]
    norm_ref[...] = linked * norm_ref[...] + gzb_ref[0]
    fw = fw_ref[...]
    gq = dq_ref[...] * qe_ref[...]
    gk = dk * ke_ref[...]
    cosine = widen(cos_ref[...], width)
    sine = widen(sin_ref[...], width)

    def back(g):
        hi, lo = split(g * fw)
        turned = nt(hi, tab_ref[0]) + nt(lo, tab_ref[0]) + nt(hi, tab_ref[1])
        return turned * cosine - swap_halves(turned, head_size) * sine

    dq_raw = back(gq)
    dk_raw = back(gk)
    small_ref[0:1] += jnp.sum(dq_raw, 0, keepdims=True)
    small_ref[1:2] += jnp.sum(dk_raw, 0, keepdims=True)
    small_ref[2:3] += jnp.sum(dv, 0, keepdims=True)
    small_ref[3:4] += jnp.sum(gq + gk, 0, keepdims=True)
    start = pl.multiple_of(block * rows, rows)
    for c, d in enumerate((dq_raw, dk_raw, dv)):
        low = d.astype(bf16)
        low_ref[c] = low
        all_ref[c, pl.ds(start, rows)] = low

    @pl.when(step == last)
    def _():
        me = rank_ref[0]
        part = keep0_ref.shape[2]
        for c in range(4):
            g = gout_ref[...] if c == 3 else nn(ln1t_ref[...], all_ref[c]).astype(bf16)

            def put(ref, slot, value):
                ref[slot, c % 2] = value

            pair = (keep1_ref, send1_ref) if c >= 2 else (keep0_ref, send0_ref)
            store_blocks(g, 0, me, functools.partial(put, pair[0]), functools.partial(put, pair[1]), part)


def e_kernel(
    me_ref,
    dpre_ref,
    low_ref,
    w_ref,
    win_ref,
    xhat_ref,
    gains_ref,
    keep_ref,
    send_ref,
    stat_ref,
    scratch_ref,
):
    step = pl.program_id(0)
    rows, model = xhat_ref.shape

    @pl.when(step == 0)
    def _():
        stat_ref[8:16] = jnp.zeros((8, stat_ref.shape[1]), f32)

    d_ln1 = nt(low_ref[0], w_ref[0]) + nt(low_ref[1], w_ref[1]) + nt(low_ref[2], w_ref[2])
    d_ln2 = nt(dpre_ref[...], win_ref[...])
    xhat = xhat_ref[...].astype(f32)
    e = d_ln1 * gains_ref[0:1] + d_ln2 * gains_ref[2:3]
    spread(e, keep_ref, send_ref, scratch_ref, me_ref)
    ones = jnp.ones((8, model), bf16)
    hi, lo = split(e)
    sum_e = nt(ones, hi) + nt(ones, lo)
    hi, lo = split(e * xhat)
    sum_ex = nt(ones, hi) + nt(ones, lo)
    row = lax.broadcasted_iota(jnp.int32, sum_e.shape, 0)
    start = pl.multiple_of(step * rows, rows)
    stat_ref[0:8, pl.ds(start, rows)] = jnp.where(row == 0, sum_e, sum_ex)
    stat_ref[8:9, :model] += jnp.sum(d_ln1 * xhat, 0, keepdims=True)
    stat_ref[9:10, :model] += jnp.sum(d_ln1, 0, keepdims=True)
    stat_ref[10:11, :model] += jnp.sum(d_ln2 * xhat, 0, keepdims=True)
    stat_ref[11:12, :model] += jnp.sum(d_ln2, 0, keepdims=True)


def spread_rows(rank_ref, own_ref, other_ref, slab, write):
    half, _, part, _ = own_ref.shape
    for parity in range(2):

        @pl.when(rank_ref[0] % 2 == parity)
        def _():
            for i in range(half):
                for odd in range(2):
                    ref = own_ref if odd == parity else other_ref
                    slot = (rank_ref[0] // 2) ^ i
                    write((2 * i + odd) * part, part, ref[slot, slab].astype(f32))


def widen0_kernel(rank_ref, own_ref, other_ref, qkv_ref):
    def write(start, size, value):
        qkv_ref[0, start : start + size] = value

    spread_rows(rank_ref, own_ref, other_ref, 0, write)


def widen1_kernel(rank_ref, own_ref, other_ref, qkv_in_ref, qkv_ref, out_ref, scratch_ref):
    c = pl.program_id(0)

    def write_qkv(start, size, value):
        qkv_ref[0, start : start + size] = value

    def write_out(start, size, value):
        scratch_ref[start : start + size] = value

    @pl.when(c == 0)
    def _():
        spread_rows(rank_ref, own_ref, other_ref, 0, write_qkv)

    @pl.when(c == 1)
    def _():
        spread_rows(rank_ref, own_ref, other_ref, 0, write_out)
        out_ref[...] = scratch_ref[...].T


def whole(*shape):
    return pl.BlockSpec(shape, lambda *_: (0,) * len(shape))


def rows_of(*shape):
    return pl.BlockSpec(shape, lambda i: (i,) + (0,) * (len(shape) - 1))


def smem():
    return pl.BlockSpec(memory_space=pltpu.SMEM)


def sds(shape, dtype):
    return jax.ShapeDtypeStruct(shape, dtype)


def call(kernel, grid, in_specs, out_specs, out_shape, scratch, flops, moved, aliases={}):
    return pl.pallas_call(
        kernel,
        grid=(grid,),
        in_specs=in_specs,
        out_specs=out_specs,
        out_shape=out_shape,
        scratch_shapes=scratch,
        input_output_aliases=aliases,
        compiler_params=pltpu.CompilerParams(vmem_limit_bytes=VMEM_LIMIT),
        cost_estimate=pl.CostEstimate(
            flops=int(flops * COST_SCALE), bytes_accessed=int(moved * COST_SCALE), transcendentals=0
        ),
        name=getattr(kernel, "func", kernel).__name__,
    )


def exchange(x, axis, mask):
    count = lax.axis_size(axis)
    return lax.ppermute(x, axis, [(i, i ^ mask) for i in range(count)])


def gather_far(x, axis):
    pieces = {0: x}
    mask = lax.axis_size(axis) // 2
    while mask > 1:
        pieces.update({k ^ mask: exchange(p, axis, mask) for k, p in sorted(pieces.items())})
        mask //= 2
    return pieces


def gather_near(pieces, axis):
    pieces = pieces | {k ^ 1: exchange(p, axis, 1) for k, p in sorted(pieces.items())}
    return [pieces[k] for k in sorted(pieces)]


def scatter_sum(keep, send, axis):
    mask = 1
    while True:
        got = exchange(send, axis, mask)
        if keep.shape[0] == 1:
            return keep[0].astype(f32) + got[0].astype(f32)
        total_keep = keep[0::2].astype(f32) + got[0::2].astype(f32)
        total_send = keep[1::2].astype(f32) + got[1::2].astype(f32)
        keep, send = total_keep.astype(bf16), total_send.astype(bf16)
        mask *= 2


def sum_all(x, axis):
    mask = 1
    while mask < lax.axis_size(axis):
        x = x + exchange(x, axis, mask)
        mask *= 2
    return x


def reduce_pairs(keep, send, pin):
    got = after(exchange(send, "seq", 1), pin)
    return (keep.astype(f32) + got.astype(f32)).astype(bf16)


def reduce_groups(half, pin):
    terms = [half[0]] + [exchange(half[k], "seq", 2 * k) for k in range(1, half.shape[0])]
    terms = after(tuple(terms), pin)
    return sum(t.astype(f32) for t in terms).astype(bf16)


def gather_blocks(block):
    count = lax.axis_size("seq")
    own = jnp.stack([block] + [exchange(block, "seq", 2 * k) for k in range(1, count // 2)])
    return own, exchange(own, "seq", 1)


def sum_before(packet):
    count = lax.axis_size("seq")
    copies = jnp.broadcast_to(packet[None], (count,) + packet.shape)
    packets = lax.all_to_all(copies, "seq", 0, 0, tiled=True)
    wanted = (jnp.arange(count) < lax.axis_index("seq")).astype(f32)
    return jnp.sum(packets * wanted[:, None, None], 0)


def after(x, *others):
    return lax.optimization_barrier((x,) + others)[0]


def neighbour_sum(packet, sign, pin):
    count = lax.axis_size("seq")
    outer = 4 if count % 4 == 0 else 1
    inner = count // outer
    me = lax.axis_index("seq")
    mine = me % inner
    group = packet
    before = jnp.zeros_like(packet)
    for k in range(1, inner):
        route = [(i, i - i % inner + (i % inner + k) % inner) for i in range(count)]
        got = after(lax.ppermute(packet, "seq", route), pin)
        sender = (mine - k) % inner
        group = group + got
        before = before + jnp.where((sender < mine) if sign > 0 else (sender > mine), got, 0.0)
    for k in range(1, outer):
        shift = sign * k * inner
        route = [(i, i + shift) for i in range(count) if 0 <= i + shift < count]
        before = before + lax.ppermute(group, "seq", route)
    return before


def body(
    tokens,
    lengths,
    pad_mask,
    ln1_gain,
    ln1_bias,
    ln2_gain,
    ln2_bias,
    w_qkv,
    b_qkv,
    feat_weight,
    w_out,
    b_out,
    w_in,
    b_in,
    w_down,
    b_down,
    grad_out,
):
    rows, share = tokens.shape
    heads, feats = feat_weight.shape
    width = w_qkv.shape[2]
    head_size = width // heads
    model, hidden = w_in.shape
    blocks = rows // BT
    n_head = lax.axis_size("head")
    offset = lax.axis_index("head") * share
    with jax.named_scope("gather_tokens"):
        token_far = gather_far(tokens, "head")
    me_head = jnp.reshape(lax.axis_index("head"), (1,)).astype(jnp.int32)
    me_seq = jnp.reshape(lax.axis_index("seq"), (1,)).astype(jnp.int32)
    n_seq = lax.axis_size("seq")

    index_all = lax.axis_index("seq") * rows + jnp.arange(rows, dtype=jnp.int32)
    seq_ends = jnp.cumsum(lengths).astype(jnp.int32)
    starts = seq_ends - lengths

    def seg_of(index):
        return jnp.sum((index[:, None] >= seq_ends[None, :]).astype(jnp.int32), 1)

    segment = seg_of(index_all)
    picked = segment[:, None] == jnp.arange(lengths.shape[0])[None, :]
    position = index_all - jnp.sum(jnp.where(picked, starts[None, :], 0), 1)
    base = lax.axis_index("seq") * rows + jnp.arange(blocks, dtype=jnp.int32) * BT
    label_in = seg_of(jnp.maximum(base - 1, 0))
    label_last = seg_of(base + (BT - 1))
    label_first = jnp.broadcast_to(segment[0], (blocks,))
    labels = jnp.stack([label_in, label_last, label_first], 1)
    seg_col = segment[:, None]
    seg_row = segment[None, :]
    lane = np.arange(LANES) % head_size
    inverse = np.where(lane < ROT, rope_base ** (-2.0 * (lane % (ROT // 2)) / ROT), 0.0)
    angles = position.astype(f32)[:, None] * jnp.asarray(inverse, f32)[None, :]
    sign = np.where(lane < ROT // 2, -1.0, np.where(lane < ROT, 1.0, 0.0))
    cosine = jnp.cos(angles)
    sine = jnp.sin(angles) * jnp.asarray(sign, f32)[None, :]
    valid = pad_mask.astype(f32)[:, None]
    table = np.kron(np.eye(heads), feature_table(feats, head_size).T).astype(np.float32)
    table_hi = table.astype(bf16)
    table_lo = (table - table_hi.astype(np.float32)).astype(bf16)
    tab = jnp.asarray(np.stack([table_hi, table_lo]))
    gains = jnp.stack([ln1_gain, ln1_bias, ln2_gain, ln2_bias])
    fw = feat_weight.reshape(1, width)
    bias_out = jnp.sum(grad_out.astype(f32), 0, keepdims=True)
    with jax.named_scope("gather_grads"):
        early = (cosine, sine, gains, bias_out, labels, valid, seg_col, seg_row, fw)
        grad_far = gather_far(after(grad_out, *early), "head")
    with jax.named_scope("gather_tokens"):
        token_pieces = gather_near({k: after(p, *early) if k else p for k, p in token_far.items()}, "head")
    packet_shape = (head_size + 8, width)

    ln1t, ln2, ln2t, xhat, inv_std, q_expo, k_expo, qf, kf, v, s_own = call(
        functools.partial(pre_kernel, head_size, n_head),
        blocks,
        [
            smem(),
            smem(),
            *[rows_of(BT, share)] * n_head,
            whole(4, model),
            whole(3, model, width),
            whole(3, width),
            whole(1, width),
            whole(2, width, width),
            rows_of(BT, LANES),
            rows_of(BT, LANES),
            rows_of(BT, 1),
            rows_of(BT, 1),
        ],
        [
            pl.BlockSpec((model, BT), lambda i: (0, i)),
            rows_of(BT, model),
            pl.BlockSpec((model, BT), lambda i: (0, i)),
            rows_of(BT, model),
            rows_of(BT, 1),
            rows_of(BT, width),
            rows_of(BT, width),
            rows_of(BT, width),
            rows_of(BT, width),
            rows_of(BT, width),
            whole(*packet_shape),
        ],
        [
            sds((model, rows), bf16),
            sds((rows, model), bf16),
            sds((model, rows), bf16),
            sds((rows, model), bf16),
            sds((rows, 1), f32),
            sds((rows, width), f32),
            sds((rows, width), f32),
            sds((rows, width), bf16),
            sds((rows, width), bf16),
            sds((rows, width), bf16),
            sds(packet_shape, f32),
        ],
        [pltpu.VMEM((BT, model), bf16), pltpu.VMEM((width, width), f32), pltpu.VMEM((8, width), f32)],
        2 * rows * model * 3 * width + 16 * rows * width * width,
        rows * model * 10 + 6 * model * width,
    )(labels, me_head, *token_pieces, gains, w_qkv, b_qkv, fw, tab, cosine, sine, valid, seg_col)

    with jax.named_scope("gather_grads"):
        grad_pieces = gather_near({k: after(p, s_own) for k, p in grad_far.items()}, "head")
    with jax.named_scope("state"):
        s_in = sum_before(s_own)

    fb = 256
    full_grad, hid, dpre, g_down, g_in, gb_in = call(
        functools.partial(ff_kernel, n_head),
        hidden // fb,
        [
            smem(),
            *[whole(rows, share)] * n_head,
            whole(rows, model),
            whole(model, rows),
            pl.BlockSpec((model, fb), lambda i: (0, i)),
            pl.BlockSpec((1, fb), lambda i: (0, i)),
            pl.BlockSpec((fb, model), lambda i: (i, 0)),
        ],
        [
            whole(rows, model),
            pl.BlockSpec((rows, fb), lambda i: (0, i)),
            pl.BlockSpec((rows, fb), lambda i: (0, i)),
            pl.BlockSpec((fb, model), lambda i: (i, 0)),
            pl.BlockSpec((model, fb), lambda i: (0, i)),
            pl.BlockSpec((1, fb), lambda i: (0, i)),
        ],
        [
            sds((rows, model), bf16),
            sds((rows, hidden), bf16),
            sds((rows, hidden), bf16),
            sds((hidden, model), bf16),
            sds((model, hidden), bf16),
            sds((1, hidden), f32),
        ],
        [],
        8 * rows * model * hidden,
        6 * rows * model + 8 * model * hidden,
    )(me_head, *grad_pieces, ln2, ln2t, w_in, b_in[None, :], w_down)

    with jax.named_scope("ff_sum"):
        g_down, g_in = lax.psum((g_down, g_in), "seq")
    s_in = after(s_in, hid)

    att, dq, dk, dv, gb, gzb, g_own = call(
        functools.partial(attn_kernel, head_size),
        blocks,
        [
            smem(),
            rows_of(BT, width),
            rows_of(BT, width),
            rows_of(BT, width),
            rows_of(BT, model),
            whole(width, model),
            rows_of(BT, 1),
            pl.BlockSpec((1, BT), lambda i: (0, i)),
            whole(*packet_shape),
        ],
        [
            rows_of(BT, width),
            rows_of(BT, width),
            rows_of(BT, width),
            rows_of(BT, width),
            rows_of(1, width, width),
            rows_of(1, 8, width),
            whole(*packet_shape),
        ],
        [
            sds((rows, width), bf16),
            sds((rows, width), f32),
            sds((rows, width), f32),
            sds((rows, width), f32),
            sds((blocks, width, width), f32),
            sds((blocks, 8, width), f32),
            sds(packet_shape, f32),
        ],
        [
            pltpu.VMEM((width, width), f32),
            pltpu.VMEM((8, width), f32),
            pltpu.VMEM((width, width), f32),
            pltpu.VMEM((8, width), f32),
        ],
        24 * rows * heads * BT * width,
        rows * model * 2 + rows * width * 20,
    )(labels, qf, kf, v, full_grad, w_out, seg_col, seg_row, s_in)

    with jax.named_scope("grad_state"):
        grad_in = neighbour_sum(g_own, -1, hid)

    value = jnp.dot(hid, w_down, preferred_element_type=f32) + jnp.dot(att, w_out, preferred_element_type=f32)
    value = value.astype(bf16)
    me = lax.axis_index("head")
    order = [lax.dynamic_slice_in_dim(value, (me ^ k) * share, share, 1) for k in range(n_head)]
    val_keep, val_send = jnp.stack(order[0::2]), jnp.stack(order[1::2])
    g_out = lax.dot_general(full_grad, att, (((0,), (0,)), ((), ())), preferred_element_type=f32).astype(bf16)
    grad_in = after(grad_in, g_out, value)


    def back_rows(*shape):
        return pl.BlockSpec(shape, lambda i: (blocks - 1 - i,) + (0,) * (len(shape) - 1))

    part = model // n_seq
    low, small, *w_parts = call(
        functools.partial(tail_kernel, head_size),
        blocks,
        [
            smem(),
            *[back_rows(BT, width)] * 7,
            back_rows(1, width, width),
            back_rows(1, 8, width),
            whole(*packet_shape),
            back_rows(BT, 1),
            back_rows(BT, LANES),
            back_rows(BT, LANES),
            whole(1, width),
            whole(2, width, width),
            whole(model, rows),
            whole(model, width),
            smem(),
        ],
        [
            pl.BlockSpec((3, BT, width), lambda i: (0, blocks - 1 - i, 0)),
            whole(8, width),
            *[whole(n_seq // 2, 2, part, width)] * 4,
        ],
        [
            sds((3, rows, width), bf16),
            sds((8, width), f32),
            *[sds((n_seq // 2, 2, part, width), bf16)] * 4,
        ],
        [
            pltpu.VMEM((width, width), f32),
            pltpu.VMEM((8, width), f32),
            pltpu.VMEM((3, rows, width), bf16),
        ],
        2 * rows * model * 3 * width,
        rows * width * 30 + rows * model * 2 + 6 * model * width,
    )(labels, dq, dk, dv, q_expo, k_expo, kf, v, gb, gzb, grad_in, seg_col, cosine, sine, fw, tab, ln1t, g_out, me_seq)

    stat_width = max(rows, model)
    e_keep, e_send, stats = call(
        e_kernel,
        blocks,
        [
            smem(),
            rows_of(BT, hidden),
            pl.BlockSpec((3, BT, width), lambda i: (0, i, 0)),
            whole(3, model, width),
            whole(model, hidden),
            rows_of(BT, model),
            whole(4, model),
        ],
        [
            pl.BlockSpec((n_head // 2, BT, share), lambda i: (0, i, 0)),
            pl.BlockSpec((n_head // 2, BT, share), lambda i: (0, i, 0)),
            whole(16, stat_width),
        ],
        [
            sds((n_head // 2, rows, share), bf16),
            sds((n_head // 2, rows, share), bf16),
            sds((16, stat_width), f32),
        ],
        [pltpu.VMEM((BT, model), bf16)],
        2 * rows * model * (3 * width + hidden),
        rows * width * 6 + rows * model * 6 + 8 * model * width + 2 * hidden * model,
    )(me_head, dpre, low, w_qkv, w_in, xhat, gains)

    with jax.named_scope("reduce_qk"):
        first = reduce_pairs(*w_parts[:2], low)
    with jax.named_scope("reduce_vo"):
        second = reduce_pairs(*w_parts[2:], low)
    with jax.named_scope("reduce_qk"):
        first = gather_blocks(reduce_groups(first, low))
    with jax.named_scope("reduce_vo"):
        second = gather_blocks(reduce_groups(second, low))
    g_down = g_down.astype(f32)
    g_in = g_in.astype(f32)

    def slab():
        return pl.BlockSpec((n_seq // 2, 1, part, width), lambda c: (0, c, 0, 0))

    g_qkv = call(
        widen0_kernel,
        2,
        [smem(), slab(), slab()],
        pl.BlockSpec((1, model, width), lambda c: (c, 0, 0)),
        sds((3, model, width), f32),
        [],
        0,
        END_COST * model * width,
    )(me_seq, *first)
    g_qkv, g_out = call(
        widen1_kernel,
        2,
        [smem(), slab(), slab(), pl.BlockSpec(memory_space=pl.ANY)],
        [pl.BlockSpec((1, model, width), lambda c: (2, 0, 0)), whole(width, model)],
        [sds((3, model, width), f32), sds((width, model), f32)],
        [pltpu.VMEM((model, width), f32)],
        0,
        END_COST * model * width,
        {3: 0},
    )(me_seq, *second, g_qkv)

    with jax.named_scope("mixed_sum"):
        mixed_share = scatter_sum(val_keep, after(val_send, low), "head")
    with jax.named_scope("e_sum"):
        e_share = scatter_sum(e_keep, e_send, "head")
    with jax.named_scope("stats_sum"):
        gains_own = stats[8:12, :model]
        stats = sum_all(stats[:8], "head")
    with jax.named_scope("small_sum"):
        local = jnp.concatenate([small[:4], gb_in.reshape(-1, share), bias_out], 0)
        mine = (jnp.arange(n_head) == lax.axis_index("head")).astype(f32)
        spread_gains = gains_own.reshape(4, n_head, share).transpose(1, 0, 2)
        packet = jnp.concatenate([spread_gains, mine[:, None, None] * local[None]], 1)
        packet = jnp.broadcast_to(packet[None], (n_seq,) + packet.shape).reshape((-1,) + packet.shape[1:])
        packet = jnp.sum(lax.all_to_all(packet, ("seq", "head"), 0, 0, tiled=True), 0)
    gain_share, small, gb_in, bias_out = packet[:4], packet[4:8], packet[8:-1].reshape(-1), packet[-1]
    stats = stats[:2, :rows].T * (1.0 / model)

    bias = lax.dynamic_slice_in_dim(b_out, offset, share) + lax.dynamic_slice_in_dim(b_down, offset, share)
    mixed = (tokens.astype(f32) + mixed_share + bias).astype(bf16)
    xhat_share = lax.dynamic_slice_in_dim(xhat, offset, share, 1).astype(f32)
    grad_input = grad_out.astype(f32) + inv_std * (
        e_share - stats[:, 0:1] - xhat_share * stats[:, 1:2]
    )
    return (
        mixed,
        grad_input,
        gain_share[0],
        gain_share[1],
        gain_share[2],
        gain_share[3],
        g_qkv,
        small[:3],
        small[3].reshape(heads, feats),
        g_out,
        bias_out,
        g_in,
        gb_in,
        g_down,
        bias_out,
    )


def solution(mesh):
    in_specs = (
        P("seq", "head"),
        P(),
        P("seq"),
        P(),
        P(),
        P(),
        P(),
        P(None, None, "head"),
        P(None, "head"),
        P("head", None),
        P("head", None),
        P(),
        P(None, "head"),
        P("head"),
        P("head", None),
        P(),
        P("seq", "head"),
    )
    out_specs = (
        P("seq", "head"),
        P("seq", "head"),
        P("head"),
        P("head"),
        P("head"),
        P("head"),
        P(None, None, "head"),
        P(None, "head"),
        P("head", None),
        P("head", None),
        P("head"),
        P(None, "head"),
        P("head"),
        P("head", None),
        P("head"),
    )
    return jax.shard_map(body, mesh=mesh, in_specs=in_specs, out_specs=out_specs, check_vma=False)
```

```python
import functools
import math
from statistics import NormalDist

import jax
import jax.numpy as jnp
import numpy as np
from jax import lax
from jax.experimental import pallas as pl
from jax.experimental.pallas import tpu as pltpu
from jax.sharding import PartitionSpec as P

ROT = 16
eps_norm = 1e-05
rope_base = 10000.0
feature_scale = 0.5
BT = 256
LANES = 128
bf16 = jnp.bfloat16
f32 = jnp.float32
COST_SCALE = 0.02
END_COST = 12
BEFORE = "DI"
AFTER = "DCIICDCIC"
PINNED = "C"
LATE = 3
VMEM_LIMIT = 56 * 1024 * 1024


def nn(a, b):
    return lax.dot_general(a, b, (((1,), (0,)), ((), ())), preferred_element_type=f32)


def nt(a, b):
    return lax.dot_general(a, b, (((1,), (1,)), ((), ())), preferred_element_type=f32)


def tn(a, b):
    return lax.dot_general(a, b, (((0,), (0,)), ((), ())), preferred_element_type=f32)


def split(x):
    hi = x.astype(bf16)
    return hi, (x - hi.astype(f32)).astype(bf16)


def feature_table(feat_count, head_size):
    rows = np.arange(feat_count)
    cols = np.arange(head_size)
    cosines = np.cos(math.pi * (cols[None, :] + 0.5) * rows[:, None] / head_size)
    scaling = np.where(rows == 0, math.sqrt(1.0 / head_size), math.sqrt(2.0 / head_size))
    points = np.array([NormalDist().inv_cdf((r + 0.5) / feat_count) for r in range(feat_count)])
    return feature_scale * (points * scaling)[:, None] * cosines


def lane_head(shape, head_size):
    return lax.broadcasted_iota(jnp.int32, shape, len(shape) - 1) // head_size


def block_ones(size, head_size):
    rows = lax.broadcasted_iota(jnp.int32, (size, size), 0) // head_size
    cols = lax.broadcasted_iota(jnp.int32, (size, size), 1) // head_size
    return rows == cols


def swap_halves(x, head_size):
    width = x.shape[1]
    lane = lax.broadcasted_iota(jnp.int32, x.shape, 1) % head_size
    ahead = pltpu.roll(x, width - ROT // 2, 1)
    behind = pltpu.roll(x, ROT // 2, 1)
    return jnp.where(lane < ROT // 2, ahead, behind)


def widen(table, width):
    return table if table.shape[1] == width else jnp.concatenate([table] * (width // table.shape[1]), 1)


def pack_state(state, norm, head_size):
    size = state.shape[0]
    masked = jnp.where(block_ones(size, head_size), state, 0.0)
    packed = masked[:head_size]
    for h in range(1, size // head_size):
        packed = packed + masked[h * head_size : (h + 1) * head_size]
    return packed, norm


def unpack_state(packed, head_size):
    size = packed.shape[1]
    rows = jnp.concatenate([packed[:head_size]] * (size // head_size), 0)
    return jnp.where(block_ones(size, head_size), rows, 0.0)


def place(full_ref, piece_refs, me_ref):
    for k, ref in enumerate(piece_refs):
        size = ref.shape[1]
        start = pl.multiple_of((me_ref[0] ^ k) * size, LANES)
        full_ref[:, pl.ds(start, size)] = ref[...]


def pre_kernel(
    head_size,
    pieces,
    labels_ref,
    me_ref,
    *refs,
):
    x_refs = refs[:pieces]
    (
        gains_ref,
        w_ref,
        bq_ref,
        fw_ref,
        tab_ref,
        cos_ref,
        sin_ref,
        valid_ref,
        seg_ref,
        ln1t_ref,
        ln2_ref,
        ln2t_ref,
        xhat_ref,
        inv_ref,
        qe_ref,
        ke_ref,
        qf_ref,
        kf_ref,
        v_ref,
        pk_ref,
        full_ref,
        state_ref,
        norm_ref,
    ) = refs[pieces:]
    step = pl.program_id(0)
    width = qe_ref.shape[1]
    place(full_ref, x_refs, me_ref)
    x = full_ref[...].astype(f32)
    centered = x - jnp.mean(x, -1, keepdims=True)
    inv = lax.rsqrt(jnp.mean(centered * centered, -1, keepdims=True) + eps_norm)
    xhat = centered * inv
    inv_ref[...] = inv
    xhat_ref[...] = xhat.astype(bf16)
    ln1 = (xhat * gains_ref[0:1] + gains_ref[1:2]).astype(bf16)
    ln2 = (xhat * gains_ref[2:3] + gains_ref[3:4]).astype(bf16)
    ln2_ref[...] = ln2
    ln1t_ref[...] = ln1.T
    ln2t_ref[...] = ln2.T
    cosine = widen(cos_ref[...], width)
    sine = widen(sin_ref[...], width)

    def features(c):
        raw = nn(ln1, w_ref[c]) + bq_ref[c : c + 1]
        turned = raw * cosine + swap_halves(raw, head_size) * sine
        hi, lo = split(turned)
        return jnp.exp(nn(hi, tab_ref[0]) + nn(lo, tab_ref[0]) + nn(hi, tab_ref[1]))

    fw = fw_ref[...]
    qe = features(0)
    ke = features(1) * valid_ref[...]
    qe_ref[...] = qe
    ke_ref[...] = ke
    qf_ref[...] = (fw * qe).astype(bf16)
    kf = (fw * ke).astype(bf16)
    kf_ref[...] = kf
    v = (nn(ln1, w_ref[2]) + bq_ref[2:3]).astype(bf16)
    v_ref[...] = v

    @pl.when(step == 0)
    def _():
        state_ref[...] = jnp.zeros_like(state_ref)
        norm_ref[...] = jnp.zeros_like(norm_ref)

    tail = kf.astype(f32) * (seg_ref[...] == labels_ref[pl.num_programs(0) - 1, 1]).astype(f32)
    state_ref[...] += tn(tail.astype(bf16), v)
    norm_ref[...] += jnp.broadcast_to(jnp.sum(tail, 0, keepdims=True), norm_ref.shape)

    @pl.when(step == pl.num_programs(0) - 1)
    def _():
        packed, norm = pack_state(state_ref[...], norm_ref[...], head_size)
        pk_ref[:head_size] = packed
        pk_ref[head_size:] = norm


def slot_of(relative, count):
    place = 0
    mask = 4
    while mask < count:
        place = 2 * place + (relative // mask) % 2
        mask *= 2
    return place


def store_blocks(block, base, me, refs, part, rest=()):
    count = 4 * refs[0].shape[0]
    for low in range(4):

        @pl.when(me % 4 == low)
        def _():
            for j in range(block.shape[0] // part):
                ref = refs[(low ^ (base + j)) % 4]
                ref[(slot_of(me ^ (base + j), count),) + rest] = block[j * part : (j + 1) * part]


def ff_kernel(pieces, me_ref, rank_ref, *refs):
    grad_refs = refs[:pieces]
    (
        ln2_ref,
        ln2t_ref,
        win_ref,
        bin_ref,
        wdown_ref,
        grad_ref,
        hid_ref,
        dpre_ref,
        *sum_refs,
        gb_ref,
    ) = refs[pieces:]

    @pl.when(pl.program_id(0) == 0)
    def _():
        place(grad_ref, grad_refs, me_ref)

    chunk = ln2_ref.shape[0] // 4
    sums = jnp.zeros((1, win_ref.shape[1]), f32)
    for r in range(4):
        part = slice(r * chunk, (r + 1) * chunk)
        pre = nn(ln2_ref[part], win_ref[...]) + bin_ref[...]
        phi_cum = 0.5 + 0.5 * lax.erf(pre * (1.0 / math.sqrt(2.0)))
        hid_ref[part] = (pre * phi_cum).astype(bf16)
        slope = phi_cum + pre * jnp.exp(-0.5 * pre * pre) * (1.0 / math.sqrt(2.0 * math.pi))
        dpre = nt(grad_ref[part], wdown_ref[...]) * slope
        sums = sums + jnp.sum(dpre, 0, keepdims=True)
        dpre_ref[part] = dpre.astype(bf16)
    gb_ref[...] = sums
    me = rank_ref[0]
    g_down = tn(hid_ref[...], grad_ref[...]).astype(bf16)
    part = sum_refs[0].shape[1]
    steps = 4 * sum_refs[0].shape[0] * part // g_down.shape[0]
    for step in range(steps):

        @pl.when(pl.program_id(0) == step)
        def _():
            store_blocks(g_down, step * (g_down.shape[0] // part), me, sum_refs[:4], part)

    g_in = nn(ln2t_ref[...], dpre_ref[...]).astype(bf16)
    store_blocks(g_in, 0, me, sum_refs[4:], sum_refs[4].shape[1])


def block_out_kernel(rank_ref, *refs):
    out_ref = refs[4]
    part = refs[0].shape[1]
    for low in range(4):

        @pl.when(rank_ref[0] % 4 == low)
        def _():
            for j in range(4):
                out_ref[j * part : (j + 1) * part] = refs[low ^ j][0].astype(f32)


def attn_kernel(
    head_size,
    labels_ref,
    qf_ref,
    kf_ref,
    v_ref,
    grad_ref,
    wout_ref,
    segc_ref,
    segr_ref,
    spk_ref,
    att_ref,
    dq_ref,
    dk_ref,
    dv_ref,
    gb_ref,
    gzb_ref,
    gpk_ref,
    gout_ref,
    state_ref,
    norm_ref,
    lead_ref,
    leadz_ref,
    acc_ref,
):
    step = pl.program_id(0)
    last = pl.num_programs(0) - 1
    rows, width = qf_ref.shape
    heads = width // head_size
    same = block_ones(width, head_size)
    ones = same.astype(f32).astype(bf16)

    def head_sum(x):
        hi, lo = split(x)
        return nn(hi, ones) + nn(lo, ones)

    @pl.when(step == 0)
    def _():
        state_ref[...] = unpack_state(spk_ref[...], head_size)
        norm_ref[...] = spk_ref[head_size : head_size + 8]
        lead_ref[...] = jnp.zeros_like(lead_ref)
        leadz_ref[...] = jnp.zeros_like(leadz_ref)
        acc_ref[...] = jnp.zeros_like(acc_ref)

    seg = segc_ref[...]
    enters = (seg == labels_ref[step, 0]).astype(f32)
    tail = (seg == labels_ref[step, 1]).astype(f32)
    lead = (seg == labels_ref[0, 2]).astype(f32)
    linked = (labels_ref[step, 0] == labels_ref[step, 1]).astype(f32)
    qf = qf_ref[...]
    kf = kf_ref[...]
    v = v_ref[...]
    qf32 = qf.astype(f32)
    norm = norm_ref[0:1]
    lane = lane_head((rows, width), head_size)
    zero16 = jnp.zeros((rows, width), bf16)

    def stack(x):
        return jnp.concatenate([jnp.where(lane == h, x, zero16) for h in range(heads)], 0)

    def unstack(x):
        total = jnp.where(lane == 0, x[:rows], 0.0)
        for h in range(1, heads):
            total = jnp.where(lane == h, x[h * rows : (h + 1) * rows], total)
        return total

    causal = lax.broadcasted_iota(jnp.int32, (rows, rows), 0) >= lax.broadcasted_iota(
        jnp.int32, (rows, rows), 1
    )
    joined = causal & (seg == segr_ref[...])
    joined_all = jnp.concatenate([joined.astype(f32)] * heads, 0)
    q_stack = stack(qf)
    scores = (nt(q_stack, kf) * joined_all).astype(bf16)
    ones_v = jnp.ones((rows, LANES), bf16)
    sums = nn(scores, ones_v)
    den_in = jnp.where(lane == 0, widen(sums[:rows], width), 0.0)
    for h in range(1, heads):
        den_in = jnp.where(lane == h, widen(sums[h * rows : (h + 1) * rows], width), den_in)
    s_hi, s_lo = split(state_ref[...])
    num = unstack(nn(scores, v)) + enters * (nn(qf, s_hi) + nn(qf, s_lo))
    den = den_in + enters * head_sum(qf32 * norm)
    inv_den = 1.0 / den
    att = num * inv_den
    att_low = att.astype(bf16)
    att_ref[...] = att_low
    acc_ref[...] += tn(att_low, grad_ref[...])
    d_att = nt(grad_ref[...], wout_ref[...])
    d_num = d_att * inv_den
    d_den = -head_sum(d_att * att) * inv_den
    dn_hi, dn_lo = split(d_num)
    dn_stack = stack(dn_hi)
    dden_all = jnp.concatenate([d_den[:, h * head_size : h * head_size + 1] for h in range(heads)], 0)
    d_scores = ((nt(dn_stack, v) + dden_all) * joined_all).astype(bf16)
    inter = nt(dn_hi, s_hi) + nt(dn_lo, s_hi) + nt(dn_hi, s_lo) + d_den * norm
    dq_ref[...] = unstack(nn(d_scores, kf)) + enters * inter
    dk_ref[...] = tn(d_scores, q_stack)
    dv_ref[...] = tn(scores, dn_stack)
    q_in = (qf32 * enters).astype(bf16)
    gb_ref[0] = jnp.where(same, tn(q_in, dn_hi) + tn(q_in, dn_lo), 0.0)
    weighted = qf32 * d_den
    gzb_ref[0] = jnp.broadcast_to(jnp.sum(weighted * enters, 0, keepdims=True), (8, width))
    q_lead = (qf32 * lead).astype(bf16)
    lead_ref[...] += tn(q_lead, dn_hi) + tn(q_lead, dn_lo)
    leadz_ref[...] += jnp.broadcast_to(jnp.sum(weighted * lead, 0, keepdims=True), (8, width))
    k_tail = kf.astype(f32) * tail
    state_ref[...] = linked * state_ref[...] + jnp.where(same, tn(k_tail.astype(bf16), v), 0.0)
    norm_ref[...] = linked * norm_ref[...] + jnp.broadcast_to(jnp.sum(k_tail, 0, keepdims=True), (8, width))

    @pl.when(step == last)
    def _():
        packed, z = pack_state(lead_ref[...], leadz_ref[...], head_size)
        gpk_ref[:head_size] = packed
        gpk_ref[head_size:] = z
        gout_ref[...] = acc_ref[...].T.astype(bf16)


def spread(full, keep_ref, send_ref, scratch_ref, me_ref):
    scratch_ref[...] = full.astype(bf16)
    size = keep_ref.shape[2]
    for k in range(2 * keep_ref.shape[0]):
        start = pl.multiple_of((me_ref[0] ^ k) * size, LANES)
        (send_ref if k % 2 else keep_ref)[k // 2] = scratch_ref[:, pl.ds(start, size)]


def tail_kernel(
    head_size,
    labels_ref,
    dq_ref,
    dk_ref,
    dv_ref,
    qe_ref,
    ke_ref,
    kf_ref,
    v_ref,
    gb_ref,
    gzb_ref,
    gin_ref,
    segc_ref,
    cos_ref,
    sin_ref,
    fw_ref,
    tab_ref,
    ln1t_ref,
    gout_ref,
    rank_ref,
    low_ref,
    small_ref,
    sum0_ref,
    sum1_ref,
    sum2_ref,
    sum3_ref,
    state_ref,
    norm_ref,
    all_ref,
):
    step = pl.program_id(0)
    last = pl.num_programs(0) - 1
    block = last - step
    rows, width = dq_ref.shape

    @pl.when(step == 0)
    def _():
        state_ref[...] = unpack_state(gin_ref[...], head_size)
        norm_ref[...] = gin_ref[head_size : head_size + 8]
        small_ref[...] = jnp.zeros_like(small_ref)

    tail = (segc_ref[...] == labels_ref[block, 1]).astype(f32)
    linked = (labels_ref[block, 0] == labels_ref[block, 1]).astype(f32)
    g_hi, g_lo = split(state_ref[...])
    v = v_ref[...]
    kf = kf_ref[...]
    dk = dk_ref[...] + tail * (nt(v, g_hi) + nt(v, g_lo) + norm_ref[0:1])
    dv = dv_ref[...] + tail * (nn(kf, g_hi) + nn(kf, g_lo))
    state_ref[...] = linked * state_ref[...] + gb_ref[0]
    norm_ref[...] = linked * norm_ref[...] + gzb_ref[0]
    fw = fw_ref[...]
    gq = dq_ref[...] * qe_ref[...]
    gk = dk * ke_ref[...]
    cosine = widen(cos_ref[...], width)
    sine = widen(sin_ref[...], width)

    def back(g):
        hi, lo = split(g * fw)
        turned = nt(hi, tab_ref[0]) + nt(lo, tab_ref[0]) + nt(hi, tab_ref[1])
        return turned * cosine - swap_halves(turned, head_size) * sine

    dq_raw = back(gq)
    dk_raw = back(gk)
    small_ref[0:1] += jnp.sum(dq_raw, 0, keepdims=True)
    small_ref[1:2] += jnp.sum(dk_raw, 0, keepdims=True)
    small_ref[2:3] += jnp.sum(dv, 0, keepdims=True)
    small_ref[3:4] += jnp.sum(gq + gk, 0, keepdims=True)
    start = pl.multiple_of(block * rows, rows)
    for c, d in enumerate((dq_raw, dk_raw, dv)):
        low = d.astype(bf16)
        low_ref[c] = low
        all_ref[c, pl.ds(start, rows)] = low

    @pl.when(step == last)
    def _():
        me = rank_ref[0]
        part = sum0_ref.shape[2]
        for c in range(4):
            g = gout_ref[...] if c == 3 else nn(ln1t_ref[...], all_ref[c]).astype(bf16)

            store_blocks(g, 0, me, (sum0_ref, sum1_ref, sum2_ref, sum3_ref), part, (c,))


def finish_kernel(
    me_ref,
    hid_ref,
    wdown_ref,
    att_ref,
    wout_ref,
    dpre_ref,
    low_ref,
    w_ref,
    win_ref,
    xhat_ref,
    gains_ref,
    val_keep_ref,
    val_send_ref,
    keep_ref,
    send_ref,
    stat_ref,
    scratch_ref,
):
    value = nn(hid_ref[...], wdown_ref[...]) + nn(att_ref[...], wout_ref[...])
    spread(value, val_keep_ref, val_send_ref, scratch_ref, me_ref)
    step = pl.program_id(0)
    rows, model = xhat_ref.shape

    @pl.when(step == 0)
    def _():
        stat_ref[8:16] = jnp.zeros((8, stat_ref.shape[1]), f32)

    d_ln1 = nt(low_ref[0], w_ref[0]) + nt(low_ref[1], w_ref[1]) + nt(low_ref[2], w_ref[2])
    d_ln2 = nt(dpre_ref[...], win_ref[...])
    xhat = xhat_ref[...].astype(f32)
    e = d_ln1 * gains_ref[0:1] + d_ln2 * gains_ref[2:3]
    spread(e, keep_ref, send_ref, scratch_ref, me_ref)
    ones = jnp.ones((8, model), bf16)
    hi, lo = split(e)
    sum_e = nt(ones, hi) + nt(ones, lo)
    hi, lo = split(e * xhat)
    sum_ex = nt(ones, hi) + nt(ones, lo)
    row = lax.broadcasted_iota(jnp.int32, sum_e.shape, 0)
    start = pl.multiple_of(step * rows, rows)
    stat_ref[0:8, pl.ds(start, rows)] = jnp.where(row == 0, sum_e, sum_ex)
    stat_ref[8:9, :model] += jnp.sum(d_ln1 * xhat, 0, keepdims=True)
    stat_ref[9:10, :model] += jnp.sum(d_ln1, 0, keepdims=True)
    stat_ref[10:11, :model] += jnp.sum(d_ln2 * xhat, 0, keepdims=True)
    stat_ref[11:12, :model] += jnp.sum(d_ln2, 0, keepdims=True)


def widen_kernel(rank_ref, *refs):
    qkv_ref, out_ref, scratch_ref = refs[4:]
    c = pl.program_id(0)
    quarter, _, part, _ = refs[0].shape
    me = rank_ref[0]
    for low in range(4):

        @pl.when(me % 4 == low)
        def _():
            for j in range(4 * quarter):
                slot = slot_of(me ^ j, 4 * quarter)
                scratch_ref[j * part : (j + 1) * part] = refs[(low ^ j) % 4][slot, 0].astype(f32)

    @pl.when(c < 3)
    def _():
        qkv_ref[0] = scratch_ref[...]

    @pl.when(c == 3)
    def _():
        out_ref[...] = scratch_ref[...].T


def whole(*shape):
    return pl.BlockSpec(shape, lambda *_: (0,) * len(shape))


def rows_of(*shape):
    return pl.BlockSpec(shape, lambda i: (i,) + (0,) * (len(shape) - 1))


def smem():
    return pl.BlockSpec(memory_space=pltpu.SMEM)


def sds(shape, dtype):
    return jax.ShapeDtypeStruct(shape, dtype)


def call(kernel, grid, in_specs, out_specs, out_shape, scratch, flops, moved, aliases={}):
    return pl.pallas_call(
        kernel,
        grid=(grid,),
        in_specs=in_specs,
        out_specs=out_specs,
        out_shape=out_shape,
        scratch_shapes=scratch,
        input_output_aliases=aliases,
        compiler_params=pltpu.CompilerParams(vmem_limit_bytes=VMEM_LIMIT),
        cost_estimate=pl.CostEstimate(
            flops=int(flops * COST_SCALE), bytes_accessed=int(moved * COST_SCALE), transcendentals=0
        ),
        name=getattr(kernel, "func", kernel).__name__,
    )


def exchange(x, axis, mask):
    count = lax.axis_size(axis)
    return lax.ppermute(x, axis, [(i, i ^ mask) for i in range(count)])


def gather_far(x, axis):
    pieces = {0: x}
    mask = lax.axis_size(axis) // 2
    while mask > 1:
        pieces.update({k ^ mask: exchange(p, axis, mask) for k, p in sorted(pieces.items())})
        mask //= 2
    return pieces


def gather_near(pieces, axis):
    pieces = pieces | {k ^ 1: exchange(p, axis, 1) for k, p in sorted(pieces.items())}
    return [pieces[k] for k in sorted(pieces)]


def scatter_sum(keep, send, axis):
    mask = 1
    while True:
        got = exchange(send, axis, mask)
        if keep.shape[0] == 1:
            return keep[0].astype(f32) + got[0].astype(f32)
        total_keep = keep[0::2].astype(f32) + got[0::2].astype(f32)
        total_send = keep[1::2].astype(f32) + got[1::2].astype(f32)
        keep, send = total_keep.astype(bf16), total_send.astype(bf16)
        mask *= 2


def sum_all(x, axis):
    mask = 1
    while mask < lax.axis_size(axis):
        x = x + exchange(x, axis, mask)
        mask *= 2
    return x


class Sum:
    def __init__(self, name, arrays):
        self.name, self.arrays = name, list(arrays)
        masks = []
        while 4 * 2 ** len(masks) < lax.axis_size("seq"):
            masks.append(4 * 2 ** len(masks))
        self.plan = [("group", 0)] + [("reduce", m) for m in masks]
        self.plan += [("gather", m) for m in masks[::-1]] + [("spread", 0)]

    def halves(self, terms):
        half = terms[0].shape[0] // 2

        def total(part):
            return sum(t[part].astype(f32) for t in terms).astype(bf16)

        if half:
            self.keep, self.send = total(slice(0, half)), total(slice(half, None))
        else:
            self.keep = self.send = total(slice(None))
        return self.send

    def step(self, *pins):
        kind, mask = self.plan.pop(0)
        with jax.named_scope(self.name):
            if kind == "group":
                got = after(tuple(exchange(self.arrays[g], "seq", g) for g in (1, 2, 3)), *pins)
                return self.halves([self.arrays[0], *got])
            if kind == "reduce":
                return self.halves([self.keep, after(exchange(self.send, "seq", mask), *pins)])
            if kind == "gather":
                self.keep = jnp.concatenate([self.keep, after(exchange(self.keep, "seq", mask), *pins)])
                return self.keep
            self.arrays = [self.keep, *after(tuple(exchange(self.keep, "seq", g) for g in (1, 2, 3)), *pins)]
            return self.arrays[1]


def block_out(chunk, me_seq):
    quarter, part, width = chunk.keep.shape
    block = pl.BlockSpec((1, part, width), lambda i, me: (slot_of(((me[0] // 4) ^ i) * 4, 4 * quarter), 0, 0))
    return pl.pallas_call(
        block_out_kernel,
        grid_spec=pltpu.PrefetchScalarGridSpec(
            num_scalar_prefetch=1,
            grid=(quarter,),
            in_specs=[block] * 4,
            out_specs=pl.BlockSpec((4 * part, width), lambda i, me: (i, 0)),
        ),
        out_shape=sds((4 * quarter * part, width), f32),
        compiler_params=pltpu.CompilerParams(vmem_limit_bytes=VMEM_LIMIT),
        cost_estimate=pl.CostEstimate(flops=0, bytes_accessed=24 * quarter * part * width, transcendentals=0),
        name="block_out_kernel",
    )(me_seq, *chunk.arrays)


def sum_before(packet):
    count = lax.axis_size("seq")
    copies = jnp.broadcast_to(packet[None], (count,) + packet.shape)
    packets = lax.all_to_all(copies, "seq", 0, 0, tiled=True)
    wanted = (jnp.arange(count) < lax.axis_index("seq")).astype(f32)
    return jnp.sum(packets * wanted[:, None, None], 0)


def after(x, *others):
    return lax.optimization_barrier((x,) + others)[0]


def neighbour_sum(packet, sign, pin, event):
    count = lax.axis_size("seq")
    outer = 4 if count % 4 == 0 else 1
    inner = count // outer
    me = lax.axis_index("seq")
    mine = me % inner
    group = packet
    before = jnp.zeros_like(packet)
    for k in range(1, inner):
        route = [(i, i - i % inner + (i % inner + k) % inner) for i in range(count)]
        got = after(lax.ppermute(packet, "seq", route), pin)
        event(got)
        sender = (mine - k) % inner
        group = group + got
        before = before + jnp.where((sender < mine) if sign > 0 else (sender > mine), got, 0.0)
    for k in range(1, outer):
        shift = sign * k * inner
        route = [(i, i + shift) for i in range(count) if 0 <= i + shift < count]
        before = before + lax.ppermute(group, "seq", route)
    return before


def body(
    tokens,
    lengths,
    pad_mask,
    ln1_gain,
    ln1_bias,
    ln2_gain,
    ln2_bias,
    w_qkv,
    b_qkv,
    feat_weight,
    w_out,
    b_out,
    w_in,
    b_in,
    w_down,
    b_down,
    grad_out,
):
    rows, share = tokens.shape
    heads, feats = feat_weight.shape
    width = w_qkv.shape[2]
    head_size = width // heads
    model, hidden = w_in.shape
    blocks = rows // BT
    n_head = lax.axis_size("head")
    offset = lax.axis_index("head") * share
    with jax.named_scope("gather_tokens"):
        token_far = gather_far(tokens, "head")
    me_head = jnp.reshape(lax.axis_index("head"), (1,)).astype(jnp.int32)
    me_seq = jnp.reshape(lax.axis_index("seq"), (1,)).astype(jnp.int32)
    n_seq = lax.axis_size("seq")

    index_all = lax.axis_index("seq") * rows + jnp.arange(rows, dtype=jnp.int32)
    seq_ends = jnp.cumsum(lengths).astype(jnp.int32)
    starts = seq_ends - lengths

    def seg_of(index):
        return jnp.sum((index[:, None] >= seq_ends[None, :]).astype(jnp.int32), 1)

    segment = seg_of(index_all)
    picked = segment[:, None] == jnp.arange(lengths.shape[0])[None, :]
    position = index_all - jnp.sum(jnp.where(picked, starts[None, :], 0), 1)
    base = lax.axis_index("seq") * rows + jnp.arange(blocks, dtype=jnp.int32) * BT
    label_in = seg_of(jnp.maximum(base - 1, 0))
    label_last = seg_of(base + (BT - 1))
    label_first = jnp.broadcast_to(segment[0], (blocks,))
    labels = jnp.stack([label_in, label_last, label_first], 1)
    seg_col = segment[:, None]
    seg_row = segment[None, :]
    lane = np.arange(LANES) % head_size
    inverse = np.where(lane < ROT, rope_base ** (-2.0 * (lane % (ROT // 2)) / ROT), 0.0)
    angles = position.astype(f32)[:, None] * jnp.asarray(inverse, f32)[None, :]
    sign = np.where(lane < ROT // 2, -1.0, np.where(lane < ROT, 1.0, 0.0))
    cosine = jnp.cos(angles)
    sine = jnp.sin(angles) * jnp.asarray(sign, f32)[None, :]
    valid = pad_mask.astype(f32)[:, None]
    table = np.kron(np.eye(heads), feature_table(feats, head_size).T).astype(np.float32)
    table_hi = table.astype(bf16)
    table_lo = (table - table_hi.astype(np.float32)).astype(bf16)
    tab = jnp.asarray(np.stack([table_hi, table_lo]))
    gains = jnp.stack([ln1_gain, ln1_bias, ln2_gain, ln2_bias])
    fw = feat_weight.reshape(1, width)
    bias_out = jnp.sum(grad_out.astype(f32), 0, keepdims=True)
    with jax.named_scope("gather_grads"):
        early = (cosine, sine, gains, bias_out, labels, valid, seg_col, seg_row, fw)
        grad_far = gather_far(after(grad_out, *early), "head")
    with jax.named_scope("gather_tokens"):
        token_pieces = gather_near({k: after(p, *early) if k else p for k, p in token_far.items()}, "head")
    packet_shape = (head_size + 8, width)

    ln1t, ln2, ln2t, xhat, inv_std, q_expo, k_expo, qf, kf, v, s_own = call(
        functools.partial(pre_kernel, head_size, n_head),
        blocks,
        [
            smem(),
            smem(),
            *[rows_of(BT, share)] * n_head,
            whole(4, model),
            whole(3, model, width),
            whole(3, width),
            whole(1, width),
            whole(2, width, width),
            rows_of(BT, LANES),
            rows_of(BT, LANES),
            rows_of(BT, 1),
            rows_of(BT, 1),
        ],
        [
            pl.BlockSpec((model, BT), lambda i: (0, i)),
            rows_of(BT, model),
            pl.BlockSpec((model, BT), lambda i: (0, i)),
            rows_of(BT, model),
            rows_of(BT, 1),
            rows_of(BT, width),
            rows_of(BT, width),
            rows_of(BT, width),
            rows_of(BT, width),
            rows_of(BT, width),
            whole(*packet_shape),
        ],
        [
            sds((model, rows), bf16),
            sds((rows, model), bf16),
            sds((model, rows), bf16),
            sds((rows, model), bf16),
            sds((rows, 1), f32),
            sds((rows, width), f32),
            sds((rows, width), f32),
            sds((rows, width), bf16),
            sds((rows, width), bf16),
            sds((rows, width), bf16),
            sds(packet_shape, f32),
        ],
        [pltpu.VMEM((BT, model), bf16), pltpu.VMEM((width, width), f32), pltpu.VMEM((8, width), f32)],
        2 * rows * model * 3 * width + 16 * rows * width * width,
        rows * model * 10 + 6 * model * width,
    )(labels, me_head, *token_pieces, gains, w_qkv, b_qkv, fw, tab, cosine, sine, valid, seg_col)

    with jax.named_scope("gather_grads"):
        grad_pieces = gather_near({k: after(p, s_own) for k, p in grad_far.items()}, "head")
    with jax.named_scope("state"):
        s_in = sum_before(s_own)

    fb = 256
    quarter = n_seq // 4
    full_grad, hid, dpre, *ff_sums, gb_in = call(
        functools.partial(ff_kernel, n_head),
        hidden // fb,
        [
            smem(),
            smem(),
            *[whole(rows, share)] * n_head,
            whole(rows, model),
            whole(model, rows),
            pl.BlockSpec((model, fb), lambda i: (0, i)),
            pl.BlockSpec((1, fb), lambda i: (0, i)),
            pl.BlockSpec((fb, model), lambda i: (i, 0)),
        ],
        [
            whole(rows, model),
            pl.BlockSpec((rows, fb), lambda i: (0, i)),
            pl.BlockSpec((rows, fb), lambda i: (0, i)),
            *[whole(quarter, hidden // n_seq, model)] * 4,
            *[pl.BlockSpec((quarter, model // n_seq, fb), lambda i: (0, 0, i))] * 4,
            pl.BlockSpec((1, fb), lambda i: (0, i)),
        ],
        [
            sds((rows, model), bf16),
            sds((rows, hidden), bf16),
            sds((rows, hidden), bf16),
            *[sds((quarter, hidden // n_seq, model), bf16)] * 4,
            *[sds((quarter, model // n_seq, hidden), bf16)] * 4,
            sds((1, hidden), f32),
        ],
        [],
        8 * rows * model * hidden,
        6 * rows * model + 8 * model * hidden,
    )(me_head, me_seq, *grad_pieces, ln2, ln2t, w_in, b_in[None, :], w_down)

    s_in = after(s_in, hid)

    att, dq, dk, dv, gb, gzb, g_own, g_out = call(
        functools.partial(attn_kernel, head_size),
        blocks,
        [
            smem(),
            rows_of(BT, width),
            rows_of(BT, width),
            rows_of(BT, width),
            rows_of(BT, model),
            whole(width, model),
            rows_of(BT, 1),
            pl.BlockSpec((1, BT), lambda i: (0, i)),
            whole(*packet_shape),
        ],
        [
            rows_of(BT, width),
            rows_of(BT, width),
            rows_of(BT, width),
            rows_of(BT, width),
            rows_of(1, width, width),
            rows_of(1, 8, width),
            whole(*packet_shape),
            whole(model, width),
        ],
        [
            sds((rows, width), bf16),
            sds((rows, width), f32),
            sds((rows, width), f32),
            sds((rows, width), f32),
            sds((blocks, width, width), f32),
            sds((blocks, 8, width), f32),
            sds(packet_shape, f32),
            sds((model, width), bf16),
        ],
        [
            pltpu.VMEM((width, width), f32),
            pltpu.VMEM((8, width), f32),
            pltpu.VMEM((width, width), f32),
            pltpu.VMEM((8, width), f32),
            pltpu.VMEM((width, model), f32),
        ],
        24 * rows * heads * BT * width,
        rows * model * 2 + rows * width * 20,
    )(labels, qf, kf, v, full_grad, w_out, seg_col, seg_row, s_in)

    down = Sum("reduce_down", ff_sums[:4])
    seen = []
    with jax.named_scope("grad_state"):
        grad_in = neighbour_sum(g_own, -1, hid, seen.append)
    inn = Sum("reduce_in", [ff_sums[4], *after(tuple(ff_sums[5:]), *seen)])
    event = down.step(*seen)
    grad_in = after(grad_in, event)

    def back_rows(*shape):
        return pl.BlockSpec(shape, lambda i: (blocks - 1 - i,) + (0,) * (len(shape) - 1))

    part = model // n_seq
    low, small, *w_parts = call(
        functools.partial(tail_kernel, head_size),
        blocks,
        [
            smem(),
            *[back_rows(BT, width)] * 7,
            back_rows(1, width, width),
            back_rows(1, 8, width),
            whole(*packet_shape),
            back_rows(BT, 1),
            back_rows(BT, LANES),
            back_rows(BT, LANES),
            whole(1, width),
            whole(2, width, width),
            whole(model, rows),
            whole(model, width),
            smem(),
        ],
        [
            pl.BlockSpec((3, BT, width), lambda i: (0, blocks - 1 - i, 0)),
            whole(8, width),
            *[whole(quarter, 4, part, width)] * 4,
        ],
        [
            sds((3, rows, width), bf16),
            sds((8, width), f32),
            *[sds((quarter, 4, part, width), bf16)] * 4,
        ],
        [
            pltpu.VMEM((width, width), f32),
            pltpu.VMEM((8, width), f32),
            pltpu.VMEM((3, rows, width), bf16),
        ],
        2 * rows * model * 3 * width,
        rows * width * 30 + rows * model * 2 + 6 * model * width,
    )(labels, dq, dk, dv, q_expo, k_expo, kf, v, gb, gzb, grad_in, seg_col, cosine, sine, fw, tab, ln1t, g_out, me_seq)

    qkvo = Sum("reduce_attn", w_parts)
    event = low
    chunks = {"D": down, "I": inn, "C": qkvo}
    for name in BEFORE:
        event = chunks[name].step(event)

    stat_width = max(rows, model)
    val_keep, val_send, e_keep, e_send, stats = call(
        finish_kernel,
        blocks,
        [
            smem(),
            rows_of(BT, hidden),
            whole(hidden, model),
            rows_of(BT, width),
            whole(width, model),
            rows_of(BT, hidden),
            pl.BlockSpec((3, BT, width), lambda i: (0, i, 0)),
            whole(3, model, width),
            whole(model, hidden),
            rows_of(BT, model),
            whole(4, model),
        ],
        [
            *[pl.BlockSpec((n_head // 2, BT, share), lambda i: (0, i, 0))] * 4,
            whole(16, stat_width),
        ],
        [
            *[sds((n_head // 2, rows, share), bf16)] * 4,
            sds((16, stat_width), f32),
        ],
        [pltpu.VMEM((BT, model), bf16)],
        2 * rows * model * (3 * width + hidden),
        rows * width * 6 + rows * model * 6 + 8 * model * width + 2 * hidden * model,
    )(me_head, hid, w_down, att, w_out, dpre, after(low, event), w_qkv, w_in, xhat, gains)
    with jax.named_scope("mixed_sum"):
        mixed_share = scatter_sum(val_keep, after(val_send, low), "head")
    with jax.named_scope("e_sum"):
        e_share = scatter_sum(e_keep, e_send, "head")
    with jax.named_scope("stats_sum"):
        gains_own = stats[8:12, :model]
        stats = sum_all(stats[:8], "head")
    stats = stats[:2, :rows].T * (1.0 / model)

    bias = lax.dynamic_slice_in_dim(b_out, offset, share) + lax.dynamic_slice_in_dim(b_down, offset, share)
    mixed = (tokens.astype(f32) + mixed_share + bias).astype(bf16)
    xhat_share = lax.dynamic_slice_in_dim(xhat, offset, share, 1).astype(f32)
    grad_input = grad_out.astype(f32) + inv_std * (
        e_share - stats[:, 0:1] - xhat_share * stats[:, 1:2]
    )
    event = late = e_send
    for name in AFTER:
        chunk = chunks[name]
        if chunk.plan:
            pins = (mixed, grad_input) if len(chunk.plan) == 1 and name in PINNED else ()
            event = chunk.step(event, *pins)
        late = event if len(qkvo.plan) == LATE else late
    for chunk in chunks.values():
        while chunk.plan:
            event = chunk.step(event)
    g_down = block_out(down, me_seq)
    g_in = block_out(inn, me_seq)
    g_qkv, g_out = call(
        widen_kernel,
        4,
        [smem(), *[pl.BlockSpec((quarter, 1, part, width), lambda c: (0, c, 0, 0))] * 4],
        [
            pl.BlockSpec((1, model, width), lambda c: (jnp.minimum(c, 2), 0, 0)),
            whole(width, model),
        ],
        [sds((3, model, width), f32), sds((width, model), f32)],
        [pltpu.VMEM((model, width), f32)],
        0,
        END_COST * model * width,
    )(me_seq, *qkvo.arrays)

    with jax.named_scope("small_sum"):
        local = jnp.concatenate([small[:4], gb_in.reshape(-1, share), bias_out], 0)
        mine = (jnp.arange(n_head) == lax.axis_index("head")).astype(f32)
        spread_gains = gains_own.reshape(4, n_head, share).transpose(1, 0, 2)
        packet = jnp.concatenate([spread_gains, mine[:, None, None] * local[None]], 1)
        packet = jnp.broadcast_to(packet[None], (n_seq,) + packet.shape).reshape((-1,) + packet.shape[1:])
        packet = jnp.sum(lax.all_to_all(after(packet, late), ("seq", "head"), 0, 0, tiled=True), 0)
    gain_share, small, gb_in, bias_out = packet[:4], packet[4:8], packet[8:-1].reshape(-1), packet[-1]
    return (
        mixed,
        grad_input,
        gain_share[0],
        gain_share[1],
        gain_share[2],
        gain_share[3],
        g_qkv,
        small[:3],
        small[3].reshape(heads, feats),
        g_out,
        bias_out,
        g_in,
        gb_in,
        g_down,
        bias_out,
    )


def solution(mesh):
    in_specs = (
        P("seq", "head"),
        P(),
        P("seq"),
        P(),
        P(),
        P(),
        P(),
        P(None, None, "head"),
        P(None, "head"),
        P("head", None),
        P("head", None),
        P(),
        P(None, "head"),
        P("head"),
        P("head", None),
        P(),
        P("seq", "head"),
    )
    out_specs = (
        P("seq", "head"),
        P("seq", "head"),
        P("head"),
        P("head"),
        P("head"),
        P("head"),
        P(None, None, "head"),
        P(None, "head"),
        P("head", None),
        P("head", None),
        P("head"),
        P(None, "head"),
        P("head"),
        P("head", None),
        P("head"),
    )
    return jax.shard_map(body, mesh=mesh, in_specs=in_specs, out_specs=out_specs, check_vma=False)
```

```python
import functools
import math
from statistics import NormalDist

import jax
import jax.numpy as jnp
import numpy as np
from jax import lax
from jax.experimental import pallas as pl
from jax.experimental.pallas import tpu as pltpu
from jax.sharding import PartitionSpec as P

ROT = 16
eps_norm = 1e-05
rope_base = 10000.0
feature_scale = 0.5
BT = 256
LANES = 128
bf16 = jnp.bfloat16
f32 = jnp.float32
COST_SCALE = 1.0
END_COST = 12
BEFORE = "DI"
AFTER = "DCICIDCIC"
PINNED = "C"
LATE = 3
VMEM_LIMIT = 56 * 1024 * 1024


def nn(a, b):
    return lax.dot_general(a, b, (((1,), (0,)), ((), ())), preferred_element_type=f32)


def nt(a, b):
    return lax.dot_general(a, b, (((1,), (1,)), ((), ())), preferred_element_type=f32)


def tn(a, b):
    return lax.dot_general(a, b, (((0,), (0,)), ((), ())), preferred_element_type=f32)


def split(x):
    hi = x.astype(bf16)
    return hi, (x - hi.astype(f32)).astype(bf16)


def feature_table(feat_count, head_size):
    rows = np.arange(feat_count)
    cols = np.arange(head_size)
    cosines = np.cos(math.pi * (cols[None, :] + 0.5) * rows[:, None] / head_size)
    scaling = np.where(rows == 0, math.sqrt(1.0 / head_size), math.sqrt(2.0 / head_size))
    points = np.array([NormalDist().inv_cdf((r + 0.5) / feat_count) for r in range(feat_count)])
    return feature_scale * (points * scaling)[:, None] * cosines


def lane_head(shape, head_size):
    return lax.broadcasted_iota(jnp.int32, shape, len(shape) - 1) // head_size


def block_ones(size, head_size):
    rows = lax.broadcasted_iota(jnp.int32, (size, size), 0) // head_size
    cols = lax.broadcasted_iota(jnp.int32, (size, size), 1) // head_size
    return rows == cols


def swap_halves(x, head_size):
    width = x.shape[1]
    lane = lax.broadcasted_iota(jnp.int32, x.shape, 1) % head_size
    ahead = pltpu.roll(x, width - ROT // 2, 1)
    behind = pltpu.roll(x, ROT // 2, 1)
    return jnp.where(lane < ROT // 2, ahead, behind)


def widen(table, width):
    return table if table.shape[1] == width else jnp.concatenate([table] * (width // table.shape[1]), 1)


def pack_state(state, norm, head_size):
    size = state.shape[0]
    masked = jnp.where(block_ones(size, head_size), state, 0.0)
    packed = masked[:head_size]
    for h in range(1, size // head_size):
        packed = packed + masked[h * head_size : (h + 1) * head_size]
    return packed, norm


def unpack_state(packed, head_size):
    size = packed.shape[1]
    rows = jnp.concatenate([packed[:head_size]] * (size // head_size), 0)
    return jnp.where(block_ones(size, head_size), rows, 0.0)


def place(full_ref, piece_refs, me_ref):
    for k, ref in enumerate(piece_refs):
        size = ref.shape[1]
        start = pl.multiple_of((me_ref[0] ^ k) * size, LANES)
        full_ref[:, pl.ds(start, size)] = ref[...]


def pre_kernel(
    head_size,
    pieces,
    labels_ref,
    me_ref,
    *refs,
):
    x_refs = refs[:pieces]
    (
        gains_ref,
        w_ref,
        bq_ref,
        fw_ref,
        tab_ref,
        cos_ref,
        sin_ref,
        valid_ref,
        seg_ref,
        ln1t_ref,
        ln2_ref,
        ln2t_ref,
        xhat_ref,
        inv_ref,
        qe_ref,
        ke_ref,
        qf_ref,
        kf_ref,
        v_ref,
        pk_ref,
        full_ref,
        state_ref,
        norm_ref,
    ) = refs[pieces:]
    step = pl.program_id(0)
    width = qe_ref.shape[1]
    place(full_ref, x_refs, me_ref)
    x = full_ref[...].astype(f32)
    centered = x - jnp.mean(x, -1, keepdims=True)
    inv = lax.rsqrt(jnp.mean(centered * centered, -1, keepdims=True) + eps_norm)
    xhat = centered * inv
    inv_ref[...] = inv
    xhat_ref[...] = xhat.astype(bf16)
    ln1 = (xhat * gains_ref[0:1] + gains_ref[1:2]).astype(bf16)
    ln2 = (xhat * gains_ref[2:3] + gains_ref[3:4]).astype(bf16)
    ln2_ref[...] = ln2
    ln1t_ref[...] = ln1.T
    ln2t_ref[...] = ln2.T
    cosine = widen(cos_ref[...], width)
    sine = widen(sin_ref[...], width)

    def features(c):
        raw = nn(ln1, w_ref[c]) + bq_ref[c : c + 1]
        turned = raw * cosine + swap_halves(raw, head_size) * sine
        hi, lo = split(turned)
        return jnp.exp(nn(hi, tab_ref[0]) + nn(lo, tab_ref[0]) + nn(hi, tab_ref[1]))

    fw = fw_ref[...]
    qe = features(0)
    ke = features(1) * valid_ref[...]
    qe_ref[...] = qe
    ke_ref[...] = ke
    qf_ref[...] = (fw * qe).astype(bf16)
    kf = (fw * ke).astype(bf16)
    kf_ref[...] = kf
    v = (nn(ln1, w_ref[2]) + bq_ref[2:3]).astype(bf16)
    v_ref[...] = v

    @pl.when(step == 0)
    def _():
        state_ref[...] = jnp.zeros_like(state_ref)
        norm_ref[...] = jnp.zeros_like(norm_ref)

    tail = kf.astype(f32) * (seg_ref[...] == labels_ref[pl.num_programs(0) - 1, 1]).astype(f32)
    state_ref[...] += tn(tail.astype(bf16), v)
    norm_ref[...] += jnp.broadcast_to(jnp.sum(tail, 0, keepdims=True), norm_ref.shape)

    @pl.when(step == pl.num_programs(0) - 1)
    def _():
        packed, norm = pack_state(state_ref[...], norm_ref[...], head_size)
        for i in range(pk_ref.shape[0]):
            pk_ref[i, :head_size] = packed
            pk_ref[i, head_size:] = norm


def slot_of(relative, count):
    place = 0
    mask = 4
    while mask < count:
        place = 2 * place + (relative // mask) % 2
        mask *= 2
    return place


def store_blocks(block, base, me, refs, part, rest=()):
    count = 4 * refs[0].shape[0]
    for low in range(4):

        @pl.when(me % 4 == low)
        def _():
            for j in range(block.shape[0] // part):
                ref = refs[(low ^ (base + j)) % 4]
                ref[(slot_of(me ^ (base + j), count),) + rest] = block[j * part : (j + 1) * part]


def ff_kernel(pieces, me_ref, rank_ref, *refs):
    grad_refs = refs[:pieces]
    (
        ln2_ref,
        ln2t_ref,
        win_ref,
        bin_ref,
        wdown_ref,
        grad_ref,
        hid_ref,
        dpre_ref,
        *sum_refs,
        gb_ref,
    ) = refs[pieces:]

    @pl.when(pl.program_id(0) == 0)
    def _():
        place(grad_ref, grad_refs, me_ref)

    chunk = ln2_ref.shape[0] // 4
    sums = jnp.zeros((1, win_ref.shape[1]), f32)
    for r in range(4):
        part = slice(r * chunk, (r + 1) * chunk)
        pre = nn(ln2_ref[part], win_ref[...]) + bin_ref[...]
        phi_cum = 0.5 + 0.5 * lax.erf(pre * (1.0 / math.sqrt(2.0)))
        hid_ref[part] = (pre * phi_cum).astype(bf16)
        slope = phi_cum + pre * jnp.exp(-0.5 * pre * pre) * (1.0 / math.sqrt(2.0 * math.pi))
        dpre = nt(grad_ref[part], wdown_ref[...]) * slope
        sums = sums + jnp.sum(dpre, 0, keepdims=True)
        dpre_ref[part] = dpre.astype(bf16)
    gb_ref[...] = sums
    me = rank_ref[0]
    g_down = tn(hid_ref[...], grad_ref[...]).astype(bf16)
    part = sum_refs[0].shape[1]
    steps = 4 * sum_refs[0].shape[0] * part // g_down.shape[0]
    for step in range(steps):

        @pl.when(pl.program_id(0) == step)
        def _():
            store_blocks(g_down, step * (g_down.shape[0] // part), me, sum_refs[:4], part)

    g_in = nn(ln2t_ref[...], dpre_ref[...]).astype(bf16)
    store_blocks(g_in, 0, me, sum_refs[4:], sum_refs[4].shape[1])


def block_out_kernel(rank_ref, *refs):
    out_ref = refs[4]
    part = refs[0].shape[1]
    for low in range(4):

        @pl.when(rank_ref[0] % 4 == low)
        def _():
            for j in range(4):
                out_ref[j * part : (j + 1) * part] = refs[low ^ j][0].astype(f32)


def attn_kernel(
    head_size,
    labels_ref,
    qf_ref,
    kf_ref,
    v_ref,
    grad_ref,
    wout_ref,
    segc_ref,
    segr_ref,
    spk_ref,
    att_ref,
    dq_ref,
    dk_ref,
    dv_ref,
    gb_ref,
    gzb_ref,
    gpk_ref,
    gout_ref,
    state_ref,
    norm_ref,
    lead_ref,
    leadz_ref,
    acc_ref,
):
    step = pl.program_id(0)
    last = pl.num_programs(0) - 1
    rows, width = qf_ref.shape
    heads = width // head_size
    same = block_ones(width, head_size)
    ones = same.astype(f32).astype(bf16)

    def head_sum(x):
        hi, lo = split(x)
        return nn(hi, ones) + nn(lo, ones)

    @pl.when(step == 0)
    def _():
        state_ref[...] = unpack_state(spk_ref[...], head_size)
        norm_ref[...] = spk_ref[head_size : head_size + 8]
        lead_ref[...] = jnp.zeros_like(lead_ref)
        leadz_ref[...] = jnp.zeros_like(leadz_ref)
        acc_ref[...] = jnp.zeros_like(acc_ref)

    seg = segc_ref[...]
    enters = (seg == labels_ref[step, 0]).astype(f32)
    tail = (seg == labels_ref[step, 1]).astype(f32)
    lead = (seg == labels_ref[0, 2]).astype(f32)
    linked = (labels_ref[step, 0] == labels_ref[step, 1]).astype(f32)
    qf = qf_ref[...]
    kf = kf_ref[...]
    v = v_ref[...]
    qf32 = qf.astype(f32)
    norm = norm_ref[0:1]
    lane = lane_head((rows, width), head_size)
    zero16 = jnp.zeros((rows, width), bf16)

    def stack(x):
        return jnp.concatenate([jnp.where(lane == h, x, zero16) for h in range(heads)], 0)

    def unstack(x):
        total = jnp.where(lane == 0, x[:rows], 0.0)
        for h in range(1, heads):
            total = jnp.where(lane == h, x[h * rows : (h + 1) * rows], total)
        return total

    causal = lax.broadcasted_iota(jnp.int32, (rows, rows), 0) >= lax.broadcasted_iota(
        jnp.int32, (rows, rows), 1
    )
    joined = causal & (seg == segr_ref[...])
    joined_all = jnp.concatenate([joined.astype(f32)] * heads, 0)
    q_stack = stack(qf)
    scores = (nt(q_stack, kf) * joined_all).astype(bf16)
    ones_v = jnp.ones((rows, LANES), bf16)
    sums = nn(scores, ones_v)
    den_in = jnp.where(lane == 0, widen(sums[:rows], width), 0.0)
    for h in range(1, heads):
        den_in = jnp.where(lane == h, widen(sums[h * rows : (h + 1) * rows], width), den_in)
    s_hi, s_lo = split(state_ref[...])
    num = unstack(nn(scores, v)) + enters * (nn(qf, s_hi) + nn(qf, s_lo))
    den = den_in + enters * head_sum(qf32 * norm)
    inv_den = 1.0 / den
    att = num * inv_den
    att_low = att.astype(bf16)
    att_ref[...] = att_low
    acc_ref[...] += tn(att_low, grad_ref[...])
    d_att = nt(grad_ref[...], wout_ref[...])
    d_num = d_att * inv_den
    d_den = -head_sum(d_att * att) * inv_den
    dn_hi, dn_lo = split(d_num)
    dn_stack = stack(dn_hi)
    dden_all = jnp.concatenate([d_den[:, h * head_size : h * head_size + 1] for h in range(heads)], 0)
    d_scores = ((nt(dn_stack, v) + dden_all) * joined_all).astype(bf16)
    inter = nt(dn_hi, s_hi) + nt(dn_lo, s_hi) + nt(dn_hi, s_lo) + d_den * norm
    dq_ref[...] = unstack(nn(d_scores, kf)) + enters * inter
    dk_ref[...] = tn(d_scores, q_stack)
    dv_ref[...] = tn(scores, dn_stack)
    q_in = (qf32 * enters).astype(bf16)
    gb_ref[0] = jnp.where(same, tn(q_in, dn_hi) + tn(q_in, dn_lo), 0.0)
    weighted = qf32 * d_den
    gzb_ref[0] = jnp.broadcast_to(jnp.sum(weighted * enters, 0, keepdims=True), (8, width))
    q_lead = (qf32 * lead).astype(bf16)
    lead_ref[...] += tn(q_lead, dn_hi) + tn(q_lead, dn_lo)
    leadz_ref[...] += jnp.broadcast_to(jnp.sum(weighted * lead, 0, keepdims=True), (8, width))
    k_tail = kf.astype(f32) * tail
    state_ref[...] = linked * state_ref[...] + jnp.where(same, tn(k_tail.astype(bf16), v), 0.0)
    norm_ref[...] = linked * norm_ref[...] + jnp.broadcast_to(jnp.sum(k_tail, 0, keepdims=True), (8, width))

    @pl.when(step == last)
    def _():
        packed, z = pack_state(lead_ref[...], leadz_ref[...], head_size)
        gpk_ref[:head_size] = packed
        gpk_ref[head_size:] = z
        gout_ref[...] = acc_ref[...].T.astype(bf16)


def spread(full, keep_ref, send_ref, scratch_ref, me_ref):
    scratch_ref[...] = full.astype(bf16)
    size = keep_ref.shape[2]
    for k in range(2 * keep_ref.shape[0]):
        start = pl.multiple_of((me_ref[0] ^ k) * size, LANES)
        (send_ref if k % 2 else keep_ref)[k // 2] = scratch_ref[:, pl.ds(start, size)]


def tail_kernel(
    head_size,
    labels_ref,
    dq_ref,
    dk_ref,
    dv_ref,
    qe_ref,
    ke_ref,
    kf_ref,
    v_ref,
    gb_ref,
    gzb_ref,
    gin_ref,
    segc_ref,
    cos_ref,
    sin_ref,
    fw_ref,
    tab_ref,
    ln1t_ref,
    gout_ref,
    rank_ref,
    low_ref,
    small_ref,
    sum0_ref,
    sum1_ref,
    sum2_ref,
    sum3_ref,
    state_ref,
    norm_ref,
    all_ref,
):
    step = pl.program_id(0)
    last = pl.num_programs(0) - 1
    block = last - step
    rows, width = dq_ref.shape

    @pl.when(step == 0)
    def _():
        state_ref[...] = unpack_state(gin_ref[...], head_size)
        norm_ref[...] = gin_ref[head_size : head_size + 8]
        small_ref[...] = jnp.zeros_like(small_ref)

    tail = (segc_ref[...] == labels_ref[block, 1]).astype(f32)
    linked = (labels_ref[block, 0] == labels_ref[block, 1]).astype(f32)
    g_hi, g_lo = split(state_ref[...])
    v = v_ref[...]
    kf = kf_ref[...]
    dk = dk_ref[...] + tail * (nt(v, g_hi) + nt(v, g_lo) + norm_ref[0:1])
    dv = dv_ref[...] + tail * (nn(kf, g_hi) + nn(kf, g_lo))
    state_ref[...] = linked * state_ref[...] + gb_ref[0]
    norm_ref[...] = linked * norm_ref[...] + gzb_ref[0]
    fw = fw_ref[...]
    gq = dq_ref[...] * qe_ref[...]
    gk = dk * ke_ref[...]
    cosine = widen(cos_ref[...], width)
    sine = widen(sin_ref[...], width)

    def back(g):
        hi, lo = split(g * fw)
        turned = nt(hi, tab_ref[0]) + nt(lo, tab_ref[0]) + nt(hi, tab_ref[1])
        return turned * cosine - swap_halves(turned, head_size) * sine

    dq_raw = back(gq)
    dk_raw = back(gk)
    small_ref[0:1] += jnp.sum(dq_raw, 0, keepdims=True)
    small_ref[1:2] += jnp.sum(dk_raw, 0, keepdims=True)
    small_ref[2:3] += jnp.sum(dv, 0, keepdims=True)
    small_ref[3:4] += jnp.sum(gq + gk, 0, keepdims=True)
    start = pl.multiple_of(block * rows, rows)
    for c, d in enumerate((dq_raw, dk_raw, dv)):
        low = d.astype(bf16)
        low_ref[c] = low
        all_ref[c, pl.ds(start, rows)] = low

    @pl.when(step == last)
    def _():
        me = rank_ref[0]
        part = sum0_ref.shape[2]
        for c in range(4):
            g = gout_ref[...] if c == 3 else nn(ln1t_ref[...], all_ref[c]).astype(bf16)

            store_blocks(g, 0, me, (sum0_ref, sum1_ref, sum2_ref, sum3_ref), part, (c,))


def finish_kernel(
    me_ref,
    hid_ref,
    wdown_ref,
    att_ref,
    wout_ref,
    dpre_ref,
    low_ref,
    w_ref,
    win_ref,
    xhat_ref,
    gains_ref,
    val_keep_ref,
    val_send_ref,
    keep_ref,
    send_ref,
    stat_ref,
    scratch_ref,
):
    value = nn(hid_ref[...], wdown_ref[...]) + nn(att_ref[...], wout_ref[...])
    spread(value, val_keep_ref, val_send_ref, scratch_ref, me_ref)
    step = pl.program_id(0)
    rows, model = xhat_ref.shape

    @pl.when(step == 0)
    def _():
        stat_ref[8:16] = jnp.zeros((8, stat_ref.shape[1]), f32)

    d_ln1 = nt(low_ref[0], w_ref[0]) + nt(low_ref[1], w_ref[1]) + nt(low_ref[2], w_ref[2])
    d_ln2 = nt(dpre_ref[...], win_ref[...])
    xhat = xhat_ref[...].astype(f32)
    e = d_ln1 * gains_ref[0:1] + d_ln2 * gains_ref[2:3]
    spread(e, keep_ref, send_ref, scratch_ref, me_ref)
    ones = jnp.ones((8, model), bf16)
    hi, lo = split(e)
    sum_e = nt(ones, hi) + nt(ones, lo)
    hi, lo = split(e * xhat)
    sum_ex = nt(ones, hi) + nt(ones, lo)
    row = lax.broadcasted_iota(jnp.int32, sum_e.shape, 0)
    start = pl.multiple_of(step * rows, rows)
    stat_ref[0:8, pl.ds(start, rows)] = jnp.where(row == 0, sum_e, sum_ex)
    stat_ref[8:9, :model] += jnp.sum(d_ln1 * xhat, 0, keepdims=True)
    stat_ref[9:10, :model] += jnp.sum(d_ln1, 0, keepdims=True)
    stat_ref[10:11, :model] += jnp.sum(d_ln2 * xhat, 0, keepdims=True)
    stat_ref[11:12, :model] += jnp.sum(d_ln2, 0, keepdims=True)


def widen_kernel(rank_ref, *refs):
    qkv_ref, out_ref, scratch_ref = refs[4:]
    c = pl.program_id(0)
    quarter, _, part, _ = refs[0].shape
    me = rank_ref[0]
    for low in range(4):

        @pl.when(me % 4 == low)
        def _():
            for j in range(4 * quarter):
                slot = slot_of(me ^ j, 4 * quarter)
                scratch_ref[j * part : (j + 1) * part] = refs[(low ^ j) % 4][slot, 0].astype(f32)

    @pl.when(c < 3)
    def _():
        qkv_ref[0] = scratch_ref[...]

    @pl.when(c == 3)
    def _():
        out_ref[...] = scratch_ref[...].T


def whole(*shape):
    return pl.BlockSpec(shape, lambda *_: (0,) * len(shape))


def rows_of(*shape):
    return pl.BlockSpec(shape, lambda i: (i,) + (0,) * (len(shape) - 1))


def smem():
    return pl.BlockSpec(memory_space=pltpu.SMEM)


def sds(shape, dtype):
    return jax.ShapeDtypeStruct(shape, dtype)


def call(kernel, grid, in_specs, out_specs, out_shape, scratch, flops, moved, aliases={}):
    return pl.pallas_call(
        kernel,
        grid=(grid,),
        in_specs=in_specs,
        out_specs=out_specs,
        out_shape=out_shape,
        scratch_shapes=scratch,
        input_output_aliases=aliases,
        compiler_params=pltpu.CompilerParams(vmem_limit_bytes=VMEM_LIMIT),
        cost_estimate=pl.CostEstimate(
            flops=int(flops * COST_SCALE), bytes_accessed=int(moved * COST_SCALE), transcendentals=0
        ),
        name=getattr(kernel, "func", kernel).__name__,
    )


def exchange(x, axis, mask):
    count = lax.axis_size(axis)
    return lax.ppermute(x, axis, [(i, i ^ mask) for i in range(count)])


def gather_far(x, axis):
    pieces = {0: x}
    mask = lax.axis_size(axis) // 2
    while mask > 1:
        pieces.update({k ^ mask: exchange(p, axis, mask) for k, p in sorted(pieces.items())})
        mask //= 2
    return pieces


def gather_near(pieces, axis):
    pieces = pieces | {k ^ 1: exchange(p, axis, 1) for k, p in sorted(pieces.items())}
    return [pieces[k] for k in sorted(pieces)]


def scatter_sum(keep, send, axis):
    mask = 1
    while True:
        got = exchange(send, axis, mask)
        if keep.shape[0] == 1:
            return keep[0].astype(f32) + got[0].astype(f32)
        total_keep = keep[0::2].astype(f32) + got[0::2].astype(f32)
        total_send = keep[1::2].astype(f32) + got[1::2].astype(f32)
        keep, send = total_keep.astype(bf16), total_send.astype(bf16)
        mask *= 2


def sum_all(x, axis):
    mask = 1
    while mask < lax.axis_size(axis):
        x = x + exchange(x, axis, mask)
        mask *= 2
    return x


class Sum:
    def __init__(self, name, arrays):
        self.name, self.arrays = name, list(arrays)
        masks = []
        while 4 * 2 ** len(masks) < lax.axis_size("seq"):
            masks.append(4 * 2 ** len(masks))
        self.plan = [("group", 0)] + [("reduce", m) for m in masks]
        self.plan += [("gather", m) for m in masks[::-1]] + [("spread", 0)]

    def halves(self, terms):
        half = terms[0].shape[0] // 2

        def total(part):
            return sum(t[part].astype(f32) for t in terms).astype(bf16)

        if half:
            self.keep, self.send = total(slice(0, half)), total(slice(half, None))
        else:
            self.keep = self.send = total(slice(None))
        return self.send

    def step(self, *pins):
        kind, mask = self.plan.pop(0)
        with jax.named_scope(self.name):
            if kind == "group":
                got = after(tuple(exchange(self.arrays[g], "seq", g) for g in (1, 2, 3)), *pins)
                return self.halves([self.arrays[0], *got])
            if kind == "reduce":
                return self.halves([self.keep, after(exchange(self.send, "seq", mask), *pins)])
            if kind == "gather":
                self.keep = jnp.concatenate([self.keep, after(exchange(self.keep, "seq", mask), *pins)])
                return self.keep
            self.arrays = [self.keep, *after(tuple(exchange(self.keep, "seq", g) for g in (1, 2, 3)), *pins)]
            return self.arrays[1]


def block_out(chunk, me_seq):
    quarter, part, width = chunk.keep.shape
    block = pl.BlockSpec((1, part, width), lambda i, me: (slot_of(((me[0] // 4) ^ i) * 4, 4 * quarter), 0, 0))
    return pl.pallas_call(
        block_out_kernel,
        grid_spec=pltpu.PrefetchScalarGridSpec(
            num_scalar_prefetch=1,
            grid=(quarter,),
            in_specs=[block] * 4,
            out_specs=pl.BlockSpec((4 * part, width), lambda i, me: (i, 0)),
        ),
        out_shape=sds((4 * quarter * part, width), f32),
        compiler_params=pltpu.CompilerParams(vmem_limit_bytes=VMEM_LIMIT),
        cost_estimate=pl.CostEstimate(flops=0, bytes_accessed=24 * quarter * part * width, transcendentals=0),
        name="block_out_kernel",
    )(me_seq, *chunk.arrays)


def sum_before(copies):
    count = lax.axis_size("seq")
    packets = lax.all_to_all(copies, "seq", 0, 0, tiled=True)
    wanted = (jnp.arange(count) < lax.axis_index("seq")).astype(f32)
    return jnp.sum(packets * wanted[:, None, None], 0)


def after(x, *others):
    return lax.optimization_barrier((x,) + others)[0]


def neighbour_sum(packet, sign, pin, event):
    count = lax.axis_size("seq")
    outer = 4 if count % 4 == 0 else 1
    inner = count // outer
    me = lax.axis_index("seq")
    mine = me % inner
    group = packet
    before = jnp.zeros_like(packet)
    for k in range(1, inner):
        route = [(i, i - i % inner + (i % inner + k) % inner) for i in range(count)]
        got = after(lax.ppermute(packet, "seq", route), pin)
        event(got)
        sender = (mine - k) % inner
        group = group + got
        before = before + jnp.where((sender < mine) if sign > 0 else (sender > mine), got, 0.0)
    for k in range(1, outer):
        shift = sign * k * inner
        route = [(i, i + shift) for i in range(count) if 0 <= i + shift < count]
        before = before + lax.ppermute(group, "seq", route)
    return before


def body(
    tokens,
    lengths,
    pad_mask,
    ln1_gain,
    ln1_bias,
    ln2_gain,
    ln2_bias,
    w_qkv,
    b_qkv,
    feat_weight,
    w_out,
    b_out,
    w_in,
    b_in,
    w_down,
    b_down,
    grad_out,
):
    rows, share = tokens.shape
    heads, feats = feat_weight.shape
    width = w_qkv.shape[2]
    head_size = width // heads
    model, hidden = w_in.shape
    blocks = rows // BT
    n_head = lax.axis_size("head")
    offset = lax.axis_index("head") * share
    with jax.named_scope("gather_tokens"):
        token_far = gather_far(tokens, "head")
    me_head = jnp.reshape(lax.axis_index("head"), (1,)).astype(jnp.int32)
    me_seq = jnp.reshape(lax.axis_index("seq"), (1,)).astype(jnp.int32)
    n_seq = lax.axis_size("seq")

    index_all = lax.axis_index("seq") * rows + jnp.arange(rows, dtype=jnp.int32)
    seq_ends = jnp.cumsum(lengths).astype(jnp.int32)
    starts = seq_ends - lengths

    def seg_of(index):
        return jnp.sum((index[:, None] >= seq_ends[None, :]).astype(jnp.int32), 1)

    segment = seg_of(index_all)
    picked = segment[:, None] == jnp.arange(lengths.shape[0])[None, :]
    position = index_all - jnp.sum(jnp.where(picked, starts[None, :], 0), 1)
    base = lax.axis_index("seq") * rows + jnp.arange(blocks, dtype=jnp.int32) * BT
    label_in = seg_of(jnp.maximum(base - 1, 0))
    label_last = seg_of(base + (BT - 1))
    label_first = jnp.broadcast_to(segment[0], (blocks,))
    labels = jnp.stack([label_in, label_last, label_first], 1)
    seg_col = segment[:, None]
    seg_row = segment[None, :]
    lane = np.arange(LANES) % head_size
    inverse = np.where(lane < ROT, rope_base ** (-2.0 * (lane % (ROT // 2)) / ROT), 0.0)
    angles = position.astype(f32)[:, None] * jnp.asarray(inverse, f32)[None, :]
    sign = np.where(lane < ROT // 2, -1.0, np.where(lane < ROT, 1.0, 0.0))
    cosine = jnp.cos(angles)
    sine = jnp.sin(angles) * jnp.asarray(sign, f32)[None, :]
    valid = pad_mask.astype(f32)[:, None]
    table = np.kron(np.eye(heads), feature_table(feats, head_size).T).astype(np.float32)
    table_hi = table.astype(bf16)
    table_lo = (table - table_hi.astype(np.float32)).astype(bf16)
    tab = jnp.asarray(np.stack([table_hi, table_lo]))
    gains = jnp.stack([ln1_gain, ln1_bias, ln2_gain, ln2_bias])
    fw = feat_weight.reshape(1, width)
    bias_out = jnp.sum(grad_out.astype(f32), 0, keepdims=True)
    with jax.named_scope("gather_grads"):
        early = (cosine, sine, gains, bias_out, labels, valid, seg_col, seg_row, fw)
        grad_far = gather_far(after(grad_out, *early), "head")
    with jax.named_scope("gather_tokens"):
        token_pieces = gather_near({k: after(p, *early) if k else p for k, p in token_far.items()}, "head")
    packet_shape = (head_size + 8, width)

    ln1t, ln2, ln2t, xhat, inv_std, q_expo, k_expo, qf, kf, v, s_own = call(
        functools.partial(pre_kernel, head_size, n_head),
        blocks,
        [
            smem(),
            smem(),
            *[rows_of(BT, share)] * n_head,
            whole(4, model),
            whole(3, model, width),
            whole(3, width),
            whole(1, width),
            whole(2, width, width),
            rows_of(BT, LANES),
            rows_of(BT, LANES),
            rows_of(BT, 1),
            rows_of(BT, 1),
        ],
        [
            pl.BlockSpec((model, BT), lambda i: (0, i)),
            rows_of(BT, model),
            pl.BlockSpec((model, BT), lambda i: (0, i)),
            rows_of(BT, model),
            rows_of(BT, 1),
            rows_of(BT, width),
            rows_of(BT, width),
            rows_of(BT, width),
            rows_of(BT, width),
            rows_of(BT, width),
            whole(n_seq, *packet_shape),
        ],
        [
            sds((model, rows), bf16),
            sds((rows, model), bf16),
            sds((model, rows), bf16),
            sds((rows, model), bf16),
            sds((rows, 1), f32),
            sds((rows, width), f32),
            sds((rows, width), f32),
            sds((rows, width), bf16),
            sds((rows, width), bf16),
            sds((rows, width), bf16),
            sds((n_seq,) + packet_shape, f32),
        ],
        [pltpu.VMEM((BT, model), bf16), pltpu.VMEM((width, width), f32), pltpu.VMEM((8, width), f32)],
        2 * rows * model * 3 * width + 16 * rows * width * width,
        rows * model * 10 + 6 * model * width,
    )(labels, me_head, *token_pieces, gains, w_qkv, b_qkv, fw, tab, cosine, sine, valid, seg_col)

    with jax.named_scope("gather_grads"):
        grad_pieces = gather_near({k: after(p, s_own) for k, p in grad_far.items()}, "head")
    with jax.named_scope("state"):
        s_in = sum_before(s_own)

    fb = 256
    quarter = n_seq // 4
    full_grad, hid, dpre, *ff_sums, gb_in = call(
        functools.partial(ff_kernel, n_head),
        hidden // fb,
        [
            smem(),
            smem(),
            *[whole(rows, share)] * n_head,
            whole(rows, model),
            whole(model, rows),
            pl.BlockSpec((model, fb), lambda i: (0, i)),
            pl.BlockSpec((1, fb), lambda i: (0, i)),
            pl.BlockSpec((fb, model), lambda i: (i, 0)),
        ],
        [
            whole(rows, model),
            pl.BlockSpec((rows, fb), lambda i: (0, i)),
            pl.BlockSpec((rows, fb), lambda i: (0, i)),
            *[whole(quarter, hidden // n_seq, model)] * 4,
            *[pl.BlockSpec((quarter, model // n_seq, fb), lambda i: (0, 0, i))] * 4,
            pl.BlockSpec((1, fb), lambda i: (0, i)),
        ],
        [
            sds((rows, model), bf16),
            sds((rows, hidden), bf16),
            sds((rows, hidden), bf16),
            *[sds((quarter, hidden // n_seq, model), bf16)] * 4,
            *[sds((quarter, model // n_seq, hidden), bf16)] * 4,
            sds((1, hidden), f32),
        ],
        [],
        8 * rows * model * hidden,
        6 * rows * model + 8 * model * hidden,
    )(me_head, me_seq, *grad_pieces, ln2, ln2t, w_in, b_in[None, :], w_down)

    s_in = after(s_in, hid)

    att, dq, dk, dv, gb, gzb, g_own, g_out = call(
        functools.partial(attn_kernel, head_size),
        blocks,
        [
            smem(),
            rows_of(BT, width),
            rows_of(BT, width),
            rows_of(BT, width),
            rows_of(BT, model),
            whole(width, model),
            rows_of(BT, 1),
            pl.BlockSpec((1, BT), lambda i: (0, i)),
            whole(*packet_shape),
        ],
        [
            rows_of(BT, width),
            rows_of(BT, width),
            rows_of(BT, width),
            rows_of(BT, width),
            rows_of(1, width, width),
            rows_of(1, 8, width),
            whole(*packet_shape),
            whole(model, width),
        ],
        [
            sds((rows, width), bf16),
            sds((rows, width), f32),
            sds((rows, width), f32),
            sds((rows, width), f32),
            sds((blocks, width, width), f32),
            sds((blocks, 8, width), f32),
            sds(packet_shape, f32),
            sds((model, width), bf16),
        ],
        [
            pltpu.VMEM((width, width), f32),
            pltpu.VMEM((8, width), f32),
            pltpu.VMEM((width, width), f32),
            pltpu.VMEM((8, width), f32),
            pltpu.VMEM((width, model), f32),
        ],
        24 * rows * heads * BT * width,
        rows * model * 2 + rows * width * 20,
    )(labels, qf, kf, v, full_grad, w_out, seg_col, seg_row, s_in)

    down = Sum("reduce_down", ff_sums[:4])
    seen = []
    with jax.named_scope("grad_state"):
        grad_in = neighbour_sum(g_own, -1, hid, seen.append)
    inn = Sum("reduce_in", [ff_sums[4], *after(tuple(ff_sums[5:]), *seen)])
    event = down.step(*seen)
    grad_in = after(grad_in, event)

    def back_rows(*shape):
        return pl.BlockSpec(shape, lambda i: (blocks - 1 - i,) + (0,) * (len(shape) - 1))

    part = model // n_seq
    low, small, *w_parts = call(
        functools.partial(tail_kernel, head_size),
        blocks,
        [
            smem(),
            *[back_rows(BT, width)] * 7,
            back_rows(1, width, width),
            back_rows(1, 8, width),
            whole(*packet_shape),
            back_rows(BT, 1),
            back_rows(BT, LANES),
            back_rows(BT, LANES),
            whole(1, width),
            whole(2, width, width),
            whole(model, rows),
            whole(model, width),
            smem(),
        ],
        [
            pl.BlockSpec((3, BT, width), lambda i: (0, blocks - 1 - i, 0)),
            whole(8, width),
            *[whole(quarter, 4, part, width)] * 4,
        ],
        [
            sds((3, rows, width), bf16),
            sds((8, width), f32),
            *[sds((quarter, 4, part, width), bf16)] * 4,
        ],
        [
            pltpu.VMEM((width, width), f32),
            pltpu.VMEM((8, width), f32),
            pltpu.VMEM((3, rows, width), bf16),
        ],
        2 * rows * model * 3 * width,
        rows * width * 30 + rows * model * 2 + 6 * model * width,
    )(labels, dq, dk, dv, q_expo, k_expo, kf, v, gb, gzb, grad_in, seg_col, cosine, sine, fw, tab, ln1t, g_out, me_seq)

    qkvo = Sum("reduce_attn", w_parts)
    event = low
    chunks = {"D": down, "I": inn, "C": qkvo}
    for name in BEFORE:
        event = chunks[name].step(event)

    stat_width = max(rows, model)
    val_keep, val_send, e_keep, e_send, stats = call(
        finish_kernel,
        blocks,
        [
            smem(),
            rows_of(BT, hidden),
            whole(hidden, model),
            rows_of(BT, width),
            whole(width, model),
            rows_of(BT, hidden),
            pl.BlockSpec((3, BT, width), lambda i: (0, i, 0)),
            whole(3, model, width),
            whole(model, hidden),
            rows_of(BT, model),
            whole(4, model),
        ],
        [
            *[pl.BlockSpec((n_head // 2, BT, share), lambda i: (0, i, 0))] * 4,
            whole(16, stat_width),
        ],
        [
            *[sds((n_head // 2, rows, share), bf16)] * 4,
            sds((16, stat_width), f32),
        ],
        [pltpu.VMEM((BT, model), bf16)],
        2 * rows * model * (3 * width + hidden),
        rows * width * 6 + rows * model * 6 + 8 * model * width + 2 * hidden * model,
    )(me_head, hid, w_down, att, w_out, dpre, after(low, event), w_qkv, w_in, xhat, gains)
    with jax.named_scope("mixed_sum"):
        mixed_share = scatter_sum(val_keep, after(val_send, low), "head")
    with jax.named_scope("e_sum"):
        e_share = scatter_sum(e_keep, e_send, "head")
    with jax.named_scope("stats_sum"):
        gains_own = stats[8:12, :model]
        stats = sum_all(stats[:8], "head")
    stats = stats[:2, :rows].T * (1.0 / model)

    bias = lax.dynamic_slice_in_dim(b_out, offset, share) + lax.dynamic_slice_in_dim(b_down, offset, share)
    mixed = (tokens.astype(f32) + mixed_share + bias).astype(bf16)
    xhat_share = lax.dynamic_slice_in_dim(xhat, offset, share, 1).astype(f32)
    grad_input = grad_out.astype(f32) + inv_std * (
        e_share - stats[:, 0:1] - xhat_share * stats[:, 1:2]
    )
    event = late = e_send
    for name in AFTER:
        chunk = chunks[name]
        if chunk.plan:
            pins = (mixed, grad_input) if len(chunk.plan) == 1 and name in PINNED else ()
            event = chunk.step(event, *pins)
        late = event if len(qkvo.plan) == LATE else late
    for chunk in chunks.values():
        while chunk.plan:
            event = chunk.step(event)
    g_down = block_out(down, me_seq)
    g_in = block_out(inn, me_seq)
    g_qkv, g_out = call(
        widen_kernel,
        4,
        [smem(), *[pl.BlockSpec((quarter, 1, part, width), lambda c: (0, c, 0, 0))] * 4],
        [
            pl.BlockSpec((1, model, width), lambda c: (jnp.minimum(c, 2), 0, 0)),
            whole(width, model),
        ],
        [sds((3, model, width), f32), sds((width, model), f32)],
        [pltpu.VMEM((model, width), f32)],
        0,
        END_COST * model * width,
    )(me_seq, *qkvo.arrays)

    with jax.named_scope("small_sum"):
        local = jnp.concatenate([small[:4], gb_in.reshape(-1, share), bias_out], 0)
        mine = (jnp.arange(n_head) == lax.axis_index("head")).astype(f32)
        spread_gains = gains_own.reshape(4, n_head, share).transpose(1, 0, 2)
        packet = jnp.concatenate([spread_gains, mine[:, None, None] * local[None]], 1)
        packet = jnp.broadcast_to(packet[None], (n_seq,) + packet.shape).reshape((-1,) + packet.shape[1:])
        packet = jnp.sum(lax.all_to_all(after(packet, late), ("seq", "head"), 0, 0, tiled=True), 0)
    gain_share, small, gb_in, bias_out = packet[:4], packet[4:8], packet[8:-1].reshape(-1), packet[-1]
    return (
        mixed,
        grad_input,
        gain_share[0],
        gain_share[1],
        gain_share[2],
        gain_share[3],
        g_qkv,
        small[:3],
        small[3].reshape(heads, feats),
        g_out,
        bias_out,
        g_in,
        gb_in,
        g_down,
        bias_out,
    )


def solution(mesh):
    in_specs = (
        P("seq", "head"),
        P(),
        P("seq"),
        P(),
        P(),
        P(),
        P(),
        P(None, None, "head"),
        P(None, "head"),
        P("head", None),
        P("head", None),
        P(),
        P(None, "head"),
        P("head"),
        P("head", None),
        P(),
        P("seq", "head"),
    )
    out_specs = (
        P("seq", "head"),
        P("seq", "head"),
        P("head"),
        P("head"),
        P("head"),
        P("head"),
        P(None, None, "head"),
        P(None, "head"),
        P("head", None),
        P("head", None),
        P("head"),
        P(None, "head"),
        P("head"),
        P("head", None),
        P("head"),
    )
    return jax.shard_map(body, mesh=mesh, in_specs=in_specs, out_specs=out_specs, check_vma=False)
```

```python
import functools
import math
from statistics import NormalDist

import jax
import jax.numpy as jnp
import numpy as np
from jax import lax
from jax.experimental import pallas as pl
from jax.experimental.pallas import tpu as pltpu
from jax.sharding import PartitionSpec as P

ROT = 16
eps_norm = 1e-05
rope_base = 10000.0
feature_scale = 0.5
BT = 512
LANES = 128
bf16 = jnp.bfloat16
f32 = jnp.float32
COST_SCALE = 1.0
END_COST = 12
BEFORE = "DI"
AFTER = "DCICIDCIC"
PINNED = "C"
LATE = 3
VMEM_LIMIT = 56 * 1024 * 1024


def nn(a, b):
    return lax.dot_general(a, b, (((1,), (0,)), ((), ())), preferred_element_type=f32)


def nt(a, b):
    return lax.dot_general(a, b, (((1,), (1,)), ((), ())), preferred_element_type=f32)


def tn(a, b):
    return lax.dot_general(a, b, (((0,), (0,)), ((), ())), preferred_element_type=f32)


def split(x):
    hi = x.astype(bf16)
    return hi, (x - hi.astype(f32)).astype(bf16)


def feature_table(feat_count, head_size):
    rows = np.arange(feat_count)
    cols = np.arange(head_size)
    cosines = np.cos(math.pi * (cols[None, :] + 0.5) * rows[:, None] / head_size)
    scaling = np.where(rows == 0, math.sqrt(1.0 / head_size), math.sqrt(2.0 / head_size))
    points = np.array([NormalDist().inv_cdf((r + 0.5) / feat_count) for r in range(feat_count)])
    return feature_scale * (points * scaling)[:, None] * cosines


def lane_head(shape, head_size):
    return lax.broadcasted_iota(jnp.int32, shape, len(shape) - 1) // head_size


def block_ones(size, head_size):
    rows = lax.broadcasted_iota(jnp.int32, (size, size), 0) // head_size
    cols = lax.broadcasted_iota(jnp.int32, (size, size), 1) // head_size
    return rows == cols


def swap_halves(x, head_size):
    width = x.shape[1]
    lane = lax.broadcasted_iota(jnp.int32, x.shape, 1) % head_size
    ahead = pltpu.roll(x, width - ROT // 2, 1)
    behind = pltpu.roll(x, ROT // 2, 1)
    return jnp.where(lane < ROT // 2, ahead, behind)


def widen(table, width):
    return table if table.shape[1] == width else jnp.concatenate([table] * (width // table.shape[1]), 1)


def pack_state(state, norm, head_size):
    size = state.shape[0]
    masked = jnp.where(block_ones(size, head_size), state, 0.0)
    packed = masked[:head_size]
    for h in range(1, size // head_size):
        packed = packed + masked[h * head_size : (h + 1) * head_size]
    return packed, norm


def unpack_state(packed, head_size):
    size = packed.shape[1]
    rows = jnp.concatenate([packed[:head_size]] * (size // head_size), 0)
    return jnp.where(block_ones(size, head_size), rows, 0.0)


def place(full_ref, piece_refs, me_ref):
    for k, ref in enumerate(piece_refs):
        size = ref.shape[1]
        start = pl.multiple_of((me_ref[0] ^ k) * size, LANES)
        full_ref[:, pl.ds(start, size)] = ref[...]


def pre_kernel(
    head_size,
    pieces,
    labels_ref,
    me_ref,
    *refs,
):
    x_refs = refs[:pieces]
    (
        gains_ref,
        w_ref,
        bq_ref,
        fw_ref,
        tab_ref,
        cos_ref,
        sin_ref,
        valid_ref,
        seg_ref,
        ln1t_ref,
        ln2_ref,
        ln2t_ref,
        xhat_ref,
        inv_ref,
        qe_ref,
        ke_ref,
        qf_ref,
        kf_ref,
        v_ref,
        pk_ref,
        full_ref,
        state_ref,
        norm_ref,
    ) = refs[pieces:]
    step = pl.program_id(0)
    width = qe_ref.shape[1]
    place(full_ref, x_refs, me_ref)
    x = full_ref[...].astype(f32)
    centered = x - jnp.mean(x, -1, keepdims=True)
    inv = lax.rsqrt(jnp.mean(centered * centered, -1, keepdims=True) + eps_norm)
    xhat = centered * inv
    inv_ref[...] = inv
    xhat_ref[...] = xhat.astype(bf16)
    ln1 = (xhat * gains_ref[0:1] + gains_ref[1:2]).astype(bf16)
    ln2 = (xhat * gains_ref[2:3] + gains_ref[3:4]).astype(bf16)
    ln2_ref[...] = ln2
    ln1t_ref[...] = ln1.T
    ln2t_ref[...] = ln2.T
    cosine = widen(cos_ref[...], width)
    sine = widen(sin_ref[...], width)

    def features(c):
        raw = nn(ln1, w_ref[c]) + bq_ref[c : c + 1]
        turned = raw * cosine + swap_halves(raw, head_size) * sine
        hi, lo = split(turned)
        return jnp.exp(nn(hi, tab_ref[0]) + nn(lo, tab_ref[0]) + nn(hi, tab_ref[1]))

    fw = fw_ref[...]
    qe = features(0)
    ke = features(1) * valid_ref[...]
    qe_ref[...] = qe
    ke_ref[...] = ke
    qf_ref[...] = (fw * qe).astype(bf16)
    kf = (fw * ke).astype(bf16)
    kf_ref[...] = kf
    v = (nn(ln1, w_ref[2]) + bq_ref[2:3]).astype(bf16)
    v_ref[...] = v

    @pl.when(step == 0)
    def _():
        state_ref[...] = jnp.zeros_like(state_ref)
        norm_ref[...] = jnp.zeros_like(norm_ref)

    tail = kf.astype(f32) * (seg_ref[...] == labels_ref[pl.num_programs(0) - 1, 1]).astype(f32)
    state_ref[...] += tn(tail.astype(bf16), v)
    norm_ref[...] += jnp.broadcast_to(jnp.sum(tail, 0, keepdims=True), norm_ref.shape)

    @pl.when(step == pl.num_programs(0) - 1)
    def _():
        packed, norm = pack_state(state_ref[...], norm_ref[...], head_size)
        for i in range(pk_ref.shape[0]):
            pk_ref[i, :head_size] = packed
            pk_ref[i, head_size:] = norm


def slot_of(relative, count):
    place = 0
    mask = 4
    while mask < count:
        place = 2 * place + (relative // mask) % 2
        mask *= 2
    return place


def store_blocks(block, base, me, refs, part, rest=()):
    count = 4 * refs[0].shape[0]
    for low in range(4):

        @pl.when(me % 4 == low)
        def _():
            for j in range(block.shape[0] // part):
                ref = refs[(low ^ (base + j)) % 4]
                ref[(slot_of(me ^ (base + j), count),) + rest] = block[j * part : (j + 1) * part]


def ff_kernel(pieces, me_ref, rank_ref, *refs):
    grad_refs = refs[:pieces]
    (
        ln2_ref,
        ln2t_ref,
        win_ref,
        bin_ref,
        wdown_ref,
        grad_ref,
        hid_ref,
        dpre_ref,
        *sum_refs,
        gb_ref,
    ) = refs[pieces:]

    @pl.when(pl.program_id(0) == 0)
    def _():
        place(grad_ref, grad_refs, me_ref)

    chunk = ln2_ref.shape[0] // 4
    sums = jnp.zeros((1, win_ref.shape[1]), f32)
    for r in range(4):
        part = slice(r * chunk, (r + 1) * chunk)
        pre = nn(ln2_ref[part], win_ref[...]) + bin_ref[...]
        phi_cum = 0.5 + 0.5 * lax.erf(pre * (1.0 / math.sqrt(2.0)))
        hid_ref[part] = (pre * phi_cum).astype(bf16)
        slope = phi_cum + pre * jnp.exp(-0.5 * pre * pre) * (1.0 / math.sqrt(2.0 * math.pi))
        dpre = nt(grad_ref[part], wdown_ref[...]) * slope
        sums = sums + jnp.sum(dpre, 0, keepdims=True)
        dpre_ref[part] = dpre.astype(bf16)
    gb_ref[...] = sums
    me = rank_ref[0]
    g_down = tn(hid_ref[...], grad_ref[...]).astype(bf16)
    part = sum_refs[0].shape[1]
    steps = 4 * sum_refs[0].shape[0] * part // g_down.shape[0]
    for step in range(steps):

        @pl.when(pl.program_id(0) == step)
        def _():
            store_blocks(g_down, step * (g_down.shape[0] // part), me, sum_refs[:4], part)

    g_in = nn(ln2t_ref[...], dpre_ref[...]).astype(bf16)
    store_blocks(g_in, 0, me, sum_refs[4:], sum_refs[4].shape[1])


def block_out_kernel(rank_ref, *refs):
    out_ref = refs[4]
    part = refs[0].shape[1]
    for low in range(4):

        @pl.when(rank_ref[0] % 4 == low)
        def _():
            for j in range(4):
                out_ref[j * part : (j + 1) * part] = refs[low ^ j][0].astype(f32)


def attn_kernel(
    head_size,
    labels_ref,
    qf_ref,
    kf_ref,
    v_ref,
    grad_ref,
    wout_ref,
    segc_ref,
    segr_ref,
    spk_ref,
    att_ref,
    dq_ref,
    dk_ref,
    dv_ref,
    gb_ref,
    gzb_ref,
    gpk_ref,
    gout_ref,
    state_ref,
    norm_ref,
    lead_ref,
    leadz_ref,
    acc_ref,
):
    step = pl.program_id(0)
    last = pl.num_programs(0) - 1
    rows, width = qf_ref.shape
    heads = width // head_size
    same = block_ones(width, head_size)
    ones = same.astype(f32).astype(bf16)

    def head_sum(x):
        hi, lo = split(x)
        return nn(hi, ones) + nn(lo, ones)

    @pl.when(step == 0)
    def _():
        state_ref[...] = unpack_state(spk_ref[...], head_size)
        norm_ref[...] = spk_ref[head_size : head_size + 8]
        lead_ref[...] = jnp.zeros_like(lead_ref)
        leadz_ref[...] = jnp.zeros_like(leadz_ref)
        acc_ref[...] = jnp.zeros_like(acc_ref)

    seg = segc_ref[...]
    enters = (seg == labels_ref[step, 0]).astype(f32)
    tail = (seg == labels_ref[step, 1]).astype(f32)
    lead = (seg == labels_ref[0, 2]).astype(f32)
    linked = (labels_ref[step, 0] == labels_ref[step, 1]).astype(f32)
    qf = qf_ref[...]
    kf = kf_ref[...]
    v = v_ref[...]
    qf32 = qf.astype(f32)
    norm = norm_ref[0:1]
    lane = lane_head((rows, width), head_size)
    zero16 = jnp.zeros((rows, width), bf16)

    def stack(x):
        return jnp.concatenate([jnp.where(lane == h, x, zero16) for h in range(heads)], 0)

    def unstack(x):
        total = jnp.where(lane == 0, x[:rows], 0.0)
        for h in range(1, heads):
            total = jnp.where(lane == h, x[h * rows : (h + 1) * rows], total)
        return total

    causal = lax.broadcasted_iota(jnp.int32, (rows, rows), 0) >= lax.broadcasted_iota(
        jnp.int32, (rows, rows), 1
    )
    joined = causal & (seg == segr_ref[...])
    joined_all = jnp.concatenate([joined.astype(f32)] * heads, 0)
    q_stack = stack(qf)
    scores = (nt(q_stack, kf) * joined_all).astype(bf16)
    ones_v = jnp.ones((rows, LANES), bf16)
    sums = nn(scores, ones_v)
    den_in = jnp.where(lane == 0, widen(sums[:rows], width), 0.0)
    for h in range(1, heads):
        den_in = jnp.where(lane == h, widen(sums[h * rows : (h + 1) * rows], width), den_in)
    s_hi, s_lo = split(state_ref[...])
    num = unstack(nn(scores, v)) + enters * (nn(qf, s_hi) + nn(qf, s_lo))
    den = den_in + enters * head_sum(qf32 * norm)
    inv_den = 1.0 / den
    att = num * inv_den
    att_low = att.astype(bf16)
    att_ref[...] = att_low
    acc_ref[...] += tn(att_low, grad_ref[...])
    d_att = nt(grad_ref[...], wout_ref[...])
    d_num = d_att * inv_den
    d_den = -head_sum(d_att * att) * inv_den
    dn_hi, dn_lo = split(d_num)
    dn_stack = stack(dn_hi)
    dden_all = jnp.concatenate([d_den[:, h * head_size : h * head_size + 1] for h in range(heads)], 0)
    d_scores = ((nt(dn_stack, v) + dden_all) * joined_all).astype(bf16)
    inter = nt(dn_hi, s_hi) + nt(dn_lo, s_hi) + nt(dn_hi, s_lo) + d_den * norm
    dq_ref[...] = unstack(nn(d_scores, kf)) + enters * inter
    dk_ref[...] = tn(d_scores, q_stack)
    dv_ref[...] = tn(scores, dn_stack)
    q_in = (qf32 * enters).astype(bf16)
    gb_ref[0] = jnp.where(same, tn(q_in, dn_hi) + tn(q_in, dn_lo), 0.0)
    weighted = qf32 * d_den
    gzb_ref[0] = jnp.broadcast_to(jnp.sum(weighted * enters, 0, keepdims=True), (8, width))
    q_lead = (qf32 * lead).astype(bf16)
    lead_ref[...] += tn(q_lead, dn_hi) + tn(q_lead, dn_lo)
    leadz_ref[...] += jnp.broadcast_to(jnp.sum(weighted * lead, 0, keepdims=True), (8, width))
    k_tail = kf.astype(f32) * tail
    state_ref[...] = linked * state_ref[...] + jnp.where(same, tn(k_tail.astype(bf16), v), 0.0)
    norm_ref[...] = linked * norm_ref[...] + jnp.broadcast_to(jnp.sum(k_tail, 0, keepdims=True), (8, width))

    @pl.when(step == last)
    def _():
        packed, z = pack_state(lead_ref[...], leadz_ref[...], head_size)
        gpk_ref[:head_size] = packed
        gpk_ref[head_size:] = z
        gout_ref[...] = acc_ref[...].T.astype(bf16)


def spread(full, keep_ref, send_ref, scratch_ref, me_ref):
    scratch_ref[...] = full.astype(bf16)
    size = keep_ref.shape[2]
    for k in range(2 * keep_ref.shape[0]):
        start = pl.multiple_of((me_ref[0] ^ k) * size, LANES)
        (send_ref if k % 2 else keep_ref)[k // 2] = scratch_ref[:, pl.ds(start, size)]


def tail_kernel(
    head_size,
    labels_ref,
    dq_ref,
    dk_ref,
    dv_ref,
    qe_ref,
    ke_ref,
    kf_ref,
    v_ref,
    gb_ref,
    gzb_ref,
    gin_ref,
    segc_ref,
    cos_ref,
    sin_ref,
    fw_ref,
    tab_ref,
    ln1t_ref,
    gout_ref,
    rank_ref,
    low_ref,
    small_ref,
    sum0_ref,
    sum1_ref,
    sum2_ref,
    sum3_ref,
    state_ref,
    norm_ref,
    all_ref,
):
    step = pl.program_id(0)
    last = pl.num_programs(0) - 1
    block = last - step
    rows, width = dq_ref.shape

    @pl.when(step == 0)
    def _():
        state_ref[...] = unpack_state(gin_ref[...], head_size)
        norm_ref[...] = gin_ref[head_size : head_size + 8]
        small_ref[...] = jnp.zeros_like(small_ref)

    tail = (segc_ref[...] == labels_ref[block, 1]).astype(f32)
    linked = (labels_ref[block, 0] == labels_ref[block, 1]).astype(f32)
    g_hi, g_lo = split(state_ref[...])
    v = v_ref[...]
    kf = kf_ref[...]
    dk = dk_ref[...] + tail * (nt(v, g_hi) + nt(v, g_lo) + norm_ref[0:1])
    dv = dv_ref[...] + tail * (nn(kf, g_hi) + nn(kf, g_lo))
    state_ref[...] = linked * state_ref[...] + gb_ref[0]
    norm_ref[...] = linked * norm_ref[...] + gzb_ref[0]
    fw = fw_ref[...]
    gq = dq_ref[...] * qe_ref[...]
    gk = dk * ke_ref[...]
    cosine = widen(cos_ref[...], width)
    sine = widen(sin_ref[...], width)

    def back(g):
        hi, lo = split(g * fw)
        turned = nt(hi, tab_ref[0]) + nt(lo, tab_ref[0]) + nt(hi, tab_ref[1])
        return turned * cosine - swap_halves(turned, head_size) * sine

    dq_raw = back(gq)
    dk_raw = back(gk)
    small_ref[0:1] += jnp.sum(dq_raw, 0, keepdims=True)
    small_ref[1:2] += jnp.sum(dk_raw, 0, keepdims=True)
    small_ref[2:3] += jnp.sum(dv, 0, keepdims=True)
    small_ref[3:4] += jnp.sum(gq + gk, 0, keepdims=True)
    start = pl.multiple_of(block * rows, rows)
    for c, d in enumerate((dq_raw, dk_raw, dv)):
        low = d.astype(bf16)
        low_ref[c] = low
        all_ref[c, pl.ds(start, rows)] = low

    @pl.when(step == last)
    def _():
        me = rank_ref[0]
        part = sum0_ref.shape[2]
        for c in range(4):
            g = gout_ref[...] if c == 3 else nn(ln1t_ref[...], all_ref[c]).astype(bf16)

            store_blocks(g, 0, me, (sum0_ref, sum1_ref, sum2_ref, sum3_ref), part, (c,))


def finish_kernel(
    me_ref,
    hid_ref,
    wdown_ref,
    att_ref,
    wout_ref,
    dpre_ref,
    low_ref,
    w_ref,
    win_ref,
    xhat_ref,
    gains_ref,
    val_keep_ref,
    val_send_ref,
    keep_ref,
    send_ref,
    stat_ref,
    scratch_ref,
):
    value = nn(hid_ref[...], wdown_ref[...]) + nn(att_ref[...], wout_ref[...])
    spread(value, val_keep_ref, val_send_ref, scratch_ref, me_ref)
    step = pl.program_id(0)
    rows, model = xhat_ref.shape

    @pl.when(step == 0)
    def _():
        stat_ref[8:16] = jnp.zeros((8, stat_ref.shape[1]), f32)

    d_ln1 = nt(low_ref[0], w_ref[0]) + nt(low_ref[1], w_ref[1]) + nt(low_ref[2], w_ref[2])
    d_ln2 = nt(dpre_ref[...], win_ref[...])
    xhat = xhat_ref[...].astype(f32)
    e = d_ln1 * gains_ref[0:1] + d_ln2 * gains_ref[2:3]
    spread(e, keep_ref, send_ref, scratch_ref, me_ref)
    ones = jnp.ones((8, model), bf16)
    hi, lo = split(e)
    sum_e = nt(ones, hi) + nt(ones, lo)
    hi, lo = split(e * xhat)
    sum_ex = nt(ones, hi) + nt(ones, lo)
    row = lax.broadcasted_iota(jnp.int32, sum_e.shape, 0)
    start = pl.multiple_of(step * rows, rows)
    stat_ref[0:8, pl.ds(start, rows)] = jnp.where(row == 0, sum_e, sum_ex)
    stat_ref[8:9, :model] += jnp.sum(d_ln1 * xhat, 0, keepdims=True)
    stat_ref[9:10, :model] += jnp.sum(d_ln1, 0, keepdims=True)
    stat_ref[10:11, :model] += jnp.sum(d_ln2 * xhat, 0, keepdims=True)
    stat_ref[11:12, :model] += jnp.sum(d_ln2, 0, keepdims=True)


def widen_kernel(rank_ref, *refs):
    qkv_ref, out_ref, scratch_ref = refs[4:]
    c = pl.program_id(0)
    quarter, _, part, _ = refs[0].shape
    me = rank_ref[0]
    for low in range(4):

        @pl.when(me % 4 == low)
        def _():
            for j in range(4 * quarter):
                slot = slot_of(me ^ j, 4 * quarter)
                scratch_ref[j * part : (j + 1) * part] = refs[(low ^ j) % 4][slot, 0].astype(f32)

    @pl.when(c < 3)
    def _():
        qkv_ref[0] = scratch_ref[...]

    @pl.when(c == 3)
    def _():
        out_ref[...] = scratch_ref[...].T


def whole(*shape):
    return pl.BlockSpec(shape, lambda *_: (0,) * len(shape))


def rows_of(*shape):
    return pl.BlockSpec(shape, lambda i: (i,) + (0,) * (len(shape) - 1))


def smem():
    return pl.BlockSpec(memory_space=pltpu.SMEM)


def sds(shape, dtype):
    return jax.ShapeDtypeStruct(shape, dtype)


def call(kernel, grid, in_specs, out_specs, out_shape, scratch, flops, moved, aliases={}):
    return pl.pallas_call(
        kernel,
        grid=(grid,),
        in_specs=in_specs,
        out_specs=out_specs,
        out_shape=out_shape,
        scratch_shapes=scratch,
        input_output_aliases=aliases,
        compiler_params=pltpu.CompilerParams(vmem_limit_bytes=VMEM_LIMIT),
        cost_estimate=pl.CostEstimate(
            flops=int(flops * COST_SCALE), bytes_accessed=int(moved * COST_SCALE), transcendentals=0
        ),
        name=getattr(kernel, "func", kernel).__name__,
    )


def exchange(x, axis, mask):
    count = lax.axis_size(axis)
    return lax.ppermute(x, axis, [(i, i ^ mask) for i in range(count)])


def gather_far(x, axis):
    pieces = {0: x}
    mask = lax.axis_size(axis) // 2
    while mask > 1:
        pieces.update({k ^ mask: exchange(p, axis, mask) for k, p in sorted(pieces.items())})
        mask //= 2
    return pieces


def gather_near(pieces, axis):
    pieces = pieces | {k ^ 1: exchange(p, axis, 1) for k, p in sorted(pieces.items())}
    return [pieces[k] for k in sorted(pieces)]


def scatter_sum(keep, send, axis):
    mask = 1
    while True:
        got = exchange(send, axis, mask)
        if keep.shape[0] == 1:
            return keep[0].astype(f32) + got[0].astype(f32)
        total_keep = keep[0::2].astype(f32) + got[0::2].astype(f32)
        total_send = keep[1::2].astype(f32) + got[1::2].astype(f32)
        keep, send = total_keep.astype(bf16), total_send.astype(bf16)
        mask *= 2


def sum_all(x, axis):
    mask = 1
    while mask < lax.axis_size(axis):
        x = x + exchange(x, axis, mask)
        mask *= 2
    return x


class Sum:
    def __init__(self, name, arrays):
        self.name, self.arrays = name, list(arrays)
        masks = []
        while 4 * 2 ** len(masks) < lax.axis_size("seq"):
            masks.append(4 * 2 ** len(masks))
        self.plan = [("group", 0)] + [("reduce", m) for m in masks]
        self.plan += [("gather", m) for m in masks[::-1]] + [("spread", 0)]

    def halves(self, terms):
        half = terms[0].shape[0] // 2

        def total(part):
            return sum(t[part].astype(f32) for t in terms).astype(bf16)

        if half:
            self.keep, self.send = total(slice(0, half)), total(slice(half, None))
        else:
            self.keep = self.send = total(slice(None))
        return self.send

    def step(self, *pins):
        kind, mask = self.plan.pop(0)
        with jax.named_scope(self.name):
            if kind == "group":
                got = after(tuple(exchange(self.arrays[g], "seq", g) for g in (1, 2, 3)), *pins)
                return self.halves([self.arrays[0], *got])
            if kind == "reduce":
                return self.halves([self.keep, after(exchange(self.send, "seq", mask), *pins)])
            if kind == "gather":
                self.keep = jnp.concatenate([self.keep, after(exchange(self.keep, "seq", mask), *pins)])
                return self.keep
            self.arrays = [self.keep, *after(tuple(exchange(self.keep, "seq", g) for g in (1, 2, 3)), *pins)]
            return self.arrays[1]


def block_out(chunk, me_seq):
    quarter, part, width = chunk.keep.shape
    block = pl.BlockSpec((1, part, width), lambda i, me: (slot_of(((me[0] // 4) ^ i) * 4, 4 * quarter), 0, 0))
    return pl.pallas_call(
        block_out_kernel,
        grid_spec=pltpu.PrefetchScalarGridSpec(
            num_scalar_prefetch=1,
            grid=(quarter,),
            in_specs=[block] * 4,
            out_specs=pl.BlockSpec((4 * part, width), lambda i, me: (i, 0)),
        ),
        out_shape=sds((4 * quarter * part, width), f32),
        compiler_params=pltpu.CompilerParams(vmem_limit_bytes=VMEM_LIMIT),
        cost_estimate=pl.CostEstimate(flops=0, bytes_accessed=24 * quarter * part * width, transcendentals=0),
        name="block_out_kernel",
    )(me_seq, *chunk.arrays)


def sum_before(copies):
    count = lax.axis_size("seq")
    packets = lax.all_to_all(copies, "seq", 0, 0, tiled=True)
    wanted = (jnp.arange(count) < lax.axis_index("seq")).astype(f32)
    return jnp.sum(packets * wanted[:, None, None], 0)


def after(x, *others):
    return lax.optimization_barrier((x,) + others)[0]


def neighbour_sum(packet, sign, pin, event):
    count = lax.axis_size("seq")
    outer = 4 if count % 4 == 0 else 1
    inner = count // outer
    me = lax.axis_index("seq")
    mine = me % inner
    group = packet
    before = jnp.zeros_like(packet)
    for k in range(1, inner):
        route = [(i, i - i % inner + (i % inner + k) % inner) for i in range(count)]
        got = after(lax.ppermute(packet, "seq", route), pin)
        event(got)
        sender = (mine - k) % inner
        group = group + got
        before = before + jnp.where((sender < mine) if sign > 0 else (sender > mine), got, 0.0)
    for k in range(1, outer):
        shift = sign * k * inner
        route = [(i, i + shift) for i in range(count) if 0 <= i + shift < count]
        before = before + lax.ppermute(group, "seq", route)
    return before


def body(
    tokens,
    lengths,
    pad_mask,
    ln1_gain,
    ln1_bias,
    ln2_gain,
    ln2_bias,
    w_qkv,
    b_qkv,
    feat_weight,
    w_out,
    b_out,
    w_in,
    b_in,
    w_down,
    b_down,
    grad_out,
):
    rows, share = tokens.shape
    heads, feats = feat_weight.shape
    width = w_qkv.shape[2]
    head_size = width // heads
    model, hidden = w_in.shape
    blocks = rows // BT
    n_head = lax.axis_size("head")
    offset = lax.axis_index("head") * share
    with jax.named_scope("gather_tokens"):
        token_far = gather_far(tokens, "head")
    me_head = jnp.reshape(lax.axis_index("head"), (1,)).astype(jnp.int32)
    me_seq = jnp.reshape(lax.axis_index("seq"), (1,)).astype(jnp.int32)
    n_seq = lax.axis_size("seq")

    index_all = lax.axis_index("seq") * rows + jnp.arange(rows, dtype=jnp.int32)
    seq_ends = jnp.cumsum(lengths).astype(jnp.int32)
    starts = seq_ends - lengths

    def seg_of(index):
        return jnp.sum((index[:, None] >= seq_ends[None, :]).astype(jnp.int32), 1)

    segment = seg_of(index_all)
    picked = segment[:, None] == jnp.arange(lengths.shape[0])[None, :]
    position = index_all - jnp.sum(jnp.where(picked, starts[None, :], 0), 1)
    base = lax.axis_index("seq") * rows + jnp.arange(blocks, dtype=jnp.int32) * BT
    label_in = seg_of(jnp.maximum(base - 1, 0))
    label_last = seg_of(base + (BT - 1))
    label_first = jnp.broadcast_to(segment[0], (blocks,))
    labels = jnp.stack([label_in, label_last, label_first], 1)
    seg_col = segment[:, None]
    seg_row = segment[None, :]
    lane = np.arange(LANES) % head_size
    inverse = np.where(lane < ROT, rope_base ** (-2.0 * (lane % (ROT // 2)) / ROT), 0.0)
    angles = position.astype(f32)[:, None] * jnp.asarray(inverse, f32)[None, :]
    sign = np.where(lane < ROT // 2, -1.0, np.where(lane < ROT, 1.0, 0.0))
    cosine = jnp.cos(angles)
    sine = jnp.sin(angles) * jnp.asarray(sign, f32)[None, :]
    valid = pad_mask.astype(f32)[:, None]
    table = np.kron(np.eye(heads), feature_table(feats, head_size).T).astype(np.float32)
    table_hi = table.astype(bf16)
    table_lo = (table - table_hi.astype(np.float32)).astype(bf16)
    tab = jnp.asarray(np.stack([table_hi, table_lo]))
    gains = jnp.stack([ln1_gain, ln1_bias, ln2_gain, ln2_bias])
    fw = feat_weight.reshape(1, width)
    bias_out = jnp.sum(grad_out.astype(f32), 0, keepdims=True)
    with jax.named_scope("gather_grads"):
        early = (cosine, sine, gains, bias_out, labels, valid, seg_col, seg_row, fw)
        grad_far = gather_far(after(grad_out, *early), "head")
    with jax.named_scope("gather_tokens"):
        token_pieces = gather_near({k: after(p, *early) if k else p for k, p in token_far.items()}, "head")
    packet_shape = (head_size + 8, width)

    ln1t, ln2, ln2t, xhat, inv_std, q_expo, k_expo, qf, kf, v, s_own = call(
        functools.partial(pre_kernel, head_size, n_head),
        blocks,
        [
            smem(),
            smem(),
            *[rows_of(BT, share)] * n_head,
            whole(4, model),
            whole(3, model, width),
            whole(3, width),
            whole(1, width),
            whole(2, width, width),
            rows_of(BT, LANES),
            rows_of(BT, LANES),
            rows_of(BT, 1),
            rows_of(BT, 1),
        ],
        [
            pl.BlockSpec((model, BT), lambda i: (0, i)),
            rows_of(BT, model),
            pl.BlockSpec((model, BT), lambda i: (0, i)),
            rows_of(BT, model),
            rows_of(BT, 1),
            rows_of(BT, width),
            rows_of(BT, width),
            rows_of(BT, width),
            rows_of(BT, width),
            rows_of(BT, width),
            whole(n_seq, *packet_shape),
        ],
        [
            sds((model, rows), bf16),
            sds((rows, model), bf16),
            sds((model, rows), bf16),
            sds((rows, model), bf16),
            sds((rows, 1), f32),
            sds((rows, width), f32),
            sds((rows, width), f32),
            sds((rows, width), bf16),
            sds((rows, width), bf16),
            sds((rows, width), bf16),
            sds((n_seq,) + packet_shape, f32),
        ],
        [pltpu.VMEM((BT, model), bf16), pltpu.VMEM((width, width), f32), pltpu.VMEM((8, width), f32)],
        2 * rows * model * 3 * width + 16 * rows * width * width,
        rows * model * 10 + 6 * model * width,
    )(labels, me_head, *token_pieces, gains, w_qkv, b_qkv, fw, tab, cosine, sine, valid, seg_col)

    with jax.named_scope("gather_grads"):
        grad_pieces = gather_near({k: after(p, s_own) for k, p in grad_far.items()}, "head")
    with jax.named_scope("state"):
        s_in = sum_before(s_own)

    fb = 512
    quarter = n_seq // 4
    full_grad, hid, dpre, *ff_sums, gb_in = call(
        functools.partial(ff_kernel, n_head),
        hidden // fb,
        [
            smem(),
            smem(),
            *[whole(rows, share)] * n_head,
            whole(rows, model),
            whole(model, rows),
            pl.BlockSpec((model, fb), lambda i: (0, i)),
            pl.BlockSpec((1, fb), lambda i: (0, i)),
            pl.BlockSpec((fb, model), lambda i: (i, 0)),
        ],
        [
            whole(rows, model),
            pl.BlockSpec((rows, fb), lambda i: (0, i)),
            pl.BlockSpec((rows, fb), lambda i: (0, i)),
            *[whole(quarter, hidden // n_seq, model)] * 4,
            *[pl.BlockSpec((quarter, model // n_seq, fb), lambda i: (0, 0, i))] * 4,
            pl.BlockSpec((1, fb), lambda i: (0, i)),
        ],
        [
            sds((rows, model), bf16),
            sds((rows, hidden), bf16),
            sds((rows, hidden), bf16),
            *[sds((quarter, hidden // n_seq, model), bf16)] * 4,
            *[sds((quarter, model // n_seq, hidden), bf16)] * 4,
            sds((1, hidden), f32),
        ],
        [],
        8 * rows * model * hidden,
        6 * rows * model + 8 * model * hidden,
    )(me_head, me_seq, *grad_pieces, ln2, ln2t, w_in, b_in[None, :], w_down)

    s_in = after(s_in, hid)

    att, dq, dk, dv, gb, gzb, g_own, g_out = call(
        functools.partial(attn_kernel, head_size),
        blocks,
        [
            smem(),
            rows_of(BT, width),
            rows_of(BT, width),
            rows_of(BT, width),
            rows_of(BT, model),
            whole(width, model),
            rows_of(BT, 1),
            pl.BlockSpec((1, BT), lambda i: (0, i)),
            whole(*packet_shape),
        ],
        [
            rows_of(BT, width),
            rows_of(BT, width),
            rows_of(BT, width),
            rows_of(BT, width),
            rows_of(1, width, width),
            rows_of(1, 8, width),
            whole(*packet_shape),
            whole(model, width),
        ],
        [
            sds((rows, width), bf16),
            sds((rows, width), f32),
            sds((rows, width), f32),
            sds((rows, width), f32),
            sds((blocks, width, width), f32),
            sds((blocks, 8, width), f32),
            sds(packet_shape, f32),
            sds((model, width), bf16),
        ],
        [
            pltpu.VMEM((width, width), f32),
            pltpu.VMEM((8, width), f32),
            pltpu.VMEM((width, width), f32),
            pltpu.VMEM((8, width), f32),
            pltpu.VMEM((width, model), f32),
        ],
        24 * rows * heads * BT * width,
        rows * model * 2 + rows * width * 20,
    )(labels, qf, kf, v, full_grad, w_out, seg_col, seg_row, s_in)

    down = Sum("reduce_down", ff_sums[:4])
    seen = []
    with jax.named_scope("grad_state"):
        grad_in = neighbour_sum(g_own, -1, hid, seen.append)
    inn = Sum("reduce_in", [ff_sums[4], *after(tuple(ff_sums[5:]), *seen)])
    event = down.step(*seen)
    grad_in = after(grad_in, event)

    def back_rows(*shape):
        return pl.BlockSpec(shape, lambda i: (blocks - 1 - i,) + (0,) * (len(shape) - 1))

    part = model // n_seq
    low, small, *w_parts = call(
        functools.partial(tail_kernel, head_size),
        blocks,
        [
            smem(),
            *[back_rows(BT, width)] * 7,
            back_rows(1, width, width),
            back_rows(1, 8, width),
            whole(*packet_shape),
            back_rows(BT, 1),
            back_rows(BT, LANES),
            back_rows(BT, LANES),
            whole(1, width),
            whole(2, width, width),
            whole(model, rows),
            whole(model, width),
            smem(),
        ],
        [
            pl.BlockSpec((3, BT, width), lambda i: (0, blocks - 1 - i, 0)),
            whole(8, width),
            *[whole(quarter, 4, part, width)] * 4,
        ],
        [
            sds((3, rows, width), bf16),
            sds((8, width), f32),
            *[sds((quarter, 4, part, width), bf16)] * 4,
        ],
        [
            pltpu.VMEM((width, width), f32),
            pltpu.VMEM((8, width), f32),
            pltpu.VMEM((3, rows, width), bf16),
        ],
        2 * rows * model * 3 * width,
        rows * width * 30 + rows * model * 2 + 6 * model * width,
    )(labels, dq, dk, dv, q_expo, k_expo, kf, v, gb, gzb, grad_in, seg_col, cosine, sine, fw, tab, ln1t, g_out, me_seq)

    qkvo = Sum("reduce_attn", w_parts)
    event = low
    chunks = {"D": down, "I": inn, "C": qkvo}
    for name in BEFORE:
        event = chunks[name].step(event)

    stat_width = max(rows, model)
    val_keep, val_send, e_keep, e_send, stats = call(
        finish_kernel,
        blocks,
        [
            smem(),
            rows_of(BT, hidden),
            whole(hidden, model),
            rows_of(BT, width),
            whole(width, model),
            rows_of(BT, hidden),
            pl.BlockSpec((3, BT, width), lambda i: (0, i, 0)),
            whole(3, model, width),
            whole(model, hidden),
            rows_of(BT, model),
            whole(4, model),
        ],
        [
            *[pl.BlockSpec((n_head // 2, BT, share), lambda i: (0, i, 0))] * 4,
            whole(16, stat_width),
        ],
        [
            *[sds((n_head // 2, rows, share), bf16)] * 4,
            sds((16, stat_width), f32),
        ],
        [pltpu.VMEM((BT, model), bf16)],
        2 * rows * model * (3 * width + hidden),
        rows * width * 6 + rows * model * 6 + 8 * model * width + 2 * hidden * model,
    )(me_head, hid, w_down, att, w_out, dpre, after(low, event), w_qkv, w_in, xhat, gains)
    with jax.named_scope("mixed_sum"):
        mixed_share = scatter_sum(val_keep, after(val_send, low), "head")
    with jax.named_scope("e_sum"):
        e_share = scatter_sum(e_keep, e_send, "head")
    with jax.named_scope("stats_sum"):
        gains_own = stats[8:12, :model]
        stats = sum_all(stats[:8], "head")
    stats = stats[:2, :rows].T * (1.0 / model)

    bias = lax.dynamic_slice_in_dim(b_out, offset, share) + lax.dynamic_slice_in_dim(b_down, offset, share)
    mixed = (tokens.astype(f32) + mixed_share + bias).astype(bf16)
    xhat_share = lax.dynamic_slice_in_dim(xhat, offset, share, 1).astype(f32)
    grad_input = grad_out.astype(f32) + inv_std * (
        e_share - stats[:, 0:1] - xhat_share * stats[:, 1:2]
    )
    event = late = e_send
    for name in AFTER:
        chunk = chunks[name]
        if chunk.plan:
            pins = (mixed, grad_input) if len(chunk.plan) == 1 and name in PINNED else ()
            event = chunk.step(event, *pins)
        late = event if len(qkvo.plan) == LATE else late
    for chunk in chunks.values():
        while chunk.plan:
            event = chunk.step(event)
    g_down = block_out(down, me_seq)
    g_in = block_out(inn, me_seq)
    g_qkv, g_out = call(
        widen_kernel,
        4,
        [smem(), *[pl.BlockSpec((quarter, 1, part, width), lambda c: (0, c, 0, 0))] * 4],
        [
            pl.BlockSpec((1, model, width), lambda c: (jnp.minimum(c, 2), 0, 0)),
            whole(width, model),
        ],
        [sds((3, model, width), f32), sds((width, model), f32)],
        [pltpu.VMEM((model, width), f32)],
        0,
        END_COST * model * width,
    )(me_seq, *qkvo.arrays)

    with jax.named_scope("small_sum"):
        local = jnp.concatenate([small[:4], gb_in.reshape(-1, share), bias_out], 0)
        mine = (jnp.arange(n_head) == lax.axis_index("head")).astype(f32)
        spread_gains = gains_own.reshape(4, n_head, share).transpose(1, 0, 2)
        packet = jnp.concatenate([spread_gains, mine[:, None, None] * local[None]], 1)
        packet = jnp.broadcast_to(packet[None], (n_seq,) + packet.shape).reshape((-1,) + packet.shape[1:])
        packet = jnp.sum(lax.all_to_all(after(packet, late), ("seq", "head"), 0, 0, tiled=True), 0)
    gain_share, small, gb_in, bias_out = packet[:4], packet[4:8], packet[8:-1].reshape(-1), packet[-1]
    return (
        mixed,
        grad_input,
        gain_share[0],
        gain_share[1],
        gain_share[2],
        gain_share[3],
        g_qkv,
        small[:3],
        small[3].reshape(heads, feats),
        g_out,
        bias_out,
        g_in,
        gb_in,
        g_down,
        bias_out,
    )


def solution(mesh):
    in_specs = (
        P("seq", "head"),
        P(),
        P("seq"),
        P(),
        P(),
        P(),
        P(),
        P(None, None, "head"),
        P(None, "head"),
        P("head", None),
        P("head", None),
        P(),
        P(None, "head"),
        P("head"),
        P("head", None),
        P(),
        P("seq", "head"),
    )
    out_specs = (
        P("seq", "head"),
        P("seq", "head"),
        P("head"),
        P("head"),
        P("head"),
        P("head"),
        P(None, None, "head"),
        P(None, "head"),
        P("head", None),
        P("head", None),
        P("head"),
        P(None, "head"),
        P("head"),
        P("head", None),
        P("head"),
    )
    return jax.shard_map(body, mesh=mesh, in_specs=in_specs, out_specs=out_specs, check_vma=False)
```

```python
import functools
import math
from statistics import NormalDist

import jax
import jax.numpy as jnp
import numpy as np
from jax import lax
from jax.experimental import pallas as pl
from jax.experimental.pallas import tpu as pltpu
from jax.sharding import PartitionSpec as P

ROT = 16
eps_norm = 1e-05
rope_base = 10000.0
feature_scale = 0.5
BT = 512
LANES = 128
bf16 = jnp.bfloat16
f32 = jnp.float32
COST_SCALE = 1.0
END_COST = 12
BEFORE = "DI"
AFTER = "DCICIDCIC"
PINNED = "C"
LATE = 3
VMEM_LIMIT = 56 * 1024 * 1024


def nn(a, b):
    return lax.dot_general(a, b, (((1,), (0,)), ((), ())), preferred_element_type=f32)


def nt(a, b):
    return lax.dot_general(a, b, (((1,), (1,)), ((), ())), preferred_element_type=f32)


def tn(a, b):
    return lax.dot_general(a, b, (((0,), (0,)), ((), ())), preferred_element_type=f32)


def split(x):
    hi = x.astype(bf16)
    return hi, (x - hi.astype(f32)).astype(bf16)


def feature_table(feat_count, head_size):
    rows = np.arange(feat_count)
    cols = np.arange(head_size)
    cosines = np.cos(math.pi * (cols[None, :] + 0.5) * rows[:, None] / head_size)
    scaling = np.where(rows == 0, math.sqrt(1.0 / head_size), math.sqrt(2.0 / head_size))
    points = np.array([NormalDist().inv_cdf((r + 0.5) / feat_count) for r in range(feat_count)])
    return feature_scale * (points * scaling)[:, None] * cosines


def lane_head(shape, head_size):
    return lax.broadcasted_iota(jnp.int32, shape, len(shape) - 1) // head_size


def block_ones(size, head_size):
    rows = lax.broadcasted_iota(jnp.int32, (size, size), 0) // head_size
    cols = lax.broadcasted_iota(jnp.int32, (size, size), 1) // head_size
    return rows == cols


def swap_halves(x, head_size):
    width = x.shape[1]
    lane = lax.broadcasted_iota(jnp.int32, x.shape, 1) % head_size
    ahead = pltpu.roll(x, width - ROT // 2, 1)
    behind = pltpu.roll(x, ROT // 2, 1)
    return jnp.where(lane < ROT // 2, ahead, behind)


def widen(table, width):
    return table if table.shape[1] == width else jnp.concatenate([table] * (width // table.shape[1]), 1)


def pack_state(state, norm, head_size):
    size = state.shape[0]
    masked = jnp.where(block_ones(size, head_size), state, 0.0)
    packed = masked[:head_size]
    for h in range(1, size // head_size):
        packed = packed + masked[h * head_size : (h + 1) * head_size]
    return packed, norm


def unpack_state(packed, head_size):
    size = packed.shape[1]
    rows = jnp.concatenate([packed[:head_size]] * (size // head_size), 0)
    return jnp.where(block_ones(size, head_size), rows, 0.0)


def place(full_ref, piece_refs, me_ref):
    for k, ref in enumerate(piece_refs):
        size = ref.shape[1]
        start = pl.multiple_of((me_ref[0] ^ k) * size, LANES)
        full_ref[:, pl.ds(start, size)] = ref[...]


def pre_kernel(
    head_size,
    pieces,
    labels_ref,
    me_ref,
    *refs,
):
    x_refs = refs[:pieces]
    (
        gains_ref,
        w_ref,
        bq_ref,
        fw_ref,
        tab_ref,
        cos_ref,
        sin_ref,
        valid_ref,
        seg_ref,
        ln1t_ref,
        ln2_ref,
        ln2t_ref,
        xhat_ref,
        inv_ref,
        qe_ref,
        ke_ref,
        qf_ref,
        kf_ref,
        v_ref,
        pk_ref,
        full_ref,
        state_ref,
        norm_ref,
    ) = refs[pieces:]
    step = pl.program_id(0)
    width = qe_ref.shape[1]
    place(full_ref, x_refs, me_ref)
    x = full_ref[...].astype(f32)
    centered = x - jnp.mean(x, -1, keepdims=True)
    inv = lax.rsqrt(jnp.mean(centered * centered, -1, keepdims=True) + eps_norm)
    xhat = centered * inv
    inv_ref[...] = inv
    xhat_ref[...] = xhat.astype(bf16)
    ln1 = (xhat * gains_ref[0:1] + gains_ref[1:2]).astype(bf16)
    ln2 = (xhat * gains_ref[2:3] + gains_ref[3:4]).astype(bf16)
    ln2_ref[...] = ln2
    ln1t_ref[...] = ln1.T
    ln2t_ref[...] = ln2.T
    cosine = widen(cos_ref[...], width)
    sine = widen(sin_ref[...], width)

    def features(c):
        raw = nn(ln1, w_ref[c]) + bq_ref[c : c + 1]
        turned = raw * cosine + swap_halves(raw, head_size) * sine
        hi, lo = split(turned)
        return jnp.exp(nn(hi, tab_ref[0]) + nn(lo, tab_ref[0]) + nn(hi, tab_ref[1]))

    fw = fw_ref[...]
    qe = features(0)
    ke = features(1) * valid_ref[...]
    qe_ref[...] = qe
    ke_ref[...] = ke
    qf_ref[...] = (fw * qe).astype(bf16)
    kf = (fw * ke).astype(bf16)
    kf_ref[...] = kf
    v = (nn(ln1, w_ref[2]) + bq_ref[2:3]).astype(bf16)
    v_ref[...] = v

    @pl.when(step == 0)
    def _():
        state_ref[...] = jnp.zeros_like(state_ref)
        norm_ref[...] = jnp.zeros_like(norm_ref)

    tail = kf.astype(f32) * (seg_ref[...] == labels_ref[pl.num_programs(0) - 1, 1]).astype(f32)
    state_ref[...] += tn(tail.astype(bf16), v)
    norm_ref[...] += jnp.broadcast_to(jnp.sum(tail, 0, keepdims=True), norm_ref.shape)

    @pl.when(step == pl.num_programs(0) - 1)
    def _():
        packed, norm = pack_state(state_ref[...], norm_ref[...], head_size)
        for i in range(pk_ref.shape[0]):
            pk_ref[i, :head_size] = packed
            pk_ref[i, head_size:] = norm


def slot_of(relative, count):
    place = 0
    mask = 4
    while mask < count:
        place = 2 * place + (relative // mask) % 2
        mask *= 2
    return place


def store_blocks(block, base, me, refs, part, rest=()):
    count = 4 * refs[0].shape[0]
    for low in range(4):

        @pl.when(me % 4 == low)
        def _():
            for j in range(block.shape[0] // part):
                ref = refs[(low ^ (base + j)) % 4]
                ref[(slot_of(me ^ (base + j), count),) + rest] = block[j * part : (j + 1) * part]


def ff_kernel(pieces, me_ref, rank_ref, *refs):
    grad_refs = refs[:pieces]
    (
        ln2_ref,
        ln2t_ref,
        win_ref,
        bin_ref,
        wdown_ref,
        grad_ref,
        hid_ref,
        dpre_ref,
        *sum_refs,
        gb_ref,
    ) = refs[pieces:]

    @pl.when(pl.program_id(0) == 0)
    def _():
        place(grad_ref, grad_refs, me_ref)

    chunk = ln2_ref.shape[0] // 4
    sums = jnp.zeros((1, win_ref.shape[1]), f32)
    for r in range(4):
        part = slice(r * chunk, (r + 1) * chunk)
        pre = nn(ln2_ref[part], win_ref[...]) + bin_ref[...]
        phi_cum = 0.5 + 0.5 * lax.erf(pre * (1.0 / math.sqrt(2.0)))
        hid_ref[part] = (pre * phi_cum).astype(bf16)
        slope = phi_cum + pre * jnp.exp(-0.5 * pre * pre) * (1.0 / math.sqrt(2.0 * math.pi))
        dpre = nt(grad_ref[part], wdown_ref[...]) * slope
        sums = sums + jnp.sum(dpre, 0, keepdims=True)
        dpre_ref[part] = dpre.astype(bf16)
    gb_ref[...] = sums
    me = rank_ref[0]
    g_down = tn(hid_ref[...], grad_ref[...]).astype(bf16)
    part = sum_refs[0].shape[1]
    steps = 4 * sum_refs[0].shape[0] * part // g_down.shape[0]
    for step in range(steps):

        @pl.when(pl.program_id(0) == step)
        def _():
            store_blocks(g_down, step * (g_down.shape[0] // part), me, sum_refs[:4], part)

    g_in = nn(ln2t_ref[...], dpre_ref[...]).astype(bf16)
    store_blocks(g_in, 0, me, sum_refs[4:], sum_refs[4].shape[1])


def block_out_kernel(rank_ref, *refs):
    out_ref = refs[4]
    part = refs[0].shape[1]
    for low in range(4):

        @pl.when(rank_ref[0] % 4 == low)
        def _():
            for j in range(4):
                out_ref[j * part : (j + 1) * part] = refs[low ^ j][0].astype(f32)


def attn_kernel(
    head_size,
    labels_ref,
    qf_ref,
    kf_ref,
    v_ref,
    grad_ref,
    wout_ref,
    segc_ref,
    segr_ref,
    spk_ref,
    att_ref,
    dq_ref,
    dk_ref,
    dv_ref,
    gb_ref,
    gzb_ref,
    gpk_ref,
    gout_ref,
    state_ref,
    norm_ref,
    lead_ref,
    leadz_ref,
    acc_ref,
):
    step = pl.program_id(0)
    last = pl.num_programs(0) - 1
    rows, width = qf_ref.shape
    heads = width // head_size
    same = block_ones(width, head_size)
    ones = same.astype(f32).astype(bf16)

    def head_sum(x):
        hi, lo = split(x)
        return nn(hi, ones) + nn(lo, ones)

    @pl.when(step == 0)
    def _():
        state_ref[...] = unpack_state(spk_ref[...], head_size)
        norm_ref[...] = spk_ref[head_size : head_size + 8]
        lead_ref[...] = jnp.zeros_like(lead_ref)
        leadz_ref[...] = jnp.zeros_like(leadz_ref)
        acc_ref[...] = jnp.zeros_like(acc_ref)

    seg = segc_ref[...]
    enters = (seg == labels_ref[step, 0]).astype(f32)
    tail = (seg == labels_ref[step, 1]).astype(f32)
    lead = (seg == labels_ref[0, 2]).astype(f32)
    linked = (labels_ref[step, 0] == labels_ref[step, 1]).astype(f32)
    qf = qf_ref[...]
    kf = kf_ref[...]
    v = v_ref[...]
    qf32 = qf.astype(f32)
    norm = norm_ref[0:1]
    lane = lane_head((rows, width), head_size)
    zero16 = jnp.zeros((rows, width), bf16)

    def stack(x):
        return jnp.concatenate([jnp.where(lane == h, x, zero16) for h in range(heads)], 0)

    def unstack(x):
        total = jnp.where(lane == 0, x[:rows], 0.0)
        for h in range(1, heads):
            total = jnp.where(lane == h, x[h * rows : (h + 1) * rows], total)
        return total

    causal = lax.broadcasted_iota(jnp.int32, (rows, rows), 0) >= lax.broadcasted_iota(
        jnp.int32, (rows, rows), 1
    )
    joined = causal & (seg == segr_ref[...])
    joined_all = jnp.concatenate([joined.astype(f32)] * heads, 0)
    q_stack = stack(qf)
    scores = (nt(q_stack, kf) * joined_all).astype(bf16)
    ones_v = jnp.ones((rows, LANES), bf16)
    sums = nn(scores, ones_v)
    den_in = jnp.where(lane == 0, widen(sums[:rows], width), 0.0)
    for h in range(1, heads):
        den_in = jnp.where(lane == h, widen(sums[h * rows : (h + 1) * rows], width), den_in)
    s_hi, s_lo = split(state_ref[...])
    num = unstack(nn(scores, v)) + enters * (nn(qf, s_hi) + nn(qf, s_lo))
    den = den_in + enters * head_sum(qf32 * norm)
    inv_den = 1.0 / den
    att = num * inv_den
    att_low = att.astype(bf16)
    att_ref[...] = att_low
    acc_ref[...] += tn(att_low, grad_ref[...])
    d_att = nt(grad_ref[...], wout_ref[...])
    d_num = d_att * inv_den
    d_den = -head_sum(d_att * att) * inv_den
    dn_hi, dn_lo = split(d_num)
    dn_stack = stack(dn_hi)
    dden_all = jnp.concatenate([d_den[:, h * head_size : h * head_size + 1] for h in range(heads)], 0)
    d_scores = ((nt(dn_stack, v) + dden_all) * joined_all).astype(bf16)
    inter = nt(dn_hi, s_hi) + nt(dn_lo, s_hi) + nt(dn_hi, s_lo) + d_den * norm
    dq_ref[...] = unstack(nn(d_scores, kf)) + enters * inter
    dk_ref[...] = tn(d_scores, q_stack)
    dv_ref[...] = tn(scores, dn_stack)
    q_in = (qf32 * enters).astype(bf16)
    gb_ref[0] = jnp.where(same, tn(q_in, dn_hi) + tn(q_in, dn_lo), 0.0)
    weighted = qf32 * d_den
    gzb_ref[0] = jnp.broadcast_to(jnp.sum(weighted * enters, 0, keepdims=True), (8, width))
    q_lead = (qf32 * lead).astype(bf16)
    lead_ref[...] += tn(q_lead, dn_hi) + tn(q_lead, dn_lo)
    leadz_ref[...] += jnp.broadcast_to(jnp.sum(weighted * lead, 0, keepdims=True), (8, width))
    k_tail = kf.astype(f32) * tail
    state_ref[...] = linked * state_ref[...] + jnp.where(same, tn(k_tail.astype(bf16), v), 0.0)
    norm_ref[...] = linked * norm_ref[...] + jnp.broadcast_to(jnp.sum(k_tail, 0, keepdims=True), (8, width))

    @pl.when(step == last)
    def _():
        packed, z = pack_state(lead_ref[...], leadz_ref[...], head_size)
        gpk_ref[:head_size] = packed
        gpk_ref[head_size:] = z
        gout_ref[...] = acc_ref[...].T.astype(bf16)


def spread(full, keep_ref, send_ref, scratch_ref, me_ref):
    scratch_ref[...] = full.astype(bf16)
    size = keep_ref.shape[2]
    for k in range(2 * keep_ref.shape[0]):
        start = pl.multiple_of((me_ref[0] ^ k) * size, LANES)
        (send_ref if k % 2 else keep_ref)[k // 2] = scratch_ref[:, pl.ds(start, size)]


def tail_kernel(
    head_size,
    labels_ref,
    dq_ref,
    dk_ref,
    dv_ref,
    qe_ref,
    ke_ref,
    kf_ref,
    v_ref,
    gb_ref,
    gzb_ref,
    gin_ref,
    segc_ref,
    cos_ref,
    sin_ref,
    fw_ref,
    tab_ref,
    ln1t_ref,
    gout_ref,
    rank_ref,
    low_ref,
    small_ref,
    sum0_ref,
    sum1_ref,
    sum2_ref,
    sum3_ref,
    state_ref,
    norm_ref,
    all_ref,
):
    step = pl.program_id(0)
    last = pl.num_programs(0) - 1
    block = last - step
    rows, width = dq_ref.shape

    @pl.when(step == 0)
    def _():
        state_ref[...] = unpack_state(gin_ref[...], head_size)
        norm_ref[...] = gin_ref[head_size : head_size + 8]
        small_ref[...] = jnp.zeros_like(small_ref)

    tail = (segc_ref[...] == labels_ref[block, 1]).astype(f32)
    linked = (labels_ref[block, 0] == labels_ref[block, 1]).astype(f32)
    g_hi, g_lo = split(state_ref[...])
    v = v_ref[...]
    kf = kf_ref[...]
    dk = dk_ref[...] + tail * (nt(v, g_hi) + nt(v, g_lo) + norm_ref[0:1])
    dv = dv_ref[...] + tail * (nn(kf, g_hi) + nn(kf, g_lo))
    state_ref[...] = linked * state_ref[...] + gb_ref[0]
    norm_ref[...] = linked * norm_ref[...] + gzb_ref[0]
    fw = fw_ref[...]
    gq = dq_ref[...] * qe_ref[...]
    gk = dk * ke_ref[...]
    cosine = widen(cos_ref[...], width)
    sine = widen(sin_ref[...], width)

    def back(g):
        hi, lo = split(g * fw)
        turned = nt(hi, tab_ref[0]) + nt(lo, tab_ref[0]) + nt(hi, tab_ref[1])
        return turned * cosine - swap_halves(turned, head_size) * sine

    dq_raw = back(gq)
    dk_raw = back(gk)
    small_ref[0:1] += jnp.sum(dq_raw, 0, keepdims=True)
    small_ref[1:2] += jnp.sum(dk_raw, 0, keepdims=True)
    small_ref[2:3] += jnp.sum(dv, 0, keepdims=True)
    small_ref[3:4] += jnp.sum(gq + gk, 0, keepdims=True)
    start = pl.multiple_of(block * rows, rows)
    for c, d in enumerate((dq_raw, dk_raw, dv)):
        low = d.astype(bf16)
        low_ref[c] = low
        all_ref[c, pl.ds(start, rows)] = low

    @pl.when(step == last)
    def _():
        me = rank_ref[0]
        part = sum0_ref.shape[2]
        for c in range(4):
            g = gout_ref[...] if c == 3 else nn(ln1t_ref[...], all_ref[c]).astype(bf16)

            store_blocks(g, 0, me, (sum0_ref, sum1_ref, sum2_ref, sum3_ref), part, (c,))


def finish_kernel(
    me_ref,
    hid_ref,
    wdown_ref,
    att_ref,
    wout_ref,
    dpre_ref,
    low_ref,
    w_ref,
    win_ref,
    xhat_ref,
    gains_ref,
    val_keep_ref,
    val_send_ref,
    keep_ref,
    send_ref,
    stat_ref,
    scratch_ref,
):
    value = nn(hid_ref[...], wdown_ref[...]) + nn(att_ref[...], wout_ref[...])
    spread(value, val_keep_ref, val_send_ref, scratch_ref, me_ref)
    step = pl.program_id(0)
    rows, model = xhat_ref.shape

    @pl.when(step == 0)
    def _():
        stat_ref[8:16] = jnp.zeros((8, stat_ref.shape[1]), f32)

    d_ln1 = nt(low_ref[0], w_ref[0]) + nt(low_ref[1], w_ref[1]) + nt(low_ref[2], w_ref[2])
    d_ln2 = nt(dpre_ref[...], win_ref[...])
    xhat = xhat_ref[...].astype(f32)
    e = d_ln1 * gains_ref[0:1] + d_ln2 * gains_ref[2:3]
    spread(e, keep_ref, send_ref, scratch_ref, me_ref)
    ones = jnp.ones((8, model), bf16)
    hi, lo = split(e)
    sum_e = nt(ones, hi) + nt(ones, lo)
    hi, lo = split(e * xhat)
    sum_ex = nt(ones, hi) + nt(ones, lo)
    row = lax.broadcasted_iota(jnp.int32, sum_e.shape, 0)
    start = pl.multiple_of(step * rows, rows)
    stat_ref[0:8, pl.ds(start, rows)] = jnp.where(row == 0, sum_e, sum_ex)
    stat_ref[8:9, :model] += jnp.sum(d_ln1 * xhat, 0, keepdims=True)
    stat_ref[9:10, :model] += jnp.sum(d_ln1, 0, keepdims=True)
    stat_ref[10:11, :model] += jnp.sum(d_ln2 * xhat, 0, keepdims=True)
    stat_ref[11:12, :model] += jnp.sum(d_ln2, 0, keepdims=True)


def widen_kernel(rank_ref, *refs):
    qkv_ref, out_ref, scratch_ref = refs[4:]
    c = pl.program_id(0)
    quarter, _, part, _ = refs[0].shape
    me = rank_ref[0]
    for low in range(4):

        @pl.when(me % 4 == low)
        def _():
            for j in range(4 * quarter):
                slot = slot_of(me ^ j, 4 * quarter)
                scratch_ref[j * part : (j + 1) * part] = refs[(low ^ j) % 4][slot, 0].astype(f32)

    @pl.when(c < 3)
    def _():
        qkv_ref[0] = scratch_ref[...]

    @pl.when(c == 3)
    def _():
        out_ref[...] = scratch_ref[...].T


def whole(*shape):
    return pl.BlockSpec(shape, lambda *_: (0,) * len(shape))


def rows_of(*shape):
    return pl.BlockSpec(shape, lambda i: (i,) + (0,) * (len(shape) - 1))


def smem():
    return pl.BlockSpec(memory_space=pltpu.SMEM)


def sds(shape, dtype):
    return jax.ShapeDtypeStruct(shape, dtype)


def call(kernel, grid, in_specs, out_specs, out_shape, scratch, flops, moved, aliases={}):
    return pl.pallas_call(
        kernel,
        grid=(grid,),
        in_specs=in_specs,
        out_specs=out_specs,
        out_shape=out_shape,
        scratch_shapes=scratch,
        input_output_aliases=aliases,
        compiler_params=pltpu.CompilerParams(vmem_limit_bytes=VMEM_LIMIT),
        cost_estimate=pl.CostEstimate(
            flops=int(flops * COST_SCALE), bytes_accessed=int(moved * COST_SCALE), transcendentals=0
        ),
        name=getattr(kernel, "func", kernel).__name__,
    )


def exchange(x, axis, mask):
    count = lax.axis_size(axis)
    return lax.ppermute(x, axis, [(i, i ^ mask) for i in range(count)])


def gather_far(x, axis):
    pieces = {0: x}
    mask = lax.axis_size(axis) // 2
    while mask > 1:
        pieces.update({k ^ mask: exchange(p, axis, mask) for k, p in sorted(pieces.items())})
        mask //= 2
    return pieces


def gather_near(pieces, axis):
    pieces = pieces | {k ^ 1: exchange(p, axis, 1) for k, p in sorted(pieces.items())}
    return [pieces[k] for k in sorted(pieces)]


def scatter_sum(keep, send, axis):
    mask = 1
    while True:
        got = exchange(send, axis, mask)
        if keep.shape[0] == 1:
            return keep[0].astype(f32) + got[0].astype(f32)
        total_keep = keep[0::2].astype(f32) + got[0::2].astype(f32)
        total_send = keep[1::2].astype(f32) + got[1::2].astype(f32)
        keep, send = total_keep.astype(bf16), total_send.astype(bf16)
        mask *= 2


def sum_all(x, axis):
    mask = 1
    while mask < lax.axis_size(axis):
        x = x + exchange(x, axis, mask)
        mask *= 2
    return x


class Sum:
    def __init__(self, name, arrays):
        self.name, self.arrays = name, list(arrays)
        masks = []
        while 4 * 2 ** len(masks) < lax.axis_size("seq"):
            masks.append(4 * 2 ** len(masks))
        self.plan = [("group", 0)] + [("reduce", m) for m in masks]
        self.plan += [("gather", m) for m in masks[::-1]] + [("spread", 0)]

    def halves(self, terms):
        half = terms[0].shape[0] // 2

        def total(part):
            return sum(t[part].astype(f32) for t in terms).astype(bf16)

        if half:
            self.keep, self.send = total(slice(0, half)), total(slice(half, None))
        else:
            self.keep = self.send = total(slice(None))
        return self.send

    def step(self, *pins):
        kind, mask = self.plan.pop(0)
        with jax.named_scope(self.name):
            if kind == "group":
                got = after(tuple(exchange(self.arrays[g], "seq", g) for g in (3, 2, 1)), *pins)
                return self.halves([self.arrays[0], *got])
            if kind == "reduce":
                return self.halves([self.keep, after(exchange(self.send, "seq", mask), *pins)])
            if kind == "gather":
                self.keep = jnp.concatenate([self.keep, after(exchange(self.keep, "seq", mask), *pins)])
                return self.keep
            self.arrays = [self.keep, *after(tuple(exchange(self.keep, "seq", g) for g in (1, 2, 3)), *pins)]
            return self.arrays[1]


def block_out(chunk, me_seq):
    quarter, part, width = chunk.keep.shape
    block = pl.BlockSpec((1, part, width), lambda i, me: (slot_of(((me[0] // 4) ^ i) * 4, 4 * quarter), 0, 0))
    return pl.pallas_call(
        block_out_kernel,
        grid_spec=pltpu.PrefetchScalarGridSpec(
            num_scalar_prefetch=1,
            grid=(quarter,),
            in_specs=[block] * 4,
            out_specs=pl.BlockSpec((4 * part, width), lambda i, me: (i, 0)),
        ),
        out_shape=sds((4 * quarter * part, width), f32),
        compiler_params=pltpu.CompilerParams(vmem_limit_bytes=VMEM_LIMIT),
        cost_estimate=pl.CostEstimate(flops=0, bytes_accessed=24 * quarter * part * width, transcendentals=0),
        name="block_out_kernel",
    )(me_seq, *chunk.arrays)


def sum_before(copies):
    count = lax.axis_size("seq")
    packets = lax.all_to_all(copies, "seq", 0, 0, tiled=True)
    wanted = (jnp.arange(count) < lax.axis_index("seq")).astype(f32)
    return jnp.sum(packets * wanted[:, None, None], 0)


def after(x, *others):
    return lax.optimization_barrier((x,) + others)[0]


def neighbour_sum(packet, sign, pin, event):
    count = lax.axis_size("seq")
    outer = 4 if count % 4 == 0 else 1
    inner = count // outer
    me = lax.axis_index("seq")
    mine = me % inner
    group = packet
    before = jnp.zeros_like(packet)
    for k in range(1, inner):
        route = [(i, i - i % inner + (i % inner + k) % inner) for i in range(count)]
        got = after(lax.ppermute(packet, "seq", route), pin)
        event(got)
        sender = (mine - k) % inner
        group = group + got
        before = before + jnp.where((sender < mine) if sign > 0 else (sender > mine), got, 0.0)
    for k in range(1, outer):
        shift = sign * k * inner
        route = [(i, i + shift) for i in range(count) if 0 <= i + shift < count]
        before = before + lax.ppermute(group, "seq", route)
    return before


def body(
    tokens,
    lengths,
    pad_mask,
    ln1_gain,
    ln1_bias,
    ln2_gain,
    ln2_bias,
    w_qkv,
    b_qkv,
    feat_weight,
    w_out,
    b_out,
    w_in,
    b_in,
    w_down,
    b_down,
    grad_out,
):
    rows, share = tokens.shape
    heads, feats = feat_weight.shape
    width = w_qkv.shape[2]
    head_size = width // heads
    model, hidden = w_in.shape
    blocks = rows // BT
    n_head = lax.axis_size("head")
    offset = lax.axis_index("head") * share
    with jax.named_scope("gather_tokens"):
        token_far = gather_far(tokens, "head")
    me_head = jnp.reshape(lax.axis_index("head"), (1,)).astype(jnp.int32)
    me_seq = jnp.reshape(lax.axis_index("seq"), (1,)).astype(jnp.int32)
    n_seq = lax.axis_size("seq")

    index_all = lax.axis_index("seq") * rows + jnp.arange(rows, dtype=jnp.int32)
    seq_ends = jnp.cumsum(lengths).astype(jnp.int32)
    starts = seq_ends - lengths

    def seg_of(index):
        return jnp.sum((index[:, None] >= seq_ends[None, :]).astype(jnp.int32), 1)

    segment = seg_of(index_all)
    picked = segment[:, None] == jnp.arange(lengths.shape[0])[None, :]
    position = index_all - jnp.sum(jnp.where(picked, starts[None, :], 0), 1)
    base = lax.axis_index("seq") * rows + jnp.arange(blocks, dtype=jnp.int32) * BT
    label_in = seg_of(jnp.maximum(base - 1, 0))
    label_last = seg_of(base + (BT - 1))
    label_first = jnp.broadcast_to(segment[0], (blocks,))
    labels = jnp.stack([label_in, label_last, label_first], 1)
    seg_col = segment[:, None]
    seg_row = segment[None, :]
    lane = np.arange(LANES) % head_size
    inverse = np.where(lane < ROT, rope_base ** (-2.0 * (lane % (ROT // 2)) / ROT), 0.0)
    angles = position.astype(f32)[:, None] * jnp.asarray(inverse, f32)[None, :]
    sign = np.where(lane < ROT // 2, -1.0, np.where(lane < ROT, 1.0, 0.0))
    cosine = jnp.cos(angles)
    sine = jnp.sin(angles) * jnp.asarray(sign, f32)[None, :]
    valid = pad_mask.astype(f32)[:, None]
    table = np.kron(np.eye(heads), feature_table(feats, head_size).T).astype(np.float32)
    table_hi = table.astype(bf16)
    table_lo = (table - table_hi.astype(np.float32)).astype(bf16)
    tab = jnp.asarray(np.stack([table_hi, table_lo]))
    gains = jnp.stack([ln1_gain, ln1_bias, ln2_gain, ln2_bias])
    fw = feat_weight.reshape(1, width)
    bias_out = jnp.sum(grad_out.astype(f32), 0, keepdims=True)
    with jax.named_scope("gather_grads"):
        early = (cosine, sine, gains, bias_out, labels, valid, seg_col, seg_row, fw)
        grad_far = gather_far(after(grad_out, *early), "head")
    with jax.named_scope("gather_tokens"):
        token_pieces = gather_near({k: after(p, *early) if k else p for k, p in token_far.items()}, "head")
    packet_shape = (head_size + 8, width)

    ln1t, ln2, ln2t, xhat, inv_std, q_expo, k_expo, qf, kf, v, s_own = call(
        functools.partial(pre_kernel, head_size, n_head),
        blocks,
        [
            smem(),
            smem(),
            *[rows_of(BT, share)] * n_head,
            whole(4, model),
            whole(3, model, width),
            whole(3, width),
            whole(1, width),
            whole(2, width, width),
            rows_of(BT, LANES),
            rows_of(BT, LANES),
            rows_of(BT, 1),
            rows_of(BT, 1),
        ],
        [
            pl.BlockSpec((model, BT), lambda i: (0, i)),
            rows_of(BT, model),
            pl.BlockSpec((model, BT), lambda i: (0, i)),
            rows_of(BT, model),
            rows_of(BT, 1),
            rows_of(BT, width),
            rows_of(BT, width),
            rows_of(BT, width),
            rows_of(BT, width),
            rows_of(BT, width),
            whole(n_seq, *packet_shape),
        ],
        [
            sds((model, rows), bf16),
            sds((rows, model), bf16),
            sds((model, rows), bf16),
            sds((rows, model), bf16),
            sds((rows, 1), f32),
            sds((rows, width), f32),
            sds((rows, width), f32),
            sds((rows, width), bf16),
            sds((rows, width), bf16),
            sds((rows, width), bf16),
            sds((n_seq,) + packet_shape, f32),
        ],
        [pltpu.VMEM((BT, model), bf16), pltpu.VMEM((width, width), f32), pltpu.VMEM((8, width), f32)],
        2 * rows * model * 3 * width + 16 * rows * width * width,
        rows * model * 10 + 6 * model * width,
    )(labels, me_head, *token_pieces, gains, w_qkv, b_qkv, fw, tab, cosine, sine, valid, seg_col)

    with jax.named_scope("gather_grads"):
        grad_pieces = gather_near({k: after(p, s_own) for k, p in grad_far.items()}, "head")
    with jax.named_scope("state"):
        s_in = sum_before(s_own)

    fb = 512
    quarter = n_seq // 4
    full_grad, hid, dpre, *ff_sums, gb_in = call(
        functools.partial(ff_kernel, n_head),
        hidden // fb,
        [
            smem(),
            smem(),
            *[whole(rows, share)] * n_head,
            whole(rows, model),
            whole(model, rows),
            pl.BlockSpec((model, fb), lambda i: (0, i)),
            pl.BlockSpec((1, fb), lambda i: (0, i)),
            pl.BlockSpec((fb, model), lambda i: (i, 0)),
        ],
        [
            whole(rows, model),
            pl.BlockSpec((rows, fb), lambda i: (0, i)),
            pl.BlockSpec((rows, fb), lambda i: (0, i)),
            *[whole(quarter, hidden // n_seq, model)] * 4,
            *[pl.BlockSpec((quarter, model // n_seq, fb), lambda i: (0, 0, i))] * 4,
            pl.BlockSpec((1, fb), lambda i: (0, i)),
        ],
        [
            sds((rows, model), bf16),
            sds((rows, hidden), bf16),
            sds((rows, hidden), bf16),
            *[sds((quarter, hidden // n_seq, model), bf16)] * 4,
            *[sds((quarter, model // n_seq, hidden), bf16)] * 4,
            sds((1, hidden), f32),
        ],
        [],
        8 * rows * model * hidden,
        6 * rows * model + 8 * model * hidden,
    )(me_head, me_seq, *grad_pieces, ln2, ln2t, w_in, b_in[None, :], w_down)

    s_in = after(s_in, hid)

    att, dq, dk, dv, gb, gzb, g_own, g_out = call(
        functools.partial(attn_kernel, head_size),
        blocks,
        [
            smem(),
            rows_of(BT, width),
            rows_of(BT, width),
            rows_of(BT, width),
            rows_of(BT, model),
            whole(width, model),
            rows_of(BT, 1),
            pl.BlockSpec((1, BT), lambda i: (0, i)),
            whole(*packet_shape),
        ],
        [
            rows_of(BT, width),
            rows_of(BT, width),
            rows_of(BT, width),
            rows_of(BT, width),
            rows_of(1, width, width),
            rows_of(1, 8, width),
            whole(*packet_shape),
            whole(model, width),
        ],
        [
            sds((rows, width), bf16),
            sds((rows, width), f32),
            sds((rows, width), f32),
            sds((rows, width), f32),
            sds((blocks, width, width), f32),
            sds((blocks, 8, width), f32),
            sds(packet_shape, f32),
            sds((model, width), bf16),
        ],
        [
            pltpu.VMEM((width, width), f32),
            pltpu.VMEM((8, width), f32),
            pltpu.VMEM((width, width), f32),
            pltpu.VMEM((8, width), f32),
            pltpu.VMEM((width, model), f32),
        ],
        24 * rows * heads * BT * width,
        rows * model * 2 + rows * width * 20,
    )(labels, qf, kf, v, full_grad, w_out, seg_col, seg_row, s_in)

    down = Sum("reduce_down", ff_sums[:4])
    seen = []
    with jax.named_scope("grad_state"):
        grad_in = neighbour_sum(g_own, -1, hid, seen.append)
    inn = Sum("reduce_in", [ff_sums[4], *after(tuple(ff_sums[5:]), *seen)])
    event = down.step(*seen)
    grad_in = after(grad_in, event)

    def back_rows(*shape):
        return pl.BlockSpec(shape, lambda i: (blocks - 1 - i,) + (0,) * (len(shape) - 1))

    part = model // n_seq
    low, small, *w_parts = call(
        functools.partial(tail_kernel, head_size),
        blocks,
        [
            smem(),
            *[back_rows(BT, width)] * 7,
            back_rows(1, width, width),
            back_rows(1, 8, width),
            whole(*packet_shape),
            back_rows(BT, 1),
            back_rows(BT, LANES),
            back_rows(BT, LANES),
            whole(1, width),
            whole(2, width, width),
            whole(model, rows),
            whole(model, width),
            smem(),
        ],
        [
            pl.BlockSpec((3, BT, width), lambda i: (0, blocks - 1 - i, 0)),
            whole(8, width),
            *[whole(quarter, 4, part, width)] * 4,
        ],
        [
            sds((3, rows, width), bf16),
            sds((8, width), f32),
            *[sds((quarter, 4, part, width), bf16)] * 4,
        ],
        [
            pltpu.VMEM((width, width), f32),
            pltpu.VMEM((8, width), f32),
            pltpu.VMEM((3, rows, width), bf16),
        ],
        2 * rows * model * 3 * width,
        rows * width * 30 + rows * model * 2 + 6 * model * width,
    )(labels, dq, dk, dv, q_expo, k_expo, kf, v, gb, gzb, grad_in, seg_col, cosine, sine, fw, tab, ln1t, g_out, me_seq)

    qkvo = Sum("reduce_attn", w_parts)
    event = low
    chunks = {"D": down, "I": inn, "C": qkvo}
    for name in BEFORE:
        event = chunks[name].step(event)

    stat_width = max(rows, model)
    val_keep, val_send, e_keep, e_send, stats = call(
        finish_kernel,
        blocks,
        [
            smem(),
            rows_of(BT, hidden),
            whole(hidden, model),
            rows_of(BT, width),
            whole(width, model),
            rows_of(BT, hidden),
            pl.BlockSpec((3, BT, width), lambda i: (0, i, 0)),
            whole(3, model, width),
            whole(model, hidden),
            rows_of(BT, model),
            whole(4, model),
        ],
        [
            *[pl.BlockSpec((n_head // 2, BT, share), lambda i: (0, i, 0))] * 4,
            whole(16, stat_width),
        ],
        [
            *[sds((n_head // 2, rows, share), bf16)] * 4,
            sds((16, stat_width), f32),
        ],
        [pltpu.VMEM((BT, model), bf16)],
        2 * rows * model * (3 * width + hidden),
        rows * width * 6 + rows * model * 6 + 8 * model * width + 2 * hidden * model,
    )(me_head, hid, w_down, att, w_out, dpre, after(low, event), w_qkv, w_in, xhat, gains)
    with jax.named_scope("mixed_sum"):
        mixed_share = scatter_sum(val_keep, after(val_send, low), "head")
    with jax.named_scope("e_sum"):
        e_share = scatter_sum(e_keep, e_send, "head")
    with jax.named_scope("stats_sum"):
        gains_own = stats[8:12, :model]
        stats = sum_all(stats[:8], "head")
    stats = stats[:2, :rows].T * (1.0 / model)

    bias = lax.dynamic_slice_in_dim(b_out, offset, share) + lax.dynamic_slice_in_dim(b_down, offset, share)
    mixed = (tokens.astype(f32) + mixed_share + bias).astype(bf16)
    xhat_share = lax.dynamic_slice_in_dim(xhat, offset, share, 1).astype(f32)
    grad_input = grad_out.astype(f32) + inv_std * (
        e_share - stats[:, 0:1] - xhat_share * stats[:, 1:2]
    )
    event = late = e_send
    for name in AFTER:
        chunk = chunks[name]
        if chunk.plan:
            pins = (mixed, grad_input) if len(chunk.plan) == 1 and name in PINNED else ()
            event = chunk.step(event, *pins)
        late = event if len(qkvo.plan) == LATE else late
    for chunk in chunks.values():
        while chunk.plan:
            event = chunk.step(event)
    g_down = block_out(down, me_seq)
    g_in = block_out(inn, me_seq)
    g_qkv, g_out = call(
        widen_kernel,
        4,
        [smem(), *[pl.BlockSpec((quarter, 1, part, width), lambda c: (0, c, 0, 0))] * 4],
        [
            pl.BlockSpec((1, model, width), lambda c: (jnp.minimum(c, 2), 0, 0)),
            whole(width, model),
        ],
        [sds((3, model, width), f32), sds((width, model), f32)],
        [pltpu.VMEM((model, width), f32)],
        0,
        END_COST * model * width,
    )(me_seq, *qkvo.arrays)

    with jax.named_scope("small_sum"):
        local = jnp.concatenate([small[:4], gb_in.reshape(-1, share), bias_out], 0)
        mine = (jnp.arange(n_head) == lax.axis_index("head")).astype(f32)
        spread_gains = gains_own.reshape(4, n_head, share).transpose(1, 0, 2)
        packet = jnp.concatenate([spread_gains, mine[:, None, None] * local[None]], 1)
        packet = jnp.broadcast_to(packet[None], (n_seq,) + packet.shape).reshape((-1,) + packet.shape[1:])
        packet = jnp.sum(lax.all_to_all(after(packet, late), ("seq", "head"), 0, 0, tiled=True), 0)
    gain_share, small, gb_in, bias_out = packet[:4], packet[4:8], packet[8:-1].reshape(-1), packet[-1]
    return (
        mixed,
        grad_input,
        gain_share[0],
        gain_share[1],
        gain_share[2],
        gain_share[3],
        g_qkv,
        small[:3],
        small[3].reshape(heads, feats),
        g_out,
        bias_out,
        g_in,
        gb_in,
        g_down,
        bias_out,
    )


def solution(mesh):
    in_specs = (
        P("seq", "head"),
        P(),
        P("seq"),
        P(),
        P(),
        P(),
        P(),
        P(None, None, "head"),
        P(None, "head"),
        P("head", None),
        P("head", None),
        P(),
        P(None, "head"),
        P("head"),
        P("head", None),
        P(),
        P("seq", "head"),
    )
    out_specs = (
        P("seq", "head"),
        P("seq", "head"),
        P("head"),
        P("head"),
        P("head"),
        P("head"),
        P(None, None, "head"),
        P(None, "head"),
        P("head", None),
        P("head", None),
        P("head"),
        P(None, "head"),
        P("head"),
        P("head", None),
        P("head"),
    )
    return jax.shard_map(body, mesh=mesh, in_specs=in_specs, out_specs=out_specs, check_vma=False)
```
